32 devices in a mesh: dp: 2 (over core), fsdp: 16 (over z, y, x).
Axes of the slice: x: 2, y: 2, z: 4, core: 2. Of those that a mesh axis runs over, the one named last changes fastest.
Arguments:
- x_regional: bfloat16 [1536, 512], P(('dp', 'fsdp')), may hold values from -6 to 6
- x_local: bfloat16 [1536, 49, 512], P(('dp', 'fsdp')), may hold values from -6 to 6
- w_qkv: bfloat16 [512, 1536], P('fsdp', 'dp'), may hold values from -0.25 to 0.25
- w_proj: bfloat16 [512, 512], P('fsdp', 'dp'), may hold values from -0.75 to 0.75
- w_fc1: bfloat16 [512, 2048], P('fsdp', 'dp'), may hold values from -0.25 to 0.25
- w_fc2: bfloat16 [2048, 512], P('fsdp', 'dp'), may hold values from -0.125 to 0.125
- gains: bfloat16 [3, 512], P(None, 'fsdp'), may hold values from 0.099609375 to 1.8984375
- biases: bfloat16 [11, 512], P(None, 'fsdp'), may hold values from -3 to 3
- region_counts: int32 [32], replicated, may hold values from 49 to 144, as said below
- cot_regional: bfloat16 [1536, 512], P(('dp', 'fsdp')), may hold values from -6 to 6
- cot_local: bfloat16 [1536, 49, 512], P(('dp', 'fsdp')), may hold values from -6 to 6
Outputs:
- out_regional: bfloat16 [1536, 512], P(('dp', 'fsdp'))
- out_local: bfloat16 [1536, 49, 512], P(('dp', 'fsdp'))
- grad_regional: bfloat16 [1536, 512], P(('dp', 'fsdp'))
- grad_local: bfloat16 [1536, 49, 512], P(('dp', 'fsdp'))
- grad_qkv: float32 [512, 1536], P('fsdp', 'dp')
- grad_proj: float32 [512, 512], P('fsdp', 'dp')
- grad_fc1: float32 [512, 2048], P('fsdp', 'dp')
- grad_fc2: float32 [2048, 512], P('fsdp', 'dp')
- grad_gains: float32 [3, 512], P(None, 'fsdp')
- grad_biases: float32 [11, 512], P(None, 'fsdp')
The draws below stay inside these ranges and needn't reach their ends.
Inputs may be any that keep to these rules, and one draw needn't show every extreme that they name: `region_counts`: each count is 49, 81 or 144, and one of the first three is 144. Images occupy consecutive regions in order, starting at region 0; regions of an image that would pass region 1536 are cut off, and the images after it are empty.
All inputs are finite; a program needn't handle non-finite values.
Results may differ from the reference program's by a relative error of at most 0.02.
Values may be sent and summed in bfloat16 or wider, within the bound.
No kernel may reach another device: no remote copies, remote signals or barrier semaphores. Data moves between devices by JAX's collectives and lax.ppermute only.
A program may use at most 320 MiB of HBM per device.

```python
from functools import partial
import jax
import jax.numpy as jnp
from jax import lax

D = 512
HEADS = 16
HEAD_DIM = 32
FF = 2048
LOCAL = 49
MIN_REGIONS = 49
MAX_REGIONS = 144
REGIONS = 1536
IMAGES = 32
BIAS_ROWS = 11


def draw_region_counts(key, part):
    key = jax.random.fold_in(key, 11)
    pick_key, place_key = jax.random.split(key)
    kinds = jax.random.randint(pick_key, (IMAGES,), 0, 3)
    forced = jax.random.randint(place_key, (), 0, 3)
    kinds = jnp.where(jnp.arange(IMAGES) == forced, 2, kinds)
    counts = jnp.where(kinds == 0, MIN_REGIONS, jnp.where(kinds == 1, 81, MAX_REGIONS))
    return counts.astype(jnp.int32)


def shard_levels(own_key, shape, pieces, least, top_value):
    def one(dim, shards_of):
        steps = jax.random.uniform(jax.random.fold_in(jax.random.fold_in(own_key, 6), dim), (shards_of,), jnp.float32, least / len(pieces), top_value / len(pieces))
        return jnp.repeat(jnp.exp(steps), shape[dim] // shards_of).reshape((-1,) + (1,) * (len(shape) - dim - 1))

    loudness = one(*pieces[0])
    for cut in pieces[1:]:
        loudness = loudness * one(*cut)
    return loudness


def noise(stream_key, dims, deviation, most, shards=(), held_as=jnp.bfloat16):
    entries = jax.random.normal(stream_key, dims, jnp.float32) * deviation
    if len(shards) > 0:
        entries = shard_levels(stream_key, dims, shards, -0.22, 0.18) * entries
    return jnp.clip(entries, min=-most, max=most).astype(held_as)


def setup_inputs(seed: int = 0) -> dict:
    key_of = jax.random.split(jax.random.key(seed), 12)
    x_regional = noise(key_of[0], (REGIONS, D), 1.0, 6.0, ((0, 32),))
    x_local = noise(key_of[1], (REGIONS, LOCAL, D), 1.0, 6.0, ((0, 32),))
    w_qkv = noise(key_of[2], (D, 3 * D), D ** -0.5, 0.25, ((0, 16), (1, 2)))
    w_proj = noise(key_of[3], (D, D), (D // 8) ** -0.5, 0.75, ((0, 16), (1, 2)))
    w_fc1 = noise(key_of[4], (D, FF), D ** -0.5, 0.25, ((0, 16), (1, 2)))
    w_fc2 = noise(key_of[5], (FF, D), FF ** -0.5, 0.125, ((0, 16), (1, 2)))
    gains = jnp.clip(1.0 + 0.18 * jax.random.normal(key_of[6], (3, D), jnp.float32), 0.099609375, 1.8984375).astype(jnp.bfloat16)
    biases = noise(key_of[7], (BIAS_ROWS, D), 0.5, 3.0, ((1, 16),))
    region_counts = draw_region_counts(jax.random.fold_in(key_of[11], 71), 0)
    cot_regional = noise(key_of[9], (REGIONS, D), 1.0, 6.0, ((0, 32),))
    cot_local = noise(key_of[10], (REGIONS, LOCAL, D), 1.0, 6.0, ((0, 32),))
    return dict(x_regional=x_regional, x_local=x_local, w_qkv=w_qkv, w_proj=w_proj, w_fc1=w_fc1, w_fc2=w_fc2, gains=gains, biases=biases, region_counts=region_counts, cot_regional=cot_regional, cot_local=cot_local)


EPSILON = 1e-05
NEGATIVE = -1e+30

@jax.custom_vjp
def low(v):
    return lax.optimization_barrier(v.astype(jnp.bfloat16)).astype(jnp.float32)

@jax.custom_vjp
def low_back(v):
    return v

def low_keep(v):
    return (low(v), None)

def low_pass(kept, grad):
    return (grad,)

def back_keep(v):
    return (v, None)

def back_low(kept, grad):
    return (low(grad),)
low.defvjp(low_keep, low_pass)
low_back.defvjp(back_keep, back_low)

def matmul(left_side, right_side):
    return jnp.dot(left_side, right_side, precision=lax.Precision.HIGHEST)

def layer_norm(values_in, norm_gain, norm_shift):
    centred = values_in - lax.optimization_barrier(jnp.mean(values_in, axis=-1, keepdims=True))
    inv_std = lax.rsqrt(lax.optimization_barrier(jnp.mean(centred * centred, axis=-1, keepdims=True)) + EPSILON)
    return centred * inv_std * norm_gain + norm_shift

def project(normed, w_qkv, bias_query, bias_value):
    rounded = low(normed)
    projected = matmul(rounded, w_qkv)
    queries = low(low_back(projected[:, :D] + bias_query))
    keys_in = low(low_back(projected[:, D:2 * D]))
    values_in = low(low_back(projected[:, 2 * D:] + bias_value))
    return (queries, keys_in, values_in)

def attend(queries, keys_in, values_in, allowed):
    scores = jnp.einsum('bqhe,bkhe->bhqk', queries, keys_in, precision=lax.Precision.HIGHEST) * HEAD_DIM ** (-0.5)
    scores = jnp.where(allowed[:, None], low_back(scores), NEGATIVE)
    shifted = jnp.exp(scores - lax.optimization_barrier(jnp.max(scores, axis=-1, keepdims=True)))
    probability = shifted / lax.optimization_barrier(jnp.sum(shifted, axis=-1, keepdims=True))
    return jnp.einsum('bhqk,bkhe->bqhe', low(probability), values_in, precision=lax.Precision.HIGHEST)

def forward(x_regional, x_local, w_qkv, w_proj, w_fc1, w_fc2, gains, biases, image_ids):
    bias_query, bias_value, bias_proj = (biases[3], biases[4], biases[5])
    bias_up = biases[6:6 + FF // D].reshape(FF)
    bias_down = biases[6 + FF // D]
    region_q, region_k, region_v = project(layer_norm(x_regional, gains[0], biases[0]), w_qkv, bias_query, bias_value)
    padded_k = jnp.pad(region_k, ((MAX_REGIONS, MAX_REGIONS), (0, 0)))
    padded_v = jnp.pad(region_v, ((MAX_REGIONS, MAX_REGIONS), (0, 0)))
    padded_ids = jnp.pad(image_ids, (MAX_REGIONS, MAX_REGIONS), constant_values=-1)
    block_rows = 256
    key_rows = block_rows + 2 * MAX_REGIONS

    def region_block(block_index):
        first_row = block_index * block_rows
        queries = lax.dynamic_slice_in_dim(region_q, first_row, block_rows, 0).reshape(1, block_rows, HEADS, HEAD_DIM)
        keys_in = lax.dynamic_slice_in_dim(padded_k, first_row, key_rows, 0).reshape(1, key_rows, HEADS, HEAD_DIM)
        values_in = lax.dynamic_slice_in_dim(padded_v, first_row, key_rows, 0).reshape(1, key_rows, HEADS, HEAD_DIM)
        query_ids = lax.dynamic_slice_in_dim(image_ids, first_row, block_rows, 0)
        key_ids = lax.dynamic_slice_in_dim(padded_ids, first_row, key_rows, 0)
        allowed = (query_ids[:, None] == key_ids[None, :])[None]
        return attend(queries, keys_in, values_in, allowed).reshape(block_rows, D)
    region_att = lax.map(jax.checkpoint(region_block), jnp.arange(REGIONS // block_rows, dtype=jnp.int32))
    region_att = low(low_back(region_att.reshape(REGIONS, D)))
    region_mid = x_regional + low_back(matmul(region_att, w_proj) + bias_proj)
    tokens = jnp.concatenate([region_mid[:, None, :], x_local], axis=1)
    window_count = 64
    everywhere = jnp.ones((1, 1, 1), dtype=jnp.bool_)

    def window_block(windows):
        flat_in = windows.reshape(-1, D)
        queries, keys_in, values_in = project(layer_norm(flat_in, gains[1], biases[1]), w_qkv, bias_query, bias_value)
        head_shape = (window_count, LOCAL + 1, HEADS, HEAD_DIM)
        attended = attend(queries.reshape(head_shape), keys_in.reshape(head_shape), values_in.reshape(head_shape), everywhere)
        attended = low(low_back(attended.reshape(-1, D)))
        flat_mid = flat_in + low_back(matmul(attended, w_proj) + bias_proj)
        pre_act = low_back(matmul(low(layer_norm(flat_mid, gains[2], biases[2])), w_fc1) + bias_up)
        activated = low(jax.nn.gelu(pre_act, approximate=False))
        flat_out = flat_mid + low_back(matmul(activated, w_fc2) + bias_down)
        return flat_out.reshape(windows.shape)
    result = lax.map(jax.checkpoint(window_block), tokens.reshape(REGIONS // window_count, window_count, LOCAL + 1, D))
    result = result.reshape(REGIONS, LOCAL + 1, D)
    return (result[:, 0], result[:, 1:])

def reference(x_regional, x_local, w_qkv, w_proj, w_fc1, w_fc2, gains, biases, region_counts, cot_regional, cot_local):
    image_ends = jnp.minimum(jnp.cumsum(region_counts).astype(jnp.int32), REGIONS)
    region_rows = jnp.arange(REGIONS, dtype=jnp.int32)
    image_ids = lax.optimization_barrier(jnp.sum((image_ends[None, :] <= region_rows[:, None]).astype(jnp.int32), axis=1)).astype(jnp.int32)
    primals = (x_regional.astype(jnp.float32), x_local.astype(jnp.float32), w_qkv.astype(jnp.float32), w_proj.astype(jnp.float32), w_fc1.astype(jnp.float32), w_fc2.astype(jnp.float32), gains.astype(jnp.float32), biases.astype(jnp.float32))
    outputs, pullback = jax.vjp(partial(forward, image_ids=image_ids), *primals)
    grads = pullback((cot_regional.astype(jnp.float32), cot_local.astype(jnp.float32)))
    return (outputs[0].astype(jnp.bfloat16), outputs[1].astype(jnp.bfloat16), grads[0].astype(jnp.bfloat16), grads[1].astype(jnp.bfloat16), grads[2], grads[3], grads[4], grads[5], grads[6], grads[7])
```

```python
import math
from functools import partial

import jax
import jax.numpy as jnp
from jax import lax
from jax.experimental import pallas as pl
from jax.experimental.pallas import tpu as pltpu
from jax.sharding import PartitionSpec as P

HEAD_DIM = 32
MAX_REGIONS = 144
EPSILON = 1e-05
NEGATIVE = -1e30
PITCH = 56
SLOT = 64
LANES = 128
GROUP = LANES // HEAD_DIM
EXP_SCALE = HEAD_DIM ** (-0.5) * math.log2(math.e)
FACTOR = HEAD_DIM ** (-0.5)
VMEM_BYTES = 60 * 1024 * 1024

ERFC_P = 0.42
ERFC = (
    0.23681994,
    0.23965002,
    0.19433459,
    0.27000812,
    -0.13287422,
    0.44318139,
    -0.32169076,
    0.07057076,
)

BF16 = jnp.bfloat16
F32 = jnp.float32


def dot_nn(a, b):
    return lax.dot_general(a, b, (((1,), (0,)), ((), ())), preferred_element_type=F32)


def dot_nt(a, b):
    return lax.dot_general(a, b, (((1,), (1,)), ((), ())), preferred_element_type=F32)


def dot_tn(a, b):
    return lax.dot_general(a, b, (((0,), (0,)), ((), ())), preferred_element_type=F32)


def normalise(x):
    centred = x - jnp.mean(x, axis=-1, keepdims=True)
    inv_std = lax.rsqrt(jnp.mean(centred * centred, axis=-1, keepdims=True) + EPSILON)
    return centred * inv_std, inv_std


def norm_back(dy, hat, inv_std, gain):
    scaled = dy * gain
    mean_s = jnp.mean(scaled, axis=-1, keepdims=True)
    mean_h = jnp.mean(scaled * hat, axis=-1, keepdims=True)
    return inv_std * (scaled - mean_s - hat * mean_h)


def head_masks(rows):
    lane = lax.broadcasted_iota(jnp.int32, (rows, LANES), 1) // HEAD_DIM
    return [jnp.where(lane == h, 1.0, 0.0).astype(BF16) for h in range(GROUP)]


def spread(x, masks, order=(0, 1, 2, 3)):
    return jnp.concatenate([x * masks[h] for h in order], axis=0)


def turn(p):
    both = jnp.concatenate([p[:, :LANES], p[:, LANES:]], axis=0).T
    return jnp.concatenate([both[:SLOT], both[SLOT:]], axis=1)


TURNED = (0, 2, 1, 3)


def gelu_pair(h):
    z = jnp.abs(h) * (ERFC_P * math.sqrt(0.5)) + 1.0
    t = pl.reciprocal(z, approx=True)
    poly = jnp.full_like(t, ERFC[-1])
    for c in ERFC[-2::-1]:
        poly = poly * t + c
    bell = jnp.exp2(h * h * (-0.5 * math.log2(math.e)))
    tail = (poly * t) * (bell * 0.5)
    cdf = jnp.where(h < 0, tail, 1.0 - tail)
    return h * cdf, cdf + h * (bell * (1.0 / math.sqrt(2.0 * math.pi)))


def build_windows(z_ref, local_ref, row_ref):
    count, local_len, _ = local_ref.shape
    for w in range(count):
        z_ref[w * PITCH : w * PITCH + local_len] = local_ref[w].astype(F32)
        z_ref[w * PITCH + local_len : w * PITCH + local_len + 1] = row_ref[w : w + 1].astype(F32)


def split_windows(z, local_ref, row_ref):
    count, local_len, _ = local_ref.shape
    for w in range(count):
        local_ref[w] = z[w * PITCH : w * PITCH + local_len].astype(local_ref.dtype)
        row_ref[w : w + 1] = z[w * PITCH + local_len : w * PITCH + local_len + 1].astype(row_ref.dtype)


def pack_weights_kernel(
    wqkv_ref, wproj_ref, gains_ref, biases_ref, up_ref, down_ref, att_ref, mlp_ref, small_s
):
    row = 0
    small_s[...] = jnp.zeros_like(small_s)
    count, lanes = gains_ref.shape
    small_s[:count, :lanes] = gains_ref[...].astype(F32)
    small_s[count : count + biases_ref.shape[0], :lanes] = biases_ref[...].astype(F32)
    for ref in (wqkv_ref, wproj_ref, None):
        if ref is None:
            att_ref[row : row + lanes] = small_s[...].T[:lanes].astype(BF16)
            row += lanes
            continue
        for c in range(0, ref.shape[1], LANES):
            att_ref[row : row + ref.shape[0]] = ref[:, c : c + LANES]
            row += ref.shape[0]
    row = 0
    cols = down_ref.shape[1]
    for c in range(0, up_ref.shape[1], cols):
        mlp_ref[row : row + up_ref.shape[0]] = up_ref[:, c : c + cols]
        row += up_ref.shape[0]
    mlp_ref[row:] = down_ref[...]


def block_places(place_ref, stacks, codes):
    order, far_peers = codes
    per = len(stacks) // far_peers
    for i, stack in enumerate(stacks):
        deep = stack.shape[0]
        for k in range(deep):
            yield stack, k, place_ref[0] ^ (i // per), place_ref[1] ^ order[i % per * deep + k]


def assemble_attention(place_ref, stacks, codes, wqkv_ref, wproj_ref, norms_ref, small_s):
    peers, far_peers = len(codes[0]), codes[1]
    rows = wproj_ref.shape[0] // peers
    parts = [wqkv_ref.shape[1] // far_peers // LANES, wproj_ref.shape[1] // far_peers // LANES]
    for stack, k, d, f in block_places(place_ref, stacks, codes):
        here = pl.ds(pl.multiple_of(f * rows, rows), rows)
        row = 0
        for count, ref in zip(parts, (wqkv_ref, wproj_ref)):
            for j in range(count):
                to = pl.multiple_of((d * count + j) * LANES, LANES)
                ref[here, pl.ds(to, LANES)] = stack[k, row : row + rows]
                row += rows
        small_s[here] = stack[k, row : row + rows].astype(F32)
    norms_ref[...] = small_s[...].T[: norms_ref.shape[0]]


def pair_offsets(place_ref, peers, span):
    linear = place_ref[0] * peers + place_ref[1]
    for d in range(1, span + 1):
        low = lax.rem(linear, 2 * d) < d
        yield jnp.where(low, d, -d)
        yield jnp.where(low, -d, d)


def region_forward_kernel(place_ref, kid_ref, qid_ref, *refs, near, stacks, codes):
    x_refs, refs = refs[:near], refs[near:]
    if stacks:
        stack_refs, refs = refs[:stacks], refs[stacks:]
        mid_ref, hat_ref, qkv_ref, p_ref, o_ref, wqkv_ref, wproj_ref, norms_ref, small_s, x_s = refs
        assemble_attention(place_ref, stack_refs, codes, wqkv_ref, wproj_ref, norms_ref, small_s)
        own = mid_ref.shape[0]
        span = near // 2
        x_s[span * own : (span + 1) * own] = x_refs[0][...].astype(F32)
        for ref, by in zip(x_refs[1:], pair_offsets(place_ref, len(codes[0]), span)):
            x_s[pl.ds(pl.multiple_of((span + by) * own, 8), own)] = ref[...].astype(F32)
        x = x_s[...]
    else:
        wqkv_ref, wproj_ref, norms_ref, mid_ref, hat_ref, qkv_ref, p_ref, o_ref = refs
        x = jnp.concatenate([r[...].astype(F32) for r in x_refs], axis=0)
    own, width = mid_ref.shape
    rows = x.shape[0]
    first = (rows - own) // 2
    hat, _ = normalise(x)
    u = (hat * norms_ref[0:1] + norms_ref[3:4]).astype(BF16)
    hat_ref[...] = hat.astype(BF16)
    qkv = dot_nn(u, wqkv_ref[...])
    q = (qkv[:, :width] + norms_ref[6:7]).astype(BF16)
    k = qkv[:, width : 2 * width].astype(BF16)
    v = (qkv[:, 2 * width :] + norms_ref[7:8]).astype(BF16)
    qkv_ref[:, :width] = q
    qkv_ref[:, width : 2 * width] = k
    qkv_ref[:, 2 * width :] = v
    masks = head_masks(SLOT)
    same = kid_ref[...] == qid_ref[...]
    lane = lax.broadcasted_iota(jnp.int32, (1, GROUP * SLOT), 1)
    asked = (lane % SLOT) < own
    out_masks = [m.astype(F32) for m in masks]
    for c in range(width // LANES):
        cols = slice(c * LANES, (c + 1) * LANES)
        qx = spread(q[first : first + SLOT, cols], masks)
        s = jnp.where(same, dot_nt(k[:, cols], qx), NEGATIVE)
        e = jnp.exp2((s - jnp.max(s, axis=0, keepdims=True)) * EXP_SCALE)
        total = jnp.sum(e, axis=0, keepdims=True)
        p = (e * jnp.where(asked, 1.0 / total, 0.0)).astype(BF16)
        p_ref[c] = p
        mixed = dot_tn(p, v[:, cols])
        o = sum(mixed[h * SLOT : (h + 1) * SLOT] * out_masks[h] for h in range(GROUP))
        o_ref[:, cols] = o[:own].astype(BF16)
    mid_ref[...] = x[first : first + own] + dot_nn(o_ref[...], wproj_ref[...]) + norms_ref[8:9]


def window_forward_kernel(
    local_ref,
    row_ref,
    wqkv_ref,
    wproj_ref,
    norms_ref,
    *refs,
):
    z1_ref, hat_ref, qkv_ref, p_ref, o_ref, tick_ref, z_s, qkv_s, o_s = refs[-9:]
    tick_ref[...] = jnp.zeros_like(tick_ref)
    rows, width = z_s.shape
    count, local_len, _ = local_ref.shape

    @pl.when(pl.program_id(0) == 0)
    def _():
        z_s[...] = jnp.zeros_like(z_s)
        qkv_s[rows:, :] = jnp.zeros((qkv_s.shape[0] - rows, qkv_s.shape[1]), F32)

    build_windows(z_s, local_ref, row_ref)
    hat, _ = normalise(z_s[...])
    u = (hat * norms_ref[1:2] + norms_ref[4:5]).astype(BF16)
    hat_ref[...] = hat.astype(BF16)
    qkv_s[:rows, :width] = dot_nn(u, wqkv_ref[:, :width]) + norms_ref[6:7]
    qkv_s[:rows, width : 2 * width] = dot_nn(u, wqkv_ref[:, width : 2 * width])
    qkv_s[:rows, 2 * width :] = dot_nn(u, wqkv_ref[:, 2 * width :]) + norms_ref[7:8]
    masks = head_masks(SLOT)
    is_key = lax.broadcasted_iota(jnp.int32, (SLOT, GROUP * SLOT), 0) <= local_len
    lane = lax.broadcasted_iota(jnp.int32, (1, GROUP * SLOT), 1)
    asked = (lane % SLOT) <= local_len

    def window(w):
        base = pl.multiple_of(w * PITCH, 8)
        spots = [c * LANES for c in range(width // LANES)]
        scores, values = [], []
        for at in spots:
            q = qkv_s[pl.ds(base, SLOT), at : at + LANES].astype(BF16)
            k = qkv_s[pl.ds(base, SLOT), width + at : width + at + LANES].astype(BF16)
            v = qkv_s[pl.ds(base, SLOT), 2 * width + at : 2 * width + at + LANES].astype(BF16)
            qkv_ref[w, :, at : at + LANES] = q
            qkv_ref[w, :, width + at : width + at + LANES] = k
            qkv_ref[w, :, 2 * width + at : 2 * width + at + LANES] = v
            scores.append(dot_nt(k, spread(q, masks)))
            values.append(v)
        probs = []
        for c, s in enumerate(scores):
            s = jnp.where(is_key, s, NEGATIVE)
            e = jnp.exp2((s - jnp.max(s, axis=0, keepdims=True)) * EXP_SCALE)
            total = jnp.sum(e, axis=0, keepdims=True)
            p = (e * jnp.where(asked, 1.0 / total, 0.0)).astype(BF16)
            p_ref[w, c] = p
            probs.append(turn(p))
        for at, p, v in zip(spots, probs, values):
            o = dot_nn(p, spread(v, masks, TURNED))
            o_s[pl.ds(base, PITCH), at : at + LANES] = o[:PITCH]

    def windows(i, carry):
        for j in range(2):
            window(2 * i + j)
        return carry

    lax.fori_loop(0, count // 2, windows, 0)
    o = o_s[...].astype(BF16)
    o_ref[...] = o
    z1_ref[...] = z_s[...] + dot_nn(o, wproj_ref[...]) + norms_ref[8:9]


def assemble_mlp(place_ref, block_refs, up_ref, down_ref):
    fsdp, tall, cols = block_refs[0].shape
    far = place_ref[0]
    up_rows = up_ref.shape[0] // fsdp
    down_rows = down_ref.shape[0] // fsdp
    parts = (tall - down_rows) // up_rows
    for f in range(fsdp):
        for d, blocks_ref in enumerate(block_refs):
            col = d ^ far
            for j in range(parts):
                at = pl.multiple_of((col * parts + j) * cols, LANES)
                up_ref[f * up_rows : (f + 1) * up_rows, pl.ds(at, cols)] = blocks_ref[
                    f, j * up_rows : (j + 1) * up_rows
                ]
            at = pl.multiple_of(col * cols, LANES)
            down_ref[f * down_rows : (f + 1) * down_rows, pl.ds(at, cols)] = blocks_ref[
                f, parts * up_rows :
            ]


def pack_mlp(place_ref, gup_s, gdown_s, outs):
    fsdp = outs[0].shape[0]
    far = place_ref[0]
    width, hidden = gdown_s.shape
    up_rows, up_cols = width // fsdp, hidden // len(outs)
    down_rows, down_cols = width // len(outs), hidden // fsdp
    parts = up_cols // LANES
    for r, out in enumerate(outs):
        d = r ^ far
        for f in range(fsdp):
            here = slice(f * up_rows, (f + 1) * up_rows)
            for j in range(parts):
                at = pl.multiple_of((d * parts + j) * LANES, LANES)
                out[f, j * up_rows : (j + 1) * up_rows] = gup_s[here, pl.ds(at, LANES)].astype(BF16)
            at = pl.multiple_of(d * down_rows, 8)
            out[f, parts * up_rows :] = gdown_s[
                pl.ds(at, down_rows), f * down_cols : (f + 1) * down_cols
            ].astype(BF16)


def mlp_kernel(place_ref, z_ref, cot_ref, cot_row_ref, norms_ref, *refs, packed):
    if packed:
        block_refs, refs = refs[:packed], refs[packed:]
        out_ref, out_row_ref, dz_ref, dz_row_ref, e_ref, sums_ref = refs[:6]
        grad_refs, refs = refs[6 : 6 + packed], refs[6 + packed :]
        dz_s, gup_s, gdown_s, acc_s, h_s, dg_s, g_s, eh_s, up_ref, down_ref = refs
    else:
        up_ref, down_ref, out_ref, out_row_ref, dz_ref, dz_row_ref, e_ref, sums_ref = refs[:8]
        grad_refs, refs = refs[8:10], refs[10:]
        dz_s, gup_s, gdown_s, acc_s, h_s, dg_s, g_s, eh_s = refs
    rows, width = z_ref.shape
    hidden = up_ref.shape[1]
    step = pl.program_id(0)

    @pl.when(step == 0)
    def _():
        if packed:
            assemble_mlp(place_ref, block_refs, up_ref, down_ref)
        dz_s[...] = jnp.zeros_like(dz_s)
        gup_s[...] = jnp.zeros_like(gup_s)
        gdown_s[...] = jnp.zeros_like(gdown_s)
        sums_ref[...] = jnp.zeros_like(sums_ref)

    build_windows(dz_s, cot_ref, cot_row_ref)
    hat, inv_std = normalise(z_ref[...])
    u = (hat * norms_ref[2:3] + norms_ref[5:6]).astype(BF16)
    e2 = dz_s[...].astype(BF16)
    ones = jnp.ones((16, rows), BF16)
    ut = jnp.concatenate([u.T, ones], axis=0)
    et = e2.T
    chunks = hidden // width
    strip = 16
    half = width // 2

    def begin(c):
        def up(n):
            cols = slice(c * width + n, c * width + n + half)
            h_s[c % 2, :, n : n + half] = dot_nn(u, up_ref[:, cols])

        def down(n):
            cols = slice(c * width + n, c * width + n + half)
            dg_s[c % 2, :, n : n + half] = dot_nt(e2, down_ref[cols, :])

        return [partial(f, n) for n in (0, half) for f in (up, down)]

    def middle(c):
        def part(r):
            bias = norms_ref[9 + c : 10 + c]
            g, slope = gelu_pair(h_s[c % 2, r : r + strip] + bias)
            g_s[c % 2, r : r + strip] = g.astype(BF16)
            eh_s[c % 2, r : r + strip] = (dg_s[c % 2, r : r + strip] * slope).astype(BF16)

        return [partial(part, r) for r in range(0, rows, strip)]

    def finish(c):
        whole = slice(c * width, (c + 1) * width)

        def add(ref, i, n, x):
            if c == 0:
                ref[i, :, n : n + half] = x
            else:
                ref[i, :, n : n + half] += x

        def forward(n):
            add(acc_s, 0, n, dot_nn(g_s[c % 2], down_ref[whole, n : n + half]))

        def back(n):
            add(acc_s, 1, n, dot_nt(eh_s[c % 2], up_ref[n : n + half, whole]))

        def down(n):
            cols = slice(c * width + n, c * width + n + half)
            gdown_s[:, cols] += dot_nn(et, g_s[c % 2, :, n : n + half])

        def up(n):
            cols = slice(c * width + n, c * width + n + half)
            gup_s[:, cols] += dot_nn(ut, eh_s[c % 2, :, n : n + half])

        return [partial(f, n) for n in (0, half) for f in (forward, back, down, up)]

    for f in begin(0):
        f()
    for c in range(chunks):
        products = begin(c + 1) if c + 1 < chunks else []
        if c > 0:
            products = products + finish(c - 1)
        strips = middle(c)
        done = 0
        for i, f in enumerate(strips):
            f()
            upto = len(products) * (i + 1) // len(strips)
            for g in products[done:upto]:
                g()
            done = upto
    for f in finish(chunks - 1):
        f()
    z2 = z_ref[...] + acc_s[0] + norms_ref[13:14]
    split_windows(z2, out_ref, out_row_ref)
    du = acc_s[1]
    dz2 = dz_s[...]
    sums_ref[1:2, :width] += jnp.sum(e2.astype(F32), axis=0, keepdims=True)
    sums_ref[2:3, :width] += jnp.sum(du * hat, axis=0, keepdims=True)
    sums_ref[3:4, :width] += jnp.sum(du, axis=0, keepdims=True)
    dz1 = dz2 + norm_back(du, hat, inv_std, norms_ref[2:3])
    dz_ref[...] = dz1
    local_len = cot_ref.shape[1]
    for w in range(cot_ref.shape[0]):
        at = w * PITCH + local_len
        dz_row_ref[w : w + 1] = dz1[at : at + 1]
    e = dz1.astype(BF16)
    e_ref[...] = e
    sums_ref[4:5, :width] += jnp.sum(e.astype(F32), axis=0, keepdims=True)

    @pl.when(step == pl.num_programs(0) - 1)
    def _():
        sums_ref[0:1, :] = gup_s[width : width + 1, :]
        if packed:
            pack_mlp(place_ref, gup_s, gdown_s, grad_refs)
        else:
            grad_refs[0][...] = gup_s[:width].astype(BF16)
            grad_refs[1][...] = gdown_s[...].astype(BF16)


def window_backward_kernel(
    e_ref,
    qkv_ref,
    p_ref,
    hat_ref,
    o_ref,
    wproj_ref,
    *refs,
    local_len,
):
    mixed_ref, mixed_row_ref, sums_ref, gqkv_ref, gproj_ref, do_s, mixed_s = refs[1:]
    rows, width = e_ref.shape
    count = qkv_ref.shape[0]

    @pl.when(pl.program_id(0) == 0)
    def _():
        do_s[rows:, :] = jnp.zeros((do_s.shape[0] - rows, width), F32)
        for ref in (sums_ref, gqkv_ref, gproj_ref):
            ref[...] = jnp.zeros_like(ref)

    do_s[:rows, :] = dot_nt(e_ref[...], wproj_ref[...])
    gproj_ref[...] += dot_tn(o_ref[...], e_ref[...])
    masks = head_masks(SLOT)

    spots = [c * LANES for c in range(width // LANES)]

    def window(w):
        base = pl.multiple_of(w * PITCH, 8)
        upstream, slopes = [], []
        for at in spots:
            do = spread(do_s[pl.ds(base, SLOT), at : at + LANES].astype(BF16), masks)
            v = qkv_ref[w, :, 2 * width + at : 2 * width + at + LANES]
            slopes.append(dot_nt(v, do))
            upstream.append(do)
        for c, at in enumerate(spots):
            dv = dot_nn(p_ref[w, c], upstream[c])
            mixed_s[pl.ds(base, PITCH), 2 * width + at : 2 * width + at + LANES] = dv[:PITCH]
        scores = []
        for c, dp in enumerate(slopes):
            p = p_ref[w, c].astype(F32)
            ds = p * (dp - jnp.sum(dp * p, axis=0, keepdims=True))
            scores.append(ds.astype(BF16))
        turned = [turn(ds) for ds in scores]
        for at, ds in zip(spots, scores):
            dk = dot_nn(ds, spread(qkv_ref[w, :, at : at + LANES], masks)) * FACTOR
            mixed_s[pl.ds(base, PITCH), width + at : width + at + LANES] = dk[:PITCH]
        for at, ds in zip(spots, turned):
            k = qkv_ref[w, :, width + at : width + at + LANES]
            dq = dot_nn(ds, spread(k, masks, TURNED)) * FACTOR
            mixed_s[pl.ds(base, PITCH), at : at + LANES] = dq[:PITCH]

    def windows(i, carry):
        for j in range(2):
            window(2 * i + j)
        return carry

    lax.fori_loop(0, count // 2, windows, 0)
    mixed = mixed_s[...].astype(BF16)
    mixed_ref[...] = mixed
    for w in range(count):
        at = w * PITCH + local_len
        mixed_row_ref[w : w + 1] = mixed_s[at : at + 1].astype(BF16)
    sums_ref[0:1, :] += jnp.sum(mixed.astype(F32), axis=0, keepdims=True)
    gqkv_ref[...] += dot_tn(hat_ref[...], mixed)


def local_back_kernel(local_ref, dz_ref, mixed_ref, wqkv_ref, norms_ref, *refs):
    out_ref, tick_ref, z_s = refs[-3:]
    tick_ref[...] = jnp.zeros_like(tick_ref)
    count, local_len, _ = local_ref.shape

    @pl.when(pl.program_id(0) == 0)
    def _():
        z_s[...] = jnp.zeros_like(z_s)

    for w in range(count):
        z_s[w * PITCH : w * PITCH + local_len] = local_ref[w].astype(F32)
    du = dot_nt(mixed_ref[...], wqkv_ref[...])
    hat, inv_std = normalise(z_s[...])
    dz0 = dz_ref[...] + norm_back(du, hat, inv_std, norms_ref[1:2])
    for w in range(count):
        out_ref[w] = dz0[w * PITCH : w * PITCH + local_len].astype(BF16)


def pack_attention(place_ref, gqkv_s, gproj_s, small_s, du_s, own, outs):
    wide, deep = outs[0].shape[:2]
    peers = wide * deep
    width = gproj_s.shape[0]
    rows = width // peers
    quads = width // LANES
    counts = [gqkv_s.shape[1] // len(outs) // LANES, gproj_s.shape[1] // len(outs) // LANES]
    far, me = place_ref[0], place_ref[1]
    linear = far * peers + me
    near = du_s.shape[0] // own
    for r, out in enumerate(outs):
        d = r ^ far
        for p in range(peers):
            j, i = p % wide, p // wide
            f = me ^ p
            here = pl.ds(pl.multiple_of(f * rows, 8), rows)
            row = 0
            for count, grad in zip(counts, (gqkv_s, gproj_s)):
                for c in range(count):
                    at = pl.ds(pl.multiple_of((d * count + c) * LANES, LANES), LANES)
                    out[j, i, row : row + rows] = grad[here, at].astype(BF16)
                    row += rows
            out[j, i, row : row + rows] = small_s[here].astype(BF16)
            row += rows
            away = d * peers + f - linear + near // 2
            inside = (away >= 0) & (away < near)
            at = pl.ds(pl.multiple_of(jnp.where(inside, away, 0) * own, 8), own)
            share = jnp.where(inside, 1.0, 0.0)
            for c in range(quads):
                term = du_s[at, c * LANES : (c + 1) * LANES] * share
                out[j, i, row : row + own] = term.astype(BF16)
                row += own


def region_tail_kernel(
    place_ref,
    mixed_row_ref,
    dz_row_ref,
    mid_ref,
    hat_ref,
    qkv_ref,
    p_ref,
    o_ref,
    wqkv_ref,
    wproj_ref,
    norms_ref,
    gqkv_in_ref,
    gproj_in_ref,
    att_sums_ref,
    mlp_sums_ref,
    dmid_ref,
    *refs,
    packed,
):
    outs, refs = (refs[:packed], refs[packed:]) if packed else (refs[:4], refs[4:])
    near_s, du_s, gqkv_s, gproj_s, lines_s, small_s = refs
    own, width = mid_ref.shape
    rows = qkv_ref.shape[0]
    first = (rows - own) // 2
    mine = slice(first, first + own)

    mid_hat, mid_std = normalise(mid_ref[...])
    row_du = dot_nt(mixed_row_ref[...], wqkv_ref[...])
    dmid = dz_row_ref[...] + norm_back(row_du, mid_hat, mid_std, norms_ref[1:2])
    dmid_ref[...] = dmid
    e = dmid.astype(BF16)
    do = dot_nt(e, wproj_ref[...])
    do = jnp.concatenate([do, jnp.zeros((SLOT - own, width), F32)], axis=0).astype(BF16)
    masks = head_masks(SLOT)
    out_masks = [m.astype(F32) for m in masks]
    dqs = []
    for c in range(width // LANES):
        at = c * LANES
        q = qkv_ref[first : first + SLOT, at : at + LANES]
        k = qkv_ref[:, width + at : width + at + LANES]
        v = qkv_ref[:, 2 * width + at : 2 * width + at + LANES]
        dox = spread(do[:, at : at + LANES], masks)
        p = p_ref[c]
        near_s[:, width + at : width + at + LANES] = dot_nn(p, dox).astype(BF16)
        dp = dot_nt(v, dox)
        pf = p.astype(F32)
        ds = (pf * (dp - jnp.sum(dp * pf, axis=0, keepdims=True))).astype(BF16)
        near_s[:, at : at + LANES] = (dot_nn(ds, spread(q, masks)) * FACTOR).astype(BF16)
        wide = dot_tn(ds, k)
        dq = sum(wide[h * SLOT : (h + 1) * SLOT] * out_masks[h] for h in range(GROUP))
        dqs.append((dq[:own] * FACTOR).astype(BF16))
    dq = jnp.concatenate(dqs, axis=1)
    near = near_s[...]

    du_s[...] = dot_nt(near, wqkv_ref[:, width:])
    du_s[mine] += dot_nt(dq, wqkv_ref[:, :width])

    win_sum = att_sums_ref[0:1]
    near_sum = jnp.concatenate(
        [
            jnp.sum(dq.astype(F32), axis=0, keepdims=True),
            jnp.sum(near.astype(F32), axis=0, keepdims=True),
        ],
        axis=1,
    )
    sums = jnp.concatenate([near_sum, win_sum, jnp.zeros((6, 3 * width), F32)], axis=0)
    high = sums.astype(BF16)
    rest = (sums - high.astype(F32)).astype(BF16)
    both = jnp.concatenate([high, rest], axis=0)
    shifts = dot_nt(both, wqkv_ref[...])
    shifts = shifts[:8] + shifts[8:]
    lines_s[...] = jnp.zeros_like(lines_s)
    lines_s[:16] = norms_ref[...]
    columns = lines_s[...].T
    gain_0, gain_1 = columns[:, 0:1], columns[:, 1:2]
    shift_0, shift_1 = columns[:, 3:4], columns[:, 4:5]
    dgain_0 = jnp.zeros((width, 1), F32)
    dgain_1 = jnp.zeros((width, 1), F32)
    for i in range(3):
        cols = slice(i * width, (i + 1) * width)
        if i == 0:
            region = dot_tn(hat_ref[mine, :], dq)
        else:
            region = dot_tn(hat_ref[...], near[:, (i - 1) * width : i * width])
        window = gqkv_in_ref[:, cols]
        weight = wqkv_ref[:, cols].astype(F32)
        dgain_0 += jnp.sum(weight * region, axis=1, keepdims=True)
        dgain_1 += jnp.sum(weight * window, axis=1, keepdims=True)
        gqkv_s[:, cols] = (
            region * gain_0
            + window * gain_1
            + shift_0 * near_sum[:, cols]
            + shift_1 * win_sum[:, cols]
        )
    gproj_s[...] = gproj_in_ref[...] + dot_tn(o_ref[...], e)
    total = near_sum + win_sum
    hidden = mlp_sums_ref.shape[1]
    lines = [
        None,
        None,
        mlp_sums_ref[2:3, :width],
        shifts[0:1],
        shifts[1:2],
        mlp_sums_ref[3:4, :width],
        total[:, :width],
        total[:, 2 * width :],
        jnp.sum(e.astype(F32), axis=0, keepdims=True) + mlp_sums_ref[4:5, :width],
    ]
    lines += [mlp_sums_ref[0:1, c * width : (c + 1) * width] for c in range(hidden // width)]
    lines += [mlp_sums_ref[1:2, :width]]
    lines_s[...] = jnp.zeros_like(lines_s)
    for i, line in enumerate(lines):
        if line is not None:
            lines_s[i : i + 1] = line
    small_s[...] = lines_s[...].T
    small_s[:, 0:1] = dgain_0
    small_s[:, 1:2] = dgain_1
    if packed:
        pack_attention(place_ref, gqkv_s, gproj_s, small_s, du_s, own, outs)
    else:
        outs[0][...] = gqkv_s[...].astype(BF16)
        outs[1][...] = gproj_s[...].astype(BF16)
        outs[2][...] = small_s[...]
        outs[3][...] = du_s[...].astype(BF16)


def finish_kernel(
    x_ref,
    dmid_ref,
    norms_ref,
    mlp_ref,
    *refs,
    terms,
):
    term_refs, outs = refs[:terms], refs[terms + 1 : -1]
    out_ref, gqkv_ref, gproj_ref, gup_ref, gdown_ref, ggains_ref, gbiases_ref = outs
    small_s = refs[-1]
    own, width = x_ref.shape

    def total(row, count):
        here = slice(row, row + count)
        return sum([t[here].astype(F32) for t in term_refs[1:]], term_refs[0][here].astype(F32))

    rows = gqkv_ref.shape[0]
    row = 0
    for ref in (gqkv_ref, gproj_ref):
        for c in range(0, ref.shape[1], LANES):
            ref[:, c : c + LANES] = total(row, rows)
            row += rows
    small_s[:rows] = total(row, rows)
    small = small_s[...].T
    count = ggains_ref.shape[0]
    ggains_ref[...] = small[:count, :rows]
    gbiases_ref[...] = small[count : count + gbiases_ref.shape[0], :rows]
    row += rows
    du = jnp.concatenate([total(row + c * own, own) for c in range(width // LANES)], axis=1)
    hat, inv_std = normalise(x_ref[...].astype(F32))
    out_ref[...] = (dmid_ref[...] + norm_back(du, hat, inv_std, norms_ref[0:1])).astype(BF16)
    row = 0
    for c in range(0, gup_ref.shape[1], LANES):
        gup_ref[:, c : c + LANES] = mlp_ref[row : row + rows].astype(F32)
        row += rows
    gdown_ref[...] = mlp_ref[row:].astype(F32).T


def region_end_kernel(x_ref, dmid_ref, norms_ref, *refs):
    near_refs, out_ref = refs[:-1], refs[-1]
    du = near_refs[0][...].astype(F32)
    for ref in near_refs[1:]:
        du = du + ref[...].astype(F32)
    hat, inv_std = normalise(x_ref[...].astype(F32))
    out_ref[...] = (dmid_ref[...] + norm_back(du, hat, inv_std, norms_ref[0:1])).astype(BF16)


def axis_rounds(size):
    rounds = []
    shift = 0
    while (1 << shift) < size:
        width = min(4, size >> shift)
        rounds.append((shift, width))
        shift += width.bit_length() - 1
    return rounds


def swap_by(x, axis, code):
    pairs = [(i, i ^ code) for i in range(lax.axis_size(axis))]
    return lax.ppermute(x, axis, pairs)


def gather_axis(x, axis, stacked=True):
    size = lax.axis_size(axis)
    rounds = axis_rounds(size)
    if not stacked and len(rounds) == 1:
        return [x] + [swap_by(x, axis, j) for j in range(1, size)], list(range(size))
    stack = x[None]
    codes = [0]
    for shift, width in reversed(rounds):
        parts = [stack] + [swap_by(stack, axis, j << shift) for j in range(1, width)]
        stack = jnp.concatenate(parts, axis=0)
        codes = [c ^ (j << shift) for j in range(width) for c in codes]
    return stack, codes


def in_order(stack, codes, axis):
    place = [0] * len(codes)
    for p, c in enumerate(codes):
        place[c] = p
    wanted = jnp.arange(len(codes), dtype=jnp.int32) ^ lax.axis_index(axis)
    return jnp.take(stack, jnp.asarray(place, dtype=jnp.int32)[wanted], axis=0)


def scatter_axis(blocks, axis):
    size = lax.axis_size(axis)
    me = lax.axis_index(axis)
    rest = blocks.shape[1:]
    for shift, width in axis_rounds(size):
        left = blocks.shape[0] // width
        cut = blocks.reshape((left, width) + rest)
        mine = (me >> shift) & (width - 1)
        total = lax.dynamic_index_in_dim(cut, mine, 1, keepdims=False).astype(jnp.float32)
        for j in range(1, width):
            out = lax.dynamic_index_in_dim(cut, mine ^ j, 1, keepdims=False)
            total = total + swap_by(out, axis, j << shift).astype(jnp.float32)
        blocks = total.astype(blocks.dtype)
    return blocks[0]


def join(blocks):
    dp, fsdp, rows, cols = blocks.shape
    return blocks.transpose(1, 2, 0, 3).reshape(fsdp * rows, dp * cols)


def cut(whole, dp, fsdp):
    rows, cols = whole.shape
    return whole.reshape(fsdp, rows // fsdp, dp, cols // dp).transpose(2, 0, 1, 3)


def scatter_all(blocks):
    return scatter_axis(scatter_axis(blocks, "dp"), "fsdp").astype(jnp.float32)


def shifted(x, by):
    axes = ("dp", "fsdp")
    peers = lax.axis_size(axes)
    pairs = [(i, i + by) for i in range(peers) if 0 <= i + by < peers]
    return lax.ppermute(x, axes, pairs)


def matched(x, by, second):
    axes = ("dp", "fsdp")
    peers = lax.axis_size(axes)
    pairs = []
    for i in range(peers):
        low = i % (2 * by) < by
        to = i + by if low != bool(second) else i - by
        if 0 <= to < peers:
            pairs.append((i, to))
    return lax.ppermute(x, axes, pairs)


def full(shape):
    return pl.BlockSpec(shape, lambda *_: (0,) * len(shape))


def tiled(shape, begin=0):
    return pl.BlockSpec(shape, lambda i: (i + begin,) + (0,) * (len(shape) - 1))


def like(shape, dtype):
    return jax.ShapeDtypeStruct(shape, dtype)


def smem():
    return pl.BlockSpec(memory_space=pltpu.SMEM)


def vmem():
    return pl.BlockSpec(memory_space=pltpu.VMEM)


def gather_round(stack, axis, which):
    shift, width = axis_rounds(lax.axis_size(axis))[::-1][which]
    return [stack] + [swap_by(stack, axis, j << shift) for j in range(1, width)]


def gather_parts(block, axis):
    rounds = axis_rounds(lax.axis_size(axis))[::-1]
    parts = [block[None]]
    codes = [0]
    for which, (shift, width) in enumerate(rounds):
        parts = gather_round(jnp.concatenate(parts, axis=0), axis, which)
        codes = [c ^ (j << shift) for j in range(width) for c in codes]
    return parts, codes


def far_parts(parts):
    return parts + [
        swap_by(x, "dp", r) for r in range(1, lax.axis_size("dp")) for x in parts
    ]


def send_far(grads):
    return [swap_by(g, "dp", r) for r, g in enumerate(grads) if r > 0]


def send_round(terms, step):
    return [swap_by(x, "fsdp", j * step) for j, x in enumerate(terms) if j > 0]


def reduce_round(terms, got):
    total = terms[0].astype(F32)
    for x in got:
        total = total + x.astype(F32)
    return total.astype(BF16)


def takes(us):
    return pl.CostEstimate(flops=int(us * 1.1e9), bytes_accessed=int(us * 1e6), transcendentals=0)


def params():
    return pltpu.CompilerParams(vmem_limit_bytes=VMEM_BYTES)


def on_device(
    x_regional,
    x_local,
    w_qkv,
    w_proj,
    w_fc1,
    w_fc2,
    gains,
    biases,
    region_counts,
    cot_regional,
    cot_local,
):
    regions, local_len, width = x_local.shape
    group = 8
    steps = regions // group
    rows = group * PITCH
    all_rows = regions * PITCH
    quads = width // LANES
    span = (regions + MAX_REGIONS - 2) // regions
    all_regions = regions * lax.axis_size(("dp", "fsdp"))
    linear = lax.axis_index(("dp", "fsdp"))
    first_row = linear * regions
    dp, fsdp = lax.axis_size("dp"), lax.axis_size("fsdp")
    qkv_cols, proj_cols = w_qkv.shape[1], w_proj.shape[1]
    in_blocks = qkv_cols % LANES == 0 and proj_cols % LANES == 0 and w_fc2.shape[0] == LANES
    small_rows = gains.shape[0] + biases.shape[0]

    mlp_cols = w_fc2.shape[1]
    if in_blocks:
        att_rows = (qkv_cols + proj_cols + LANES) // LANES * w_qkv.shape[0]
        mlp_rows = w_fc1.shape[0] * w_fc1.shape[1] // mlp_cols + w_fc2.shape[0]
        att_block, mlp_block = pl.pallas_call(
            pack_weights_kernel,
            out_shape=(like((att_rows, LANES), BF16), like((mlp_rows, mlp_cols), BF16)),
            scratch_shapes=[pltpu.VMEM((LANES, LANES), F32)],
            compiler_params=params(),
            cost_estimate=takes(2),
            name="pack_weights",
        )(w_qkv, w_proj, gains, biases, w_fc1, w_fc2)
    else:
        small = jnp.concatenate([gains, biases], axis=0).T
        small = jnp.pad(small, ((0, 0), (0, LANES - small_rows)))
        att_block = jnp.concatenate([w_qkv, w_proj, small], axis=1)
        up_parts = [w_fc1[:, i : i + mlp_cols] for i in range(0, w_fc1.shape[1], mlp_cols)]
        mlp_block = jnp.concatenate(up_parts + [w_fc2], axis=0)
    hidden = w_fc1.shape[1] * dp

    place = jnp.stack([lax.axis_index("dp"), lax.axis_index("fsdp")]).astype(jnp.int32)
    near_rows = (2 * span + 1) * regions
    wide = axis_rounds(fsdp)[0][1]
    if in_blocks:
        att_parts, order = gather_parts(att_block, "fsdp")
        codes = (order, dp)
        att_stacks = far_parts(att_parts)
        near = [x_regional]
        near += [matched(x_regional, d, s) for d in range(1, span + 1) for s in range(2)]
        mlp_half = lax.all_gather(mlp_block, "fsdp", axis=0, tiled=False)
    else:
        att_stack, order = gather_axis(att_block, "fsdp")
        codes = (order, dp)
        att_stacks, far_codes = gather_axis(att_stack, "dp")
        mlp_stack, _ = gather_axis(mlp_block, "fsdp")
        mlp_stack = in_order(mlp_stack, order, "fsdp")
        mlp_stack, _ = gather_axis(mlp_stack, "dp")
        mlp_stack = in_order(mlp_stack, far_codes, "dp")

    image_ends = jnp.minimum(jnp.cumsum(region_counts), all_regions)
    key_rows = first_row - span * regions + jnp.arange(near_rows, dtype=jnp.int32)
    key_image = jnp.sum((image_ends[None, :] <= key_rows[:, None]).astype(jnp.int32), axis=1)
    inside = (key_rows >= 0) & (key_rows < all_regions)
    key_image = jnp.where(inside, key_image, -1)
    query_image = jnp.pad(
        key_image[span * regions : (span + 1) * regions],
        (0, SLOT - regions),
        constant_values=-2,
    )
    query_image = jnp.tile(query_image, GROUP)[None]

    region_outs = (
        like((regions, width), F32),
        like((near_rows, width), BF16),
        like((near_rows, 3 * width), BF16),
        like((quads, near_rows, GROUP * SLOT), BF16),
        like((regions, width), BF16),
    )
    if in_blocks:
        whole = (
            like((width, 3 * width), BF16),
            like((width, width), BF16),
            like((16, width), F32),
        )
        region_mid, region_hat, region_qkv, region_p, region_o, qkv_full, proj_full, norms = (
            pl.pallas_call(
                partial(
                    region_forward_kernel, near=len(near), stacks=len(att_stacks), codes=codes
                ),
                in_specs=[smem()] + [vmem()] * (2 + len(near) + len(att_stacks)),
                out_shape=region_outs + whole,
                scratch_shapes=[
                    pltpu.VMEM((width, LANES), F32),
                    pltpu.VMEM((near_rows, width), F32),
                ],
                compiler_params=params(),
                cost_estimate=takes(6),
                name="region_forward",
            )(place, key_image[:, None], query_image, *near, *att_stacks)
        )
    else:
        near = [
            x_regional if offset == 0 else shifted(x_regional, -offset)
            for offset in range(-span, span + 1)
        ]
        blocks = in_order(jnp.stack([in_order(s, order, "fsdp") for s in att_stacks]), far_codes, "dp")
        qkv_full = join(blocks[..., :qkv_cols])
        proj_full = join(blocks[..., qkv_cols : qkv_cols + proj_cols])
        small = blocks[0, :, :, qkv_cols + proj_cols :].reshape(width, LANES)
        norms = small.astype(F32).T[:16]
        region_mid, region_hat, region_qkv, region_p, region_o = pl.pallas_call(
            partial(region_forward_kernel, near=len(near), stacks=0, codes=codes),
            in_specs=[smem()] + [vmem()] * (5 + len(near)),
            out_shape=region_outs,
            compiler_params=params(),
            cost_estimate=takes(6),
            name="region_forward",
        )(place, key_image[:, None], query_image, *near, qkv_full, proj_full, norms)

    first_half = steps // 2
    forward_outs = (
        like((all_rows, width), F32),
        like((all_rows, width), BF16),
        like((regions, SLOT, 3 * width), BF16),
        like((regions, quads, SLOT, GROUP * SLOT), BF16),
        like((all_rows, width), BF16),
        like((8, LANES), F32),
    )

    def window_forward(begin, count, held, ties):
        operands = (x_local, region_mid, qkv_full, proj_full, norms)
        return pl.pallas_call(
            window_forward_kernel,
            grid=(count,),
            in_specs=[
                tiled((group, local_len, width), begin),
                tiled((group, width), begin),
                full(qkv_full.shape),
                full(proj_full.shape),
                full(norms.shape),
            ]
            + [pl.BlockSpec(memory_space=pl.ANY)] * (len(held) + len(ties)),
            out_specs=[
                tiled((rows, width), begin),
                tiled((rows, width), begin),
                tiled((group, SLOT, 3 * width), begin),
                tiled((group, quads, SLOT, GROUP * SLOT), begin),
                tiled((rows, width), begin),
                full((8, LANES)),
            ],
            out_shape=forward_outs,
            scratch_shapes=[
                pltpu.VMEM((rows, width), F32),
                pltpu.VMEM((rows + 8, 3 * width), F32),
                pltpu.VMEM((rows, width), F32),
            ],
            input_output_aliases={len(operands) + i: i for i in range(len(held))},
            compiler_params=params(),
            cost_estimate=takes(6 * count),
            name="window_forward",
        )(*operands, *held, *ties)

    *held, tick = window_forward(0, first_half, (), ())
    if in_blocks:
        mlp_half, tick = lax.optimization_barrier((mlp_half, tick))
        mlp_stacks = far_parts([mlp_half])
    z1, win_hat, win_qkv, win_p, win_o, _ = window_forward(
        first_half, steps - first_half, held, (tick,)
    )

    mlp_outs = [
        like(x_local.shape, BF16),
        like(x_regional.shape, BF16),
        like((all_rows, width), F32),
        like(x_regional.shape, F32),
        like((all_rows, width), BF16),
        like((8, hidden), F32),
    ]
    mlp_specs = [
        tiled((group, local_len, width)),
        tiled((group, width)),
        tiled((rows, width)),
        tiled((group, width)),
        tiled((rows, width)),
        full((8, hidden)),
    ]
    mlp_scratch = [
        pltpu.VMEM((rows, width), F32),
        pltpu.VMEM((width + 16, hidden), F32),
        pltpu.VMEM((width, hidden), F32),
        pltpu.VMEM((2, rows, width), F32),
        pltpu.VMEM((2, rows, width), F32),
        pltpu.VMEM((2, rows, width), F32),
        pltpu.VMEM((2, rows, width), BF16),
        pltpu.VMEM((2, rows, width), BF16),
    ]
    if in_blocks:
        weights = tuple(mlp_stacks)
        tall = mlp_block.shape[0] * mlp_cols // LANES
        grad_shapes = [(fsdp, tall, LANES)] * dp
        mlp_scratch += [pltpu.VMEM((width, hidden), BF16), pltpu.VMEM((hidden, width), BF16)]
    else:
        blocks = mlp_stack.transpose(1, 0, 2, 3)
        up_full = blocks[:, :, : mlp_block.shape[0] - w_fc2.shape[0]]
        up_full = up_full.reshape(fsdp, dp, -1, w_fc1.shape[0], mlp_cols)
        up_full = up_full.transpose(0, 3, 1, 2, 4).reshape(width, hidden)
        down_full = blocks[:, :, mlp_block.shape[0] - w_fc2.shape[0] :]
        down_full = down_full.transpose(0, 2, 1, 3).reshape(hidden, width)
        weights = (up_full, down_full)
        grad_shapes = [(width, hidden)] * 2
    out_local, out_regional, dz1, dz_row, win_e, mlp_sums, *mlp_grads = pl.pallas_call(
        partial(mlp_kernel, packed=dp if in_blocks else 0),
        grid=(steps,),
        in_specs=[
            smem(),
            tiled((rows, width)),
            tiled((group, local_len, width)),
            tiled((group, width)),
            full(norms.shape),
        ]
        + [full(w.shape) for w in weights],
        out_specs=mlp_specs + [full(g) for g in grad_shapes],
        out_shape=mlp_outs + [like(g, BF16) for g in grad_shapes],
        scratch_shapes=mlp_scratch,
        compiler_params=params(),
        cost_estimate=takes(50),
        name="mlp",
    )(place, z1, cot_local, cot_regional, norms, *weights)

    if in_blocks:
        mlp_sum = mlp_grads[0].astype(F32)
        for g in send_far(mlp_grads):
            mlp_sum = mlp_sum + g.astype(F32)
        mlp_chip = mlp_sum.astype(BF16)
        mlp_sum = lax.psum_scatter(mlp_chip, "fsdp", scatter_dimension=0)

    win_mixed, mixed_row, att_sums, grad_qkv, grad_proj = pl.pallas_call(
        partial(window_backward_kernel, local_len=local_len),
        grid=(steps,),
        in_specs=[
            tiled((rows, width)),
            tiled((group, SLOT, 3 * width)),
            tiled((group, quads, SLOT, GROUP * SLOT)),
            tiled((rows, width)),
            tiled((rows, width)),
            full(proj_full.shape),
            pl.BlockSpec(memory_space=pl.ANY),
        ],
        out_specs=[
            tiled((rows, 3 * width)),
            tiled((group, 3 * width)),
            full((8, 3 * width)),
            full((width, 3 * width)),
            full((width, width)),
        ],
        out_shape=(
            like((all_rows, 3 * width), BF16),
            like((regions, 3 * width), BF16),
            like((8, 3 * width), F32),
            like((width, 3 * width), F32),
            like((width, width), F32),
        ),
        scratch_shapes=[
            pltpu.VMEM((rows + 8, width), F32),
            pltpu.VMEM((rows, 3 * width), F32),
        ],
        compiler_params=params(),
        name="window_backward",
    )(win_e, win_qkv, win_p, win_hat, win_o, proj_full, mlp_chip if in_blocks else norms)

    if in_blocks:
        tall = att_rows + regions * quads
        grad_shapes = [like((wide, fsdp // wide, tall, LANES), BF16)] * dp
    else:
        grad_shapes = [
            like((width, 3 * width), BF16),
            like((width, width), BF16),
            like((width, LANES), F32),
            like((near_rows, width), BF16),
        ]
    operands = (
        mixed_row,
        dz_row,
        region_mid,
        region_hat,
        region_qkv,
        region_p,
        region_o,
        qkv_full,
        proj_full,
        norms,
        grad_qkv,
        grad_proj,
        att_sums,
        mlp_sums,
    )
    dmid, *att_grads = pl.pallas_call(
        partial(region_tail_kernel, packed=dp if in_blocks else 0),
        in_specs=[smem()] + [vmem()] * len(operands),
        out_shape=[like((regions, width), F32)] + grad_shapes,
        scratch_shapes=[
            pltpu.VMEM((near_rows, 2 * width), BF16),
            pltpu.VMEM((near_rows, width), F32),
            pltpu.VMEM((width, 3 * width), F32),
            pltpu.VMEM((width, width), F32),
            pltpu.VMEM((LANES, width), F32),
            pltpu.VMEM((width, LANES), F32),
        ],
        compiler_params=params(),
        name="region_tail",
    )(place, *operands)

    def local_back(begin, count, ties, held):
        return pl.pallas_call(
            local_back_kernel,
            grid=(count,),
            in_specs=[
                tiled((group, local_len, width), begin),
                tiled((rows, width), begin),
                tiled((rows, 3 * width), begin),
                full(qkv_full.shape),
                full(norms.shape),
            ]
            + [pl.BlockSpec(memory_space=pl.ANY)] * (len(ties) + len(held)),
            out_specs=[tiled((group, local_len, width), begin), full((8, LANES))],
            out_shape=(like(x_local.shape, BF16), like((8, LANES), F32)),
            scratch_shapes=[pltpu.VMEM((rows, width), F32)],
            input_output_aliases={5: 0} if held else {},
            compiler_params=params(),
            cost_estimate=takes(3 * count),
            name="local_back",
        )(x_local, dz1, win_mixed, qkv_full, norms, *held, *ties)

    cuts = [steps * i // 3 for i in range(4)]

    def local_part(i, ties, held):
        return local_back(cuts[i], cuts[i + 1] - cuts[i], ties, held)

    if in_blocks:
        far = send_far(att_grads)
        grad_local, tick = local_part(0, (att_grads[0],), ())
        (*far, tick) = lax.optimization_barrier((*far, tick))
        terms = [
            sum([g[j].astype(F32) for g in far], att_grads[0][j].astype(F32)).astype(BF16)
            for j in range(wide)
        ]
        got = send_round(terms, 1)
        grad_local, tick = local_part(1, (tick, terms[0]), (grad_local,))
        grad_local, tick = local_part(2, (), (grad_local,))
        (*got, tick) = lax.optimization_barrier((*got, tick))
        terms = reduce_round(terms, got)
        terms = [terms[j] for j in range(fsdp // wide)]
        terms = terms[:1] + send_round(terms, wide)
        operands = (x_regional, dmid, norms, mlp_sum, *terms, tick)
        out_specs = (
            like(x_regional.shape, BF16),
            like(w_qkv.shape, F32),
            like(w_proj.shape, F32),
            like(w_fc1.shape, F32),
            like(w_fc2.shape, F32),
            like(gains.shape, F32),
            like(biases.shape, F32),
        )
        grad_regional, grad_qkv, grad_proj, grad_up, grad_down, grad_gains, grad_biases = (
            pl.pallas_call(
                partial(finish_kernel, terms=len(terms)),
                in_specs=[vmem()] * (len(operands) - 1) + [pl.BlockSpec(memory_space=pl.ANY)],
                out_shape=out_specs,
                scratch_shapes=[pltpu.VMEM((LANES, LANES), F32)],
                compiler_params=params(),
                cost_estimate=takes(2),
                name="finish",
            )(*operands)
        )
    else:
        up_rows = w_fc1.shape[0]
        up_blocks = cut(mlp_grads[0], dp, fsdp).reshape(dp, fsdp, up_rows, -1, mlp_cols)
        up_blocks = up_blocks.transpose(0, 1, 3, 2, 4).reshape(dp, fsdp, -1, mlp_cols)
        down_blocks = cut(mlp_grads[1].T, dp, fsdp)
        mlp_sum = scatter_all(jnp.concatenate([up_blocks, down_blocks], axis=2))
        grad_up = mlp_sum[: up_blocks.shape[2]].reshape(-1, up_rows, mlp_cols)
        grad_up = grad_up.transpose(1, 0, 2).reshape(w_fc1.shape)
        grad_down = mlp_sum[up_blocks.shape[2] :]
        grad_qkv, grad_proj, small, du_near = att_grads
        small = small.astype(BF16).reshape(1, fsdp, -1, LANES)
        small = jnp.broadcast_to(small, (dp,) + small.shape[1:])
        blocks = [cut(grad_qkv, dp, fsdp), cut(grad_proj, dp, fsdp), small]
        att = scatter_all(jnp.concatenate(blocks, axis=3))
        grad_qkv = att[:, :qkv_cols]
        grad_proj = att[:, qkv_cols : qkv_cols + proj_cols]
        small = att[:, qkv_cols + proj_cols :].T[:small_rows]
        grad_gains, grad_biases = small[: gains.shape[0]], small[gains.shape[0] :]
        held = ()
        for i in range(3):
            grad_local, tick = local_part(i, (), held)
            held = (grad_local,)
        returned = []
        for offset in range(-span, span + 1):
            part = du_near[(offset + span) * regions : (offset + span + 1) * regions]
            returned.append(part if offset == 0 else shifted(part, offset))
        grad_regional = pl.pallas_call(
            region_end_kernel,
            out_shape=like(x_regional.shape, BF16),
            compiler_params=params(),
            name="region_end",
        )(x_regional, dmid, norms, *returned)
    return (
        out_regional,
        out_local,
        grad_regional,
        grad_local,
        grad_qkv,
        grad_proj,
        grad_up,
        grad_down,
        grad_gains,
        grad_biases,
    )


def solution(mesh):
    in_specs = (
        P(("dp", "fsdp"), None),
        P(("dp", "fsdp"), None, None),
        P("fsdp", "dp"),
        P("fsdp", "dp"),
        P("fsdp", "dp"),
        P("fsdp", "dp"),
        P(None, "fsdp"),
        P(None, "fsdp"),
        P(),
        P(("dp", "fsdp"), None),
        P(("dp", "fsdp"), None, None),
    )
    out_specs = (
        P(("dp", "fsdp"), None),
        P(("dp", "fsdp"), None, None),
        P(("dp", "fsdp"), None),
        P(("dp", "fsdp"), None, None),
        P("fsdp", "dp"),
        P("fsdp", "dp"),
        P("fsdp", "dp"),
        P("fsdp", "dp"),
        P(None, "fsdp"),
        P(None, "fsdp"),
    )
    return jax.shard_map(
        on_device, mesh=mesh, in_specs=in_specs, out_specs=out_specs, check_vma=False
    )
```

```python
import math
from functools import partial

import jax
import jax.numpy as jnp
from jax import lax
from jax.experimental import pallas as pl
from jax.experimental.pallas import tpu as pltpu
from jax.sharding import PartitionSpec as P

HEAD_DIM = 32
MAX_REGIONS = 144
EPSILON = 1e-05
NEGATIVE = -1e30
PITCH = 56
SLOT = 64
LANES = 128
GROUP = LANES // HEAD_DIM
EXP_SCALE = HEAD_DIM ** (-0.5) * math.log2(math.e)
FACTOR = HEAD_DIM ** (-0.5)
VMEM_BYTES = 60 * 1024 * 1024

ERFC_P = 0.42
ERFC = (
    0.23681994,
    0.23965002,
    0.19433459,
    0.27000812,
    -0.13287422,
    0.44318139,
    -0.32169076,
    0.07057076,
)

BF16 = jnp.bfloat16
F32 = jnp.float32


def dot_nn(a, b):
    return lax.dot_general(a, b, (((1,), (0,)), ((), ())), preferred_element_type=F32)


def dot_nt(a, b):
    return lax.dot_general(a, b, (((1,), (1,)), ((), ())), preferred_element_type=F32)


def dot_tn(a, b):
    return lax.dot_general(a, b, (((0,), (0,)), ((), ())), preferred_element_type=F32)


def normalise(x):
    centred = x - jnp.mean(x, axis=-1, keepdims=True)
    inv_std = lax.rsqrt(jnp.mean(centred * centred, axis=-1, keepdims=True) + EPSILON)
    return centred * inv_std, inv_std


def norm_back(dy, hat, inv_std, gain):
    scaled = dy * gain
    mean_s = jnp.mean(scaled, axis=-1, keepdims=True)
    mean_h = jnp.mean(scaled * hat, axis=-1, keepdims=True)
    return inv_std * (scaled - mean_s - hat * mean_h)


def head_masks(rows):
    lane = lax.broadcasted_iota(jnp.int32, (rows, LANES), 1) // HEAD_DIM
    return [jnp.where(lane == h, 1.0, 0.0).astype(BF16) for h in range(GROUP)]


def spread(x, masks, order=(0, 1, 2, 3)):
    return jnp.concatenate([x * masks[h] for h in order], axis=0)


def turn(p):
    both = jnp.concatenate([p[:, :LANES], p[:, LANES:]], axis=0).T
    return jnp.concatenate([both[:SLOT], both[SLOT:]], axis=1)


TURNED = (0, 2, 1, 3)


def gelu_pair(h):
    z = jnp.abs(h) * (ERFC_P * math.sqrt(0.5)) + 1.0
    t = pl.reciprocal(z, approx=True)
    poly = jnp.full_like(t, ERFC[-1])
    for c in ERFC[-2::-1]:
        poly = poly * t + c
    bell = jnp.exp2(h * h * (-0.5 * math.log2(math.e)))
    tail = (poly * t) * (bell * 0.5)
    cdf = jnp.where(h < 0, tail, 1.0 - tail)
    return h * cdf, cdf + h * (bell * (1.0 / math.sqrt(2.0 * math.pi)))


def build_windows(z_ref, local_ref, row_ref):
    count, local_len, _ = local_ref.shape
    for w in range(count):
        z_ref[w * PITCH : w * PITCH + local_len] = local_ref[w].astype(F32)
        z_ref[w * PITCH + local_len : w * PITCH + local_len + 1] = row_ref[w : w + 1].astype(F32)


def split_windows(z, local_ref, row_ref):
    count, local_len, _ = local_ref.shape
    for w in range(count):
        local_ref[w] = z[w * PITCH : w * PITCH + local_len].astype(local_ref.dtype)
        row_ref[w : w + 1] = z[w * PITCH + local_len : w * PITCH + local_len + 1].astype(row_ref.dtype)


def pack_weights_kernel(
    wqkv_ref, wproj_ref, gains_ref, biases_ref, up_ref, down_ref, att_ref, mlp_ref, small_s
):
    row = 0
    small_s[...] = jnp.zeros_like(small_s)
    count, lanes = gains_ref.shape
    small_s[:count, :lanes] = gains_ref[...].astype(F32)
    small_s[count : count + biases_ref.shape[0], :lanes] = biases_ref[...].astype(F32)
    for ref in (wqkv_ref, wproj_ref, None):
        if ref is None:
            att_ref[row : row + lanes] = small_s[...].T[:lanes].astype(BF16)
            row += lanes
            continue
        for c in range(0, ref.shape[1], LANES):
            att_ref[row : row + ref.shape[0]] = ref[:, c : c + LANES]
            row += ref.shape[0]
    row = 0
    cols = down_ref.shape[1]
    for c in range(0, up_ref.shape[1], cols):
        mlp_ref[row : row + up_ref.shape[0]] = up_ref[:, c : c + cols]
        row += up_ref.shape[0]
    mlp_ref[row:] = down_ref[...]


def block_places(place_ref, stacks, codes):
    order, far_peers = codes
    per = len(stacks) // far_peers
    for i, stack in enumerate(stacks):
        deep = stack.shape[0]
        for k in range(deep):
            yield stack, k, place_ref[0] ^ (i // per), place_ref[1] ^ order[i % per * deep + k]


def assemble_attention(place_ref, stacks, codes, wqkv_ref, wproj_ref, norms_ref, small_s):
    peers, far_peers = len(codes[0]), codes[1]
    rows = wproj_ref.shape[0] // peers
    parts = [wqkv_ref.shape[1] // far_peers // LANES, wproj_ref.shape[1] // far_peers // LANES]
    for stack, k, d, f in block_places(place_ref, stacks, codes):
        here = pl.ds(pl.multiple_of(f * rows, rows), rows)
        row = 0
        for count, ref in zip(parts, (wqkv_ref, wproj_ref)):
            for j in range(count):
                to = pl.multiple_of((d * count + j) * LANES, LANES)
                ref[here, pl.ds(to, LANES)] = stack[k, row : row + rows]
                row += rows
        small_s[here] = stack[k, row : row + rows].astype(F32)
    norms_ref[...] = small_s[...].T[: norms_ref.shape[0]]


def pair_offsets(place_ref, peers, span):
    linear = place_ref[0] * peers + place_ref[1]
    for d in range(1, span + 1):
        low = lax.rem(linear, 2 * d) < d
        yield jnp.where(low, d, -d)
        yield jnp.where(low, -d, d)


def region_forward_kernel(place_ref, kid_ref, qid_ref, *refs, near, stacks, codes):
    x_refs, refs = refs[:near], refs[near:]
    if stacks:
        stack_refs, refs = refs[:stacks], refs[stacks:]
        mid_ref, hat_ref, qkv_ref, p_ref, o_ref, wqkv_ref, wproj_ref, norms_ref, small_s, x_s = refs
        assemble_attention(place_ref, stack_refs, codes, wqkv_ref, wproj_ref, norms_ref, small_s)
        own = mid_ref.shape[0]
        span = near // 2
        x_s[span * own : (span + 1) * own] = x_refs[0][...].astype(F32)
        for ref, by in zip(x_refs[1:], pair_offsets(place_ref, len(codes[0]), span)):
            x_s[pl.ds(pl.multiple_of((span + by) * own, 8), own)] = ref[...].astype(F32)
        x = x_s[...]
    else:
        wqkv_ref, wproj_ref, norms_ref, mid_ref, hat_ref, qkv_ref, p_ref, o_ref = refs
        x = jnp.concatenate([r[...].astype(F32) for r in x_refs], axis=0)
    own, width = mid_ref.shape
    rows = x.shape[0]
    first = (rows - own) // 2
    hat, _ = normalise(x)
    u = (hat * norms_ref[0:1] + norms_ref[3:4]).astype(BF16)
    hat_ref[...] = hat.astype(BF16)
    qkv = dot_nn(u, wqkv_ref[...])
    q = (qkv[:, :width] + norms_ref[6:7]).astype(BF16)
    k = qkv[:, width : 2 * width].astype(BF16)
    v = (qkv[:, 2 * width :] + norms_ref[7:8]).astype(BF16)
    qkv_ref[:, :width] = q
    qkv_ref[:, width : 2 * width] = k
    qkv_ref[:, 2 * width :] = v
    masks = head_masks(SLOT)
    same = kid_ref[...] == qid_ref[...]
    lane = lax.broadcasted_iota(jnp.int32, (1, GROUP * SLOT), 1)
    asked = (lane % SLOT) < own
    out_masks = [m.astype(F32) for m in masks]
    for c in range(width // LANES):
        cols = slice(c * LANES, (c + 1) * LANES)
        qx = spread(q[first : first + SLOT, cols], masks)
        s = jnp.where(same, dot_nt(k[:, cols], qx), NEGATIVE)
        e = jnp.exp2((s - jnp.max(s, axis=0, keepdims=True)) * EXP_SCALE)
        total = jnp.sum(e, axis=0, keepdims=True)
        p = (e * jnp.where(asked, 1.0 / total, 0.0)).astype(BF16)
        p_ref[c] = p
        mixed = dot_tn(p, v[:, cols])
        o = sum(mixed[h * SLOT : (h + 1) * SLOT] * out_masks[h] for h in range(GROUP))
        o_ref[:, cols] = o[:own].astype(BF16)
    mid_ref[...] = x[first : first + own] + dot_nn(o_ref[...], wproj_ref[...]) + norms_ref[8:9]


def window_forward_kernel(
    local_ref,
    row_ref,
    wqkv_ref,
    wproj_ref,
    norms_ref,
    *refs,
):
    z1_ref, hat_ref, qkv_ref, p_ref, o_ref, tick_ref, z_s, qkv_s, o_s = refs[-9:]
    tick_ref[...] = jnp.zeros_like(tick_ref)
    rows, width = z_s.shape
    count, local_len, _ = local_ref.shape

    @pl.when(pl.program_id(0) == 0)
    def _():
        z_s[...] = jnp.zeros_like(z_s)
        qkv_s[rows:, :] = jnp.zeros((qkv_s.shape[0] - rows, qkv_s.shape[1]), F32)

    build_windows(z_s, local_ref, row_ref)
    hat, _ = normalise(z_s[...])
    u = (hat * norms_ref[1:2] + norms_ref[4:5]).astype(BF16)
    hat_ref[...] = hat.astype(BF16)
    qkv_s[:rows, :width] = dot_nn(u, wqkv_ref[:, :width]) + norms_ref[6:7]
    qkv_s[:rows, width : 2 * width] = dot_nn(u, wqkv_ref[:, width : 2 * width])
    qkv_s[:rows, 2 * width :] = dot_nn(u, wqkv_ref[:, 2 * width :]) + norms_ref[7:8]
    masks = head_masks(SLOT)
    is_key = lax.broadcasted_iota(jnp.int32, (SLOT, GROUP * SLOT), 0) <= local_len
    lane = lax.broadcasted_iota(jnp.int32, (1, GROUP * SLOT), 1)
    asked = (lane % SLOT) <= local_len

    def window(w):
        base = pl.multiple_of(w * PITCH, 8)
        spots = [c * LANES for c in range(width // LANES)]
        scores, values = [], []
        for at in spots:
            q = qkv_s[pl.ds(base, SLOT), at : at + LANES].astype(BF16)
            k = qkv_s[pl.ds(base, SLOT), width + at : width + at + LANES].astype(BF16)
            v = qkv_s[pl.ds(base, SLOT), 2 * width + at : 2 * width + at + LANES].astype(BF16)
            qkv_ref[w, :, at : at + LANES] = q
            qkv_ref[w, :, width + at : width + at + LANES] = k
            qkv_ref[w, :, 2 * width + at : 2 * width + at + LANES] = v
            scores.append(dot_nt(k, spread(q, masks)))
            values.append(v)
        probs = []
        for c, s in enumerate(scores):
            s = jnp.where(is_key, s, NEGATIVE)
            e = jnp.exp2((s - jnp.max(s, axis=0, keepdims=True)) * EXP_SCALE)
            total = jnp.sum(e, axis=0, keepdims=True)
            p = (e * jnp.where(asked, 1.0 / total, 0.0)).astype(BF16)
            p_ref[w, c] = p
            probs.append(turn(p))
        for at, p, v in zip(spots, probs, values):
            o = dot_nn(p, spread(v, masks, TURNED))
            o_s[pl.ds(base, PITCH), at : at + LANES] = o[:PITCH]

    def windows(i, carry):
        for j in range(2):
            window(2 * i + j)
        return carry

    lax.fori_loop(0, count // 2, windows, 0)
    o = o_s[...].astype(BF16)
    o_ref[...] = o
    z1_ref[...] = z_s[...] + dot_nn(o, wproj_ref[...]) + norms_ref[8:9]


def assemble_mlp(place_ref, block_refs, up_ref, down_ref):
    fsdp, tall, cols = block_refs[0].shape
    far = place_ref[0]
    up_rows = up_ref.shape[0] // fsdp
    down_rows = down_ref.shape[0] // fsdp
    parts = (tall - down_rows) // up_rows
    for f in range(fsdp):
        for d, blocks_ref in enumerate(block_refs):
            col = d ^ far
            for j in range(parts):
                at = pl.multiple_of((col * parts + j) * cols, LANES)
                up_ref[f * up_rows : (f + 1) * up_rows, pl.ds(at, cols)] = blocks_ref[
                    f, j * up_rows : (j + 1) * up_rows
                ]
            at = pl.multiple_of(col * cols, LANES)
            down_ref[f * down_rows : (f + 1) * down_rows, pl.ds(at, cols)] = blocks_ref[
                f, parts * up_rows :
            ]


def pack_mlp(place_ref, gup_s, gdown_s, outs):
    wide, deep = outs[0].shape[:2]
    fsdp = wide * deep
    far, me = place_ref[0], place_ref[1]
    width, hidden = gdown_s.shape
    up_rows, up_cols = width // fsdp, hidden // len(outs)
    down_rows, down_cols = width // len(outs), hidden // fsdp
    parts = up_cols // LANES
    for r, out in enumerate(outs):
        d = r ^ far
        for p in range(fsdp):
            i, k = p % wide, p // wide
            f = me ^ p
            here = pl.ds(pl.multiple_of(f * up_rows, 8), up_rows)
            for j in range(parts):
                at = pl.multiple_of((d * parts + j) * LANES, LANES)
                out[i, k, j * up_rows : (j + 1) * up_rows] = gup_s[here, pl.ds(at, LANES)].astype(
                    BF16
                )
            at = pl.multiple_of(d * down_rows, 8)
            cols = pl.ds(pl.multiple_of(f * down_cols, LANES), down_cols)
            out[i, k, parts * up_rows :] = gdown_s[pl.ds(at, down_rows), cols].astype(BF16)


def mlp_kernel(place_ref, z_ref, cot_ref, cot_row_ref, norms_ref, *refs, packed):
    if packed:
        block_refs, refs = refs[:packed], refs[packed:]
        out_ref, out_row_ref, dz_ref, dz_row_ref, e_ref, sums_ref = refs[:6]
        grad_refs, refs = refs[6 : 6 + packed], refs[6 + packed :]
        dz_s, gup_s, gdown_s, acc_s, h_s, dg_s, g_s, eh_s, up_ref, down_ref = refs
    else:
        up_ref, down_ref, out_ref, out_row_ref, dz_ref, dz_row_ref, e_ref, sums_ref = refs[:8]
        grad_refs, refs = refs[8:10], refs[10:]
        dz_s, gup_s, gdown_s, acc_s, h_s, dg_s, g_s, eh_s = refs
    rows, width = z_ref.shape
    hidden = up_ref.shape[1]
    step = pl.program_id(0)

    @pl.when(step == 0)
    def _():
        if packed:
            assemble_mlp(place_ref, block_refs, up_ref, down_ref)
        dz_s[...] = jnp.zeros_like(dz_s)
        gup_s[...] = jnp.zeros_like(gup_s)
        gdown_s[...] = jnp.zeros_like(gdown_s)
        sums_ref[...] = jnp.zeros_like(sums_ref)

    build_windows(dz_s, cot_ref, cot_row_ref)
    hat, inv_std = normalise(z_ref[...])
    u = (hat * norms_ref[2:3] + norms_ref[5:6]).astype(BF16)
    e2 = dz_s[...].astype(BF16)
    ones = jnp.ones((16, rows), BF16)
    ut = jnp.concatenate([u.T, ones], axis=0)
    et = e2.T
    chunks = hidden // width
    strip = 16
    half = width // 2

    def begin(c):
        def up(n):
            cols = slice(c * width + n, c * width + n + half)
            h_s[c % 2, :, n : n + half] = dot_nn(u, up_ref[:, cols])

        def down(n):
            cols = slice(c * width + n, c * width + n + half)
            dg_s[c % 2, :, n : n + half] = dot_nt(e2, down_ref[cols, :])

        return [partial(f, n) for n in (0, half) for f in (up, down)]

    def middle(c):
        def part(r):
            bias = norms_ref[9 + c : 10 + c]
            g, slope = gelu_pair(h_s[c % 2, r : r + strip] + bias)
            g_s[c % 2, r : r + strip] = g.astype(BF16)
            eh_s[c % 2, r : r + strip] = (dg_s[c % 2, r : r + strip] * slope).astype(BF16)

        return [partial(part, r) for r in range(0, rows, strip)]

    def finish(c):
        whole = slice(c * width, (c + 1) * width)

        def add(ref, i, n, x):
            if c == 0:
                ref[i, :, n : n + half] = x
            else:
                ref[i, :, n : n + half] += x

        def forward(n):
            add(acc_s, 0, n, dot_nn(g_s[c % 2], down_ref[whole, n : n + half]))

        def back(n):
            add(acc_s, 1, n, dot_nt(eh_s[c % 2], up_ref[n : n + half, whole]))

        def down(n):
            cols = slice(c * width + n, c * width + n + half)
            gdown_s[:, cols] += dot_nn(et, g_s[c % 2, :, n : n + half])

        def up(n):
            cols = slice(c * width + n, c * width + n + half)
            gup_s[:, cols] += dot_nn(ut, eh_s[c % 2, :, n : n + half])

        return [partial(f, n) for n in (0, half) for f in (forward, back, down, up)]

    for f in begin(0):
        f()
    for c in range(chunks):
        products = begin(c + 1) if c + 1 < chunks else []
        if c > 0:
            products = products + finish(c - 1)
        strips = middle(c)
        done = 0
        for i, f in enumerate(strips):
            f()
            upto = len(products) * (i + 1) // len(strips)
            for g in products[done:upto]:
                g()
            done = upto
    for f in finish(chunks - 1):
        f()
    z2 = z_ref[...] + acc_s[0] + norms_ref[13:14]
    split_windows(z2, out_ref, out_row_ref)
    du = acc_s[1]
    dz2 = dz_s[...]
    sums_ref[1:2, :width] += jnp.sum(e2.astype(F32), axis=0, keepdims=True)
    sums_ref[2:3, :width] += jnp.sum(du * hat, axis=0, keepdims=True)
    sums_ref[3:4, :width] += jnp.sum(du, axis=0, keepdims=True)
    dz1 = dz2 + norm_back(du, hat, inv_std, norms_ref[2:3])
    dz_ref[...] = dz1
    local_len = cot_ref.shape[1]
    for w in range(cot_ref.shape[0]):
        at = w * PITCH + local_len
        dz_row_ref[w : w + 1] = dz1[at : at + 1]
    e = dz1.astype(BF16)
    e_ref[...] = e
    sums_ref[4:5, :width] += jnp.sum(e.astype(F32), axis=0, keepdims=True)

    @pl.when(step == pl.num_programs(0) - 1)
    def _():
        sums_ref[0:1, :] = gup_s[width : width + 1, :]
        if packed:
            pack_mlp(place_ref, gup_s, gdown_s, grad_refs)
        else:
            grad_refs[0][...] = gup_s[:width].astype(BF16)
            grad_refs[1][...] = gdown_s[...].astype(BF16)


def window_backward_kernel(
    e_ref,
    qkv_ref,
    p_ref,
    hat_ref,
    o_ref,
    wproj_ref,
    *refs,
    local_len,
):
    mixed_ref, mixed_row_ref, sums_ref, gqkv_ref, gproj_ref, do_s, mixed_s = refs[-7:]
    rows, width = e_ref.shape
    count = qkv_ref.shape[0]

    @pl.when(pl.program_id(0) == 0)
    def _():
        do_s[rows:, :] = jnp.zeros((do_s.shape[0] - rows, width), F32)
        for ref in (sums_ref, gqkv_ref, gproj_ref):
            ref[...] = jnp.zeros_like(ref)

    do_s[:rows, :] = dot_nt(e_ref[...], wproj_ref[...])
    gproj_ref[...] += dot_tn(o_ref[...], e_ref[...])
    masks = head_masks(SLOT)

    spots = [c * LANES for c in range(width // LANES)]

    def window(w):
        base = pl.multiple_of(w * PITCH, 8)
        upstream, slopes = [], []
        for at in spots:
            do = spread(do_s[pl.ds(base, SLOT), at : at + LANES].astype(BF16), masks)
            v = qkv_ref[w, :, 2 * width + at : 2 * width + at + LANES]
            slopes.append(dot_nt(v, do))
            upstream.append(do)
        for c, at in enumerate(spots):
            dv = dot_nn(p_ref[w, c], upstream[c])
            mixed_s[pl.ds(base, PITCH), 2 * width + at : 2 * width + at + LANES] = dv[:PITCH]
        scores = []
        for c, dp in enumerate(slopes):
            p = p_ref[w, c].astype(F32)
            ds = p * (dp - jnp.sum(dp * p, axis=0, keepdims=True))
            scores.append(ds.astype(BF16))
        turned = [turn(ds) for ds in scores]
        for at, ds in zip(spots, scores):
            dk = dot_nn(ds, spread(qkv_ref[w, :, at : at + LANES], masks)) * FACTOR
            mixed_s[pl.ds(base, PITCH), width + at : width + at + LANES] = dk[:PITCH]
        for at, ds in zip(spots, turned):
            k = qkv_ref[w, :, width + at : width + at + LANES]
            dq = dot_nn(ds, spread(k, masks, TURNED)) * FACTOR
            mixed_s[pl.ds(base, PITCH), at : at + LANES] = dq[:PITCH]

    def windows(i, carry):
        for j in range(2):
            window(2 * i + j)
        return carry

    lax.fori_loop(0, count // 2, windows, 0)
    mixed = mixed_s[...].astype(BF16)
    mixed_ref[...] = mixed
    for w in range(count):
        at = w * PITCH + local_len
        mixed_row_ref[w : w + 1] = mixed_s[at : at + 1].astype(BF16)
    sums_ref[0:1, :] += jnp.sum(mixed.astype(F32), axis=0, keepdims=True)
    gqkv_ref[...] += dot_tn(hat_ref[...], mixed)


def local_back_kernel(local_ref, dz_ref, mixed_ref, wqkv_ref, norms_ref, *refs):
    out_ref, tick_ref, z_s = refs[-3:]
    tick_ref[...] = jnp.zeros_like(tick_ref)
    count, local_len, _ = local_ref.shape

    @pl.when(pl.program_id(0) == 0)
    def _():
        z_s[...] = jnp.zeros_like(z_s)

    for w in range(count):
        z_s[w * PITCH : w * PITCH + local_len] = local_ref[w].astype(F32)
    du = dot_nt(mixed_ref[...], wqkv_ref[...])
    hat, inv_std = normalise(z_s[...])
    dz0 = dz_ref[...] + norm_back(du, hat, inv_std, norms_ref[1:2])
    for w in range(count):
        out_ref[w] = dz0[w * PITCH : w * PITCH + local_len].astype(BF16)


def pack_attention(place_ref, gqkv_s, gproj_s, small_s, du_s, own, outs):
    wide, deep = outs[0].shape[:2]
    peers = wide * deep
    width = gproj_s.shape[0]
    rows = width // peers
    quads = width // LANES
    counts = [gqkv_s.shape[1] // len(outs) // LANES, gproj_s.shape[1] // len(outs) // LANES]
    far, me = place_ref[0], place_ref[1]
    linear = far * peers + me
    near = du_s.shape[0] // own
    for r, out in enumerate(outs):
        d = r ^ far
        for p in range(peers):
            j, i = p % wide, p // wide
            f = me ^ p
            here = pl.ds(pl.multiple_of(f * rows, 8), rows)
            row = 0
            for count, grad in zip(counts, (gqkv_s, gproj_s)):
                for c in range(count):
                    at = pl.ds(pl.multiple_of((d * count + c) * LANES, LANES), LANES)
                    out[j, i, row : row + rows] = grad[here, at].astype(BF16)
                    row += rows
            out[j, i, row : row + rows] = small_s[here].astype(BF16)
            row += rows
            away = d * peers + f - linear + near // 2
            inside = (away >= 0) & (away < near)
            at = pl.ds(pl.multiple_of(jnp.where(inside, away, 0) * own, 8), own)
            share = jnp.where(inside, 1.0, 0.0)
            for c in range(quads):
                term = du_s[at, c * LANES : (c + 1) * LANES] * share
                out[j, i, row : row + own] = term.astype(BF16)
                row += own


def region_tail_kernel(
    place_ref,
    mixed_row_ref,
    dz_row_ref,
    mid_ref,
    hat_ref,
    qkv_ref,
    p_ref,
    o_ref,
    wqkv_ref,
    wproj_ref,
    norms_ref,
    gqkv_in_ref,
    gproj_in_ref,
    att_sums_ref,
    mlp_sums_ref,
    tie_ref,
    dmid_ref,
    *refs,
    packed,
):
    outs, refs = (refs[:packed], refs[packed:]) if packed else (refs[:4], refs[4:])
    near_s, du_s, gqkv_s, gproj_s, lines_s, small_s = refs
    own, width = mid_ref.shape
    rows = qkv_ref.shape[0]
    first = (rows - own) // 2
    mine = slice(first, first + own)

    mid_hat, mid_std = normalise(mid_ref[...])
    row_du = dot_nt(mixed_row_ref[...], wqkv_ref[...])
    dmid = dz_row_ref[...] + norm_back(row_du, mid_hat, mid_std, norms_ref[1:2])
    dmid_ref[...] = dmid
    e = dmid.astype(BF16)
    do = dot_nt(e, wproj_ref[...])
    do = jnp.concatenate([do, jnp.zeros((SLOT - own, width), F32)], axis=0).astype(BF16)
    masks = head_masks(SLOT)
    out_masks = [m.astype(F32) for m in masks]
    dqs = []
    for c in range(width // LANES):
        at = c * LANES
        q = qkv_ref[first : first + SLOT, at : at + LANES]
        k = qkv_ref[:, width + at : width + at + LANES]
        v = qkv_ref[:, 2 * width + at : 2 * width + at + LANES]
        dox = spread(do[:, at : at + LANES], masks)
        p = p_ref[c]
        near_s[:, width + at : width + at + LANES] = dot_nn(p, dox).astype(BF16)
        dp = dot_nt(v, dox)
        pf = p.astype(F32)
        ds = (pf * (dp - jnp.sum(dp * pf, axis=0, keepdims=True))).astype(BF16)
        near_s[:, at : at + LANES] = (dot_nn(ds, spread(q, masks)) * FACTOR).astype(BF16)
        wide = dot_tn(ds, k)
        dq = sum(wide[h * SLOT : (h + 1) * SLOT] * out_masks[h] for h in range(GROUP))
        dqs.append((dq[:own] * FACTOR).astype(BF16))
    dq = jnp.concatenate(dqs, axis=1)
    near = near_s[...]

    du_s[...] = dot_nt(near, wqkv_ref[:, width:])
    du_s[mine] += dot_nt(dq, wqkv_ref[:, :width])

    win_sum = att_sums_ref[0:1]
    near_sum = jnp.concatenate(
        [
            jnp.sum(dq.astype(F32), axis=0, keepdims=True),
            jnp.sum(near.astype(F32), axis=0, keepdims=True),
        ],
        axis=1,
    )
    sums = jnp.concatenate([near_sum, win_sum, jnp.zeros((6, 3 * width), F32)], axis=0)
    high = sums.astype(BF16)
    rest = (sums - high.astype(F32)).astype(BF16)
    both = jnp.concatenate([high, rest], axis=0)
    shifts = dot_nt(both, wqkv_ref[...])
    shifts = shifts[:8] + shifts[8:]
    lines_s[...] = jnp.zeros_like(lines_s)
    lines_s[:16] = norms_ref[...]
    columns = lines_s[...].T
    gain_0, gain_1 = columns[:, 0:1], columns[:, 1:2]
    shift_0, shift_1 = columns[:, 3:4], columns[:, 4:5]
    dgain_0 = jnp.zeros((width, 1), F32)
    dgain_1 = jnp.zeros((width, 1), F32)
    for i in range(3):
        cols = slice(i * width, (i + 1) * width)
        if i == 0:
            region = dot_tn(hat_ref[mine, :], dq)
        else:
            region = dot_tn(hat_ref[...], near[:, (i - 1) * width : i * width])
        window = gqkv_in_ref[:, cols]
        weight = wqkv_ref[:, cols].astype(F32)
        dgain_0 += jnp.sum(weight * region, axis=1, keepdims=True)
        dgain_1 += jnp.sum(weight * window, axis=1, keepdims=True)
        gqkv_s[:, cols] = (
            region * gain_0
            + window * gain_1
            + shift_0 * near_sum[:, cols]
            + shift_1 * win_sum[:, cols]
        )
    gproj_s[...] = gproj_in_ref[...] + dot_tn(o_ref[...], e)
    total = near_sum + win_sum
    hidden = mlp_sums_ref.shape[1]
    lines = [
        None,
        None,
        mlp_sums_ref[2:3, :width],
        shifts[0:1],
        shifts[1:2],
        mlp_sums_ref[3:4, :width],
        total[:, :width],
        total[:, 2 * width :],
        jnp.sum(e.astype(F32), axis=0, keepdims=True) + mlp_sums_ref[4:5, :width],
    ]
    lines += [mlp_sums_ref[0:1, c * width : (c + 1) * width] for c in range(hidden // width)]
    lines += [mlp_sums_ref[1:2, :width]]
    lines_s[...] = jnp.zeros_like(lines_s)
    for i, line in enumerate(lines):
        if line is not None:
            lines_s[i : i + 1] = line
    small_s[...] = lines_s[...].T
    small_s[:, 0:1] = dgain_0
    small_s[:, 1:2] = dgain_1
    if packed:
        pack_attention(place_ref, gqkv_s, gproj_s, small_s, du_s, own, outs)
    else:
        outs[0][...] = gqkv_s[...].astype(BF16)
        outs[1][...] = gproj_s[...].astype(BF16)
        outs[2][...] = small_s[...]
        outs[3][...] = du_s[...].astype(BF16)


def finish_kernel(
    x_ref,
    dmid_ref,
    norms_ref,
    *refs,
    terms,
):
    mlp_refs, refs = refs[:terms], refs[terms:]
    term_refs, outs = refs[:terms], refs[terms + 1 : -1]
    out_ref, gqkv_ref, gproj_ref, gup_ref, gdown_ref, ggains_ref, gbiases_ref = outs
    small_s = refs[-1]
    own, width = x_ref.shape

    def total(row, count, parts=term_refs):
        here = slice(row, row + count)
        return sum([t[here].astype(F32) for t in parts[1:]], parts[0][here].astype(F32))

    rows = gqkv_ref.shape[0]
    row = 0
    for ref in (gqkv_ref, gproj_ref):
        for c in range(0, ref.shape[1], LANES):
            ref[:, c : c + LANES] = total(row, rows)
            row += rows
    small_s[:rows] = total(row, rows)
    small = small_s[...].T
    count = ggains_ref.shape[0]
    ggains_ref[...] = small[:count, :rows]
    gbiases_ref[...] = small[count : count + gbiases_ref.shape[0], :rows]
    row += rows
    du = jnp.concatenate([total(row + c * own, own) for c in range(width // LANES)], axis=1)
    hat, inv_std = normalise(x_ref[...].astype(F32))
    out_ref[...] = (dmid_ref[...] + norm_back(du, hat, inv_std, norms_ref[0:1])).astype(BF16)
    row = 0
    for c in range(0, gup_ref.shape[1], LANES):
        gup_ref[:, c : c + LANES] = total(row, rows, mlp_refs)
        row += rows
    gdown_ref[...] = total(row, gdown_ref.shape[1], mlp_refs).T


def region_end_kernel(x_ref, dmid_ref, norms_ref, *refs):
    near_refs, out_ref = refs[:-1], refs[-1]
    du = near_refs[0][...].astype(F32)
    for ref in near_refs[1:]:
        du = du + ref[...].astype(F32)
    hat, inv_std = normalise(x_ref[...].astype(F32))
    out_ref[...] = (dmid_ref[...] + norm_back(du, hat, inv_std, norms_ref[0:1])).astype(BF16)


def axis_rounds(size):
    rounds = []
    shift = 0
    while (1 << shift) < size:
        width = min(4, size >> shift)
        rounds.append((shift, width))
        shift += width.bit_length() - 1
    return rounds


def swap_by(x, axis, code):
    pairs = [(i, i ^ code) for i in range(lax.axis_size(axis))]
    return lax.ppermute(x, axis, pairs)


def gather_axis(x, axis, stacked=True):
    size = lax.axis_size(axis)
    rounds = axis_rounds(size)
    if not stacked and len(rounds) == 1:
        return [x] + [swap_by(x, axis, j) for j in range(1, size)], list(range(size))
    stack = x[None]
    codes = [0]
    for shift, width in reversed(rounds):
        parts = [stack] + [swap_by(stack, axis, j << shift) for j in range(1, width)]
        stack = jnp.concatenate(parts, axis=0)
        codes = [c ^ (j << shift) for j in range(width) for c in codes]
    return stack, codes


def in_order(stack, codes, axis):
    place = [0] * len(codes)
    for p, c in enumerate(codes):
        place[c] = p
    wanted = jnp.arange(len(codes), dtype=jnp.int32) ^ lax.axis_index(axis)
    return jnp.take(stack, jnp.asarray(place, dtype=jnp.int32)[wanted], axis=0)


def scatter_axis(blocks, axis):
    size = lax.axis_size(axis)
    me = lax.axis_index(axis)
    rest = blocks.shape[1:]
    for shift, width in axis_rounds(size):
        left = blocks.shape[0] // width
        cut = blocks.reshape((left, width) + rest)
        mine = (me >> shift) & (width - 1)
        total = lax.dynamic_index_in_dim(cut, mine, 1, keepdims=False).astype(jnp.float32)
        for j in range(1, width):
            out = lax.dynamic_index_in_dim(cut, mine ^ j, 1, keepdims=False)
            total = total + swap_by(out, axis, j << shift).astype(jnp.float32)
        blocks = total.astype(blocks.dtype)
    return blocks[0]


def join(blocks):
    dp, fsdp, rows, cols = blocks.shape
    return blocks.transpose(1, 2, 0, 3).reshape(fsdp * rows, dp * cols)


def cut(whole, dp, fsdp):
    rows, cols = whole.shape
    return whole.reshape(fsdp, rows // fsdp, dp, cols // dp).transpose(2, 0, 1, 3)


def scatter_all(blocks):
    return scatter_axis(scatter_axis(blocks, "dp"), "fsdp").astype(jnp.float32)


def shifted(x, by):
    axes = ("dp", "fsdp")
    peers = lax.axis_size(axes)
    pairs = [(i, i + by) for i in range(peers) if 0 <= i + by < peers]
    return lax.ppermute(x, axes, pairs)


def matched(x, by, second):
    axes = ("dp", "fsdp")
    peers = lax.axis_size(axes)
    pairs = []
    for i in range(peers):
        low = i % (2 * by) < by
        to = i + by if low != bool(second) else i - by
        if 0 <= to < peers:
            pairs.append((i, to))
    return lax.ppermute(x, axes, pairs)


def full(shape):
    return pl.BlockSpec(shape, lambda *_: (0,) * len(shape))


def once(shape):
    return pl.BlockSpec(shape, lambda *_: (0,) * len(shape), pipeline_mode=pl.Buffered(1))


def tiled(shape, begin=0):
    return pl.BlockSpec(shape, lambda i: (i + begin,) + (0,) * (len(shape) - 1))


def like(shape, dtype):
    return jax.ShapeDtypeStruct(shape, dtype)


def smem():
    return pl.BlockSpec(memory_space=pltpu.SMEM)


def vmem():
    return pl.BlockSpec(memory_space=pltpu.VMEM)


def gather_round(stack, axis, which):
    shift, width = axis_rounds(lax.axis_size(axis))[::-1][which]
    return [stack] + [swap_by(stack, axis, j << shift) for j in range(1, width)]


def gather_parts(block, axis):
    rounds = axis_rounds(lax.axis_size(axis))[::-1]
    parts = [block[None]]
    codes = [0]
    for which, (shift, width) in enumerate(rounds):
        parts = gather_round(jnp.concatenate(parts, axis=0), axis, which)
        codes = [c ^ (j << shift) for j in range(width) for c in codes]
    return parts, codes


def far_parts(parts):
    return parts + [
        swap_by(x, "dp", r) for r in range(1, lax.axis_size("dp")) for x in parts
    ]


def send_far(grads):
    return [swap_by(g, "dp", r) for r, g in enumerate(grads) if r > 0]


def send_round(terms, step):
    return [swap_by(x, "fsdp", j * step) for j, x in enumerate(terms) if j > 0]


def reduce_round(terms, got):
    total = terms[0].astype(F32)
    for x in got:
        total = total + x.astype(F32)
    return total.astype(BF16)


def takes(us):
    return pl.CostEstimate(flops=int(us * 1.1e9), bytes_accessed=int(us * 1e6), transcendentals=0)


def params():
    return pltpu.CompilerParams(vmem_limit_bytes=VMEM_BYTES)


def on_device(
    x_regional,
    x_local,
    w_qkv,
    w_proj,
    w_fc1,
    w_fc2,
    gains,
    biases,
    region_counts,
    cot_regional,
    cot_local,
):
    regions, local_len, width = x_local.shape
    group = 8
    steps = regions // group
    rows = group * PITCH
    all_rows = regions * PITCH
    quads = width // LANES
    span = (regions + MAX_REGIONS - 2) // regions
    all_regions = regions * lax.axis_size(("dp", "fsdp"))
    linear = lax.axis_index(("dp", "fsdp"))
    first_row = linear * regions
    dp, fsdp = lax.axis_size("dp"), lax.axis_size("fsdp")
    qkv_cols, proj_cols = w_qkv.shape[1], w_proj.shape[1]
    in_blocks = qkv_cols % LANES == 0 and proj_cols % LANES == 0 and w_fc2.shape[0] == LANES
    small_rows = gains.shape[0] + biases.shape[0]

    mlp_cols = w_fc2.shape[1]
    if in_blocks:
        att_rows = (qkv_cols + proj_cols + LANES) // LANES * w_qkv.shape[0]
        mlp_rows = w_fc1.shape[0] * w_fc1.shape[1] // mlp_cols + w_fc2.shape[0]
        att_block, mlp_block = pl.pallas_call(
            pack_weights_kernel,
            out_shape=(like((att_rows, LANES), BF16), like((mlp_rows, mlp_cols), BF16)),
            scratch_shapes=[pltpu.VMEM((LANES, LANES), F32)],
            compiler_params=params(),
            cost_estimate=takes(2),
            name="pack_weights",
        )(w_qkv, w_proj, gains, biases, w_fc1, w_fc2)
    else:
        small = jnp.concatenate([gains, biases], axis=0).T
        small = jnp.pad(small, ((0, 0), (0, LANES - small_rows)))
        att_block = jnp.concatenate([w_qkv, w_proj, small], axis=1)
        up_parts = [w_fc1[:, i : i + mlp_cols] for i in range(0, w_fc1.shape[1], mlp_cols)]
        mlp_block = jnp.concatenate(up_parts + [w_fc2], axis=0)
    hidden = w_fc1.shape[1] * dp

    place = jnp.stack([lax.axis_index("dp"), lax.axis_index("fsdp")]).astype(jnp.int32)
    near_rows = (2 * span + 1) * regions
    wide = axis_rounds(fsdp)[0][1]
    if in_blocks:
        att_parts, order = gather_parts(att_block, "fsdp")
        codes = (order, dp)
        near = [matched(x_regional, d, s) for d in range(1, span + 1) for s in range(2)]
        (*att_parts, x_own), near = lax.optimization_barrier(((*att_parts, x_regional), near))
        near = [x_own] + near
        att_stacks = far_parts(att_parts)
        mlp_half = lax.all_gather(mlp_block, "fsdp", axis=0, tiled=False)
    else:
        att_stack, order = gather_axis(att_block, "fsdp")
        codes = (order, dp)
        att_stacks, far_codes = gather_axis(att_stack, "dp")
        mlp_stack, _ = gather_axis(mlp_block, "fsdp")
        mlp_stack = in_order(mlp_stack, order, "fsdp")
        mlp_stack, _ = gather_axis(mlp_stack, "dp")
        mlp_stack = in_order(mlp_stack, far_codes, "dp")

    image_ends = jnp.minimum(jnp.cumsum(region_counts), all_regions)
    key_rows = first_row - span * regions + jnp.arange(near_rows, dtype=jnp.int32)
    key_image = jnp.sum((image_ends[None, :] <= key_rows[:, None]).astype(jnp.int32), axis=1)
    inside = (key_rows >= 0) & (key_rows < all_regions)
    key_image = jnp.where(inside, key_image, -1)
    query_image = jnp.pad(
        key_image[span * regions : (span + 1) * regions],
        (0, SLOT - regions),
        constant_values=-2,
    )
    query_image = jnp.tile(query_image, GROUP)[None]

    region_outs = (
        like((regions, width), F32),
        like((near_rows, width), BF16),
        like((near_rows, 3 * width), BF16),
        like((quads, near_rows, GROUP * SLOT), BF16),
        like((regions, width), BF16),
    )
    if in_blocks:
        whole = (
            like((width, 3 * width), BF16),
            like((width, width), BF16),
            like((16, width), F32),
        )
        region_mid, region_hat, region_qkv, region_p, region_o, qkv_full, proj_full, norms = (
            pl.pallas_call(
                partial(
                    region_forward_kernel, near=len(near), stacks=len(att_stacks), codes=codes
                ),
                in_specs=[smem()] + [vmem()] * (2 + len(near) + len(att_stacks)),
                out_shape=region_outs + whole,
                scratch_shapes=[
                    pltpu.VMEM((width, LANES), F32),
                    pltpu.VMEM((near_rows, width), F32),
                ],
                compiler_params=params(),
                cost_estimate=takes(6),
                name="region_forward",
            )(place, key_image[:, None], query_image, *near, *att_stacks)
        )
    else:
        near = [
            x_regional if offset == 0 else shifted(x_regional, -offset)
            for offset in range(-span, span + 1)
        ]
        blocks = in_order(jnp.stack([in_order(s, order, "fsdp") for s in att_stacks]), far_codes, "dp")
        qkv_full = join(blocks[..., :qkv_cols])
        proj_full = join(blocks[..., qkv_cols : qkv_cols + proj_cols])
        small = blocks[0, :, :, qkv_cols + proj_cols :].reshape(width, LANES)
        norms = small.astype(F32).T[:16]
        region_mid, region_hat, region_qkv, region_p, region_o = pl.pallas_call(
            partial(region_forward_kernel, near=len(near), stacks=0, codes=codes),
            in_specs=[smem()] + [vmem()] * (5 + len(near)),
            out_shape=region_outs,
            compiler_params=params(),
            cost_estimate=takes(6),
            name="region_forward",
        )(place, key_image[:, None], query_image, *near, qkv_full, proj_full, norms)

    first_half = steps // 2
    forward_outs = (
        like((all_rows, width), F32),
        like((all_rows, width), BF16),
        like((regions, SLOT, 3 * width), BF16),
        like((regions, quads, SLOT, GROUP * SLOT), BF16),
        like((all_rows, width), BF16),
        like((8, LANES), F32),
    )

    def window_forward(begin, count, held, ties):
        operands = (x_local, region_mid, qkv_full, proj_full, norms)
        return pl.pallas_call(
            window_forward_kernel,
            grid=(count,),
            in_specs=[
                tiled((group, local_len, width), begin),
                tiled((group, width), begin),
                full(qkv_full.shape),
                full(proj_full.shape),
                full(norms.shape),
            ]
            + [pl.BlockSpec(memory_space=pl.ANY)] * (len(held) + len(ties)),
            out_specs=[
                tiled((rows, width), begin),
                tiled((rows, width), begin),
                tiled((group, SLOT, 3 * width), begin),
                tiled((group, quads, SLOT, GROUP * SLOT), begin),
                tiled((rows, width), begin),
                full((8, LANES)),
            ],
            out_shape=forward_outs,
            scratch_shapes=[
                pltpu.VMEM((rows, width), F32),
                pltpu.VMEM((rows + 8, 3 * width), F32),
                pltpu.VMEM((rows, width), F32),
            ],
            input_output_aliases={len(operands) + i: i for i in range(len(held))},
            compiler_params=params(),
            cost_estimate=takes(6 * count),
            name="window_forward",
        )(*operands, *held, *ties)

    *held, tick = window_forward(0, first_half, (), ())
    if in_blocks:
        mlp_half, tick = lax.optimization_barrier((mlp_half, tick))
        mlp_stacks = far_parts([mlp_half])
    z1, win_hat, win_qkv, win_p, win_o, _ = window_forward(
        first_half, steps - first_half, held, (tick,)
    )

    mlp_group = 2 * group if in_blocks else group
    mlp_steps = regions // mlp_group
    mlp_rows_in = mlp_group * PITCH
    mlp_outs = [
        like(x_local.shape, BF16),
        like(x_regional.shape, BF16),
        like((all_rows, width), F32),
        like(x_regional.shape, F32),
        like((all_rows, width), BF16),
        like((8, hidden), F32),
    ]
    mlp_specs = [
        tiled((mlp_group, local_len, width)),
        tiled((mlp_group, width)),
        tiled((mlp_rows_in, width)),
        tiled((mlp_group, width)),
        tiled((mlp_rows_in, width)),
        full((8, hidden)),
    ]
    mlp_scratch = [
        pltpu.VMEM((mlp_rows_in, width), F32),
        pltpu.VMEM((width + 16, hidden), F32),
        pltpu.VMEM((width, hidden), F32),
        pltpu.VMEM((2, mlp_rows_in, width), F32),
        pltpu.VMEM((2, mlp_rows_in, width), F32),
        pltpu.VMEM((2, mlp_rows_in, width), F32),
        pltpu.VMEM((2, mlp_rows_in, width), BF16),
        pltpu.VMEM((2, mlp_rows_in, width), BF16),
    ]
    if in_blocks:
        weights = tuple(mlp_stacks)
        tall = mlp_block.shape[0] * mlp_cols // LANES
        grad_shapes = [(wide, fsdp // wide, tall, LANES)] * dp
        mlp_scratch += [pltpu.VMEM((width, hidden), BF16), pltpu.VMEM((hidden, width), BF16)]
    else:
        blocks = mlp_stack.transpose(1, 0, 2, 3)
        up_full = blocks[:, :, : mlp_block.shape[0] - w_fc2.shape[0]]
        up_full = up_full.reshape(fsdp, dp, -1, w_fc1.shape[0], mlp_cols)
        up_full = up_full.transpose(0, 3, 1, 2, 4).reshape(width, hidden)
        down_full = blocks[:, :, mlp_block.shape[0] - w_fc2.shape[0] :]
        down_full = down_full.transpose(0, 2, 1, 3).reshape(hidden, width)
        weights = (up_full, down_full)
        grad_shapes = [(width, hidden)] * 2
    out_local, out_regional, dz1, dz_row, win_e, mlp_sums, *mlp_grads = pl.pallas_call(
        partial(mlp_kernel, packed=dp if in_blocks else 0),
        grid=(mlp_steps,),
        in_specs=[
            smem(),
            tiled((mlp_rows_in, width)),
            tiled((mlp_group, local_len, width)),
            tiled((mlp_group, width)),
            full(norms.shape),
        ]
        + [once(w.shape) for w in weights],
        out_specs=mlp_specs + [once(g) for g in grad_shapes],
        out_shape=mlp_outs + [like(g, BF16) for g in grad_shapes],
        scratch_shapes=mlp_scratch,
        compiler_params=params(),
        cost_estimate=takes(50),
        name="mlp",
    )(place, z1, cot_local, cot_regional, norms, *weights)

    ties, tail_tie = (), norms
    if in_blocks:
        far = send_far(mlp_grads)
        mlp_terms = [
            sum([g[j].astype(F32) for g in far], mlp_grads[0][j].astype(F32)).astype(BF16)
            for j in range(wide)
        ]
        mlp_got = send_round(mlp_terms, 1)
        ties = tuple(mlp_terms)

    win_mixed, mixed_row, att_sums, grad_qkv, grad_proj = pl.pallas_call(
        partial(window_backward_kernel, local_len=local_len),
        grid=(steps,),
        in_specs=[
            tiled((rows, width)),
            tiled((group, SLOT, 3 * width)),
            tiled((group, quads, SLOT, GROUP * SLOT)),
            tiled((rows, width)),
            tiled((rows, width)),
            full(proj_full.shape),
        ]
        + [pl.BlockSpec(memory_space=pl.ANY)] * len(ties),
        out_specs=[
            tiled((rows, 3 * width)),
            tiled((group, 3 * width)),
            full((8, 3 * width)),
            full((width, 3 * width)),
            full((width, width)),
        ],
        out_shape=(
            like((all_rows, 3 * width), BF16),
            like((regions, 3 * width), BF16),
            like((8, 3 * width), F32),
            like((width, 3 * width), F32),
            like((width, width), F32),
        ),
        scratch_shapes=[
            pltpu.VMEM((rows + 8, width), F32),
            pltpu.VMEM((rows, 3 * width), F32),
        ],
        compiler_params=params(),
        cost_estimate=takes(35),
        name="window_backward",
    )(win_e, win_qkv, win_p, win_hat, win_o, proj_full, *ties)
    if in_blocks:
        (*mlp_got, mixed_row) = lax.optimization_barrier((*mlp_got, mixed_row))
        tail_tie = reduce_round(mlp_terms, mlp_got)
        mlp_terms = [tail_tie[j] for j in range(fsdp // wide)]
        mlp_terms = mlp_terms[:1] + send_round(mlp_terms, wide)

    if in_blocks:
        tall = att_rows + regions * quads
        grad_shapes = [like((wide, fsdp // wide, tall, LANES), BF16)] * dp
    else:
        grad_shapes = [
            like((width, 3 * width), BF16),
            like((width, width), BF16),
            like((width, LANES), F32),
            like((near_rows, width), BF16),
        ]
    operands = (
        mixed_row,
        dz_row,
        region_mid,
        region_hat,
        region_qkv,
        region_p,
        region_o,
        qkv_full,
        proj_full,
        norms,
        grad_qkv,
        grad_proj,
        att_sums,
        mlp_sums,
        tail_tie,
    )
    dmid, *att_grads = pl.pallas_call(
        partial(region_tail_kernel, packed=dp if in_blocks else 0),
        in_specs=[smem()]
        + [vmem()] * (len(operands) - 1)
        + [pl.BlockSpec(memory_space=pl.ANY)],
        out_shape=[like((regions, width), F32)] + grad_shapes,
        scratch_shapes=[
            pltpu.VMEM((near_rows, 2 * width), BF16),
            pltpu.VMEM((near_rows, width), F32),
            pltpu.VMEM((width, 3 * width), F32),
            pltpu.VMEM((width, width), F32),
            pltpu.VMEM((LANES, width), F32),
            pltpu.VMEM((width, LANES), F32),
        ],
        compiler_params=params(),
        cost_estimate=takes(10),
        name="region_tail",
    )(place, *operands)

    def local_back(begin, count, ties, held):
        return pl.pallas_call(
            local_back_kernel,
            grid=(count,),
            in_specs=[
                tiled((group, local_len, width), begin),
                tiled((rows, width), begin),
                tiled((rows, 3 * width), begin),
                full(qkv_full.shape),
                full(norms.shape),
            ]
            + [pl.BlockSpec(memory_space=pl.ANY)] * (len(ties) + len(held)),
            out_specs=[tiled((group, local_len, width), begin), full((8, LANES))],
            out_shape=(like(x_local.shape, BF16), like((8, LANES), F32)),
            scratch_shapes=[pltpu.VMEM((rows, width), F32)],
            input_output_aliases={5: 0} if held else {},
            compiler_params=params(),
            cost_estimate=takes(3 * count),
            name="local_back",
        )(x_local, dz1, win_mixed, qkv_full, norms, *held, *ties)

    cuts = [steps * i // 3 for i in range(4)]

    def local_part(i, ties, held):
        return local_back(cuts[i], cuts[i + 1] - cuts[i], ties, held)

    if in_blocks:
        far = send_far(att_grads)
        grad_local, tick = local_part(0, (att_grads[0],), ())
        (*far, tick) = lax.optimization_barrier((*far, tick))
        terms = [
            sum([g[j].astype(F32) for g in far], att_grads[0][j].astype(F32)).astype(BF16)
            for j in range(wide)
        ]
        got = send_round(terms, 1)
        grad_local, tick = local_part(1, (tick, terms[0]), (grad_local,))
        grad_local, tick = local_part(2, (), (grad_local,))
        (*got, tick) = lax.optimization_barrier((*got, tick))
        terms = reduce_round(terms, got)
        terms = [terms[j] for j in range(fsdp // wide)]
        terms = terms[:1] + send_round(terms, wide)
        operands = (x_regional, dmid, norms, *mlp_terms, *terms, tick)
        out_specs = (
            like(x_regional.shape, BF16),
            like(w_qkv.shape, F32),
            like(w_proj.shape, F32),
            like(w_fc1.shape, F32),
            like(w_fc2.shape, F32),
            like(gains.shape, F32),
            like(biases.shape, F32),
        )
        grad_regional, grad_qkv, grad_proj, grad_up, grad_down, grad_gains, grad_biases = (
            pl.pallas_call(
                partial(finish_kernel, terms=len(terms)),
                in_specs=[vmem()] * (len(operands) - 1) + [pl.BlockSpec(memory_space=pl.ANY)],
                out_shape=out_specs,
                scratch_shapes=[pltpu.VMEM((LANES, LANES), F32)],
                compiler_params=params(),
                cost_estimate=takes(2),
                name="finish",
            )(*operands)
        )
    else:
        up_rows = w_fc1.shape[0]
        up_blocks = cut(mlp_grads[0], dp, fsdp).reshape(dp, fsdp, up_rows, -1, mlp_cols)
        up_blocks = up_blocks.transpose(0, 1, 3, 2, 4).reshape(dp, fsdp, -1, mlp_cols)
        down_blocks = cut(mlp_grads[1].T, dp, fsdp)
        mlp_sum = scatter_all(jnp.concatenate([up_blocks, down_blocks], axis=2))
        grad_up = mlp_sum[: up_blocks.shape[2]].reshape(-1, up_rows, mlp_cols)
        grad_up = grad_up.transpose(1, 0, 2).reshape(w_fc1.shape)
        grad_down = mlp_sum[up_blocks.shape[2] :]
        grad_qkv, grad_proj, small, du_near = att_grads
        small = small.astype(BF16).reshape(1, fsdp, -1, LANES)
        small = jnp.broadcast_to(small, (dp,) + small.shape[1:])
        blocks = [cut(grad_qkv, dp, fsdp), cut(grad_proj, dp, fsdp), small]
        att = scatter_all(jnp.concatenate(blocks, axis=3))
        grad_qkv = att[:, :qkv_cols]
        grad_proj = att[:, qkv_cols : qkv_cols + proj_cols]
        small = att[:, qkv_cols + proj_cols :].T[:small_rows]
        grad_gains, grad_biases = small[: gains.shape[0]], small[gains.shape[0] :]
        held = ()
        for i in range(3):
            grad_local, tick = local_part(i, (), held)
            held = (grad_local,)
        returned = []
        for offset in range(-span, span + 1):
            part = du_near[(offset + span) * regions : (offset + span + 1) * regions]
            returned.append(part if offset == 0 else shifted(part, offset))
        grad_regional = pl.pallas_call(
            region_end_kernel,
            out_shape=like(x_regional.shape, BF16),
            compiler_params=params(),
            name="region_end",
        )(x_regional, dmid, norms, *returned)
    return (
        out_regional,
        out_local,
        grad_regional,
        grad_local,
        grad_qkv,
        grad_proj,
        grad_up,
        grad_down,
        grad_gains,
        grad_biases,
    )


def solution(mesh):
    in_specs = (
        P(("dp", "fsdp"), None),
        P(("dp", "fsdp"), None, None),
        P("fsdp", "dp"),
        P("fsdp", "dp"),
        P("fsdp", "dp"),
        P("fsdp", "dp"),
        P(None, "fsdp"),
        P(None, "fsdp"),
        P(),
        P(("dp", "fsdp"), None),
        P(("dp", "fsdp"), None, None),
    )
    out_specs = (
        P(("dp", "fsdp"), None),
        P(("dp", "fsdp"), None, None),
        P(("dp", "fsdp"), None),
        P(("dp", "fsdp"), None, None),
        P("fsdp", "dp"),
        P("fsdp", "dp"),
        P("fsdp", "dp"),
        P("fsdp", "dp"),
        P(None, "fsdp"),
        P(None, "fsdp"),
    )
    return jax.shard_map(
        on_device, mesh=mesh, in_specs=in_specs, out_specs=out_specs, check_vma=False
    )
```

```python
import math
from functools import partial

import jax
import jax.numpy as jnp
from jax import lax
from jax.experimental import pallas as pl
from jax.experimental.pallas import tpu as pltpu
from jax.sharding import PartitionSpec as P

HEAD_DIM = 32
MAX_REGIONS = 144
EPSILON = 1e-05
NEGATIVE = -1e30
PITCH = 56
SLOT = 64
LANES = 128
GROUP = LANES // HEAD_DIM
EXP_SCALE = HEAD_DIM ** (-0.5) * math.log2(math.e)
FACTOR = HEAD_DIM ** (-0.5)
VMEM_BYTES = 60 * 1024 * 1024

ERFC_P = 0.42
ERFC = (
    0.23681994,
    0.23965002,
    0.19433459,
    0.27000812,
    -0.13287422,
    0.44318139,
    -0.32169076,
    0.07057076,
)

BF16 = jnp.bfloat16
F32 = jnp.float32


def dot_nn(a, b):
    return lax.dot_general(a, b, (((1,), (0,)), ((), ())), preferred_element_type=F32)


def dot_nt(a, b):
    return lax.dot_general(a, b, (((1,), (1,)), ((), ())), preferred_element_type=F32)


def dot_tn(a, b):
    return lax.dot_general(a, b, (((0,), (0,)), ((), ())), preferred_element_type=F32)


def normalise(x):
    centred = x - jnp.mean(x, axis=-1, keepdims=True)
    inv_std = lax.rsqrt(jnp.mean(centred * centred, axis=-1, keepdims=True) + EPSILON)
    return centred * inv_std, inv_std


def norm_back(dy, hat, inv_std, gain):
    scaled = dy * gain
    mean_s = jnp.mean(scaled, axis=-1, keepdims=True)
    mean_h = jnp.mean(scaled * hat, axis=-1, keepdims=True)
    return inv_std * (scaled - mean_s - hat * mean_h)


def head_masks(rows):
    lane = lax.broadcasted_iota(jnp.int32, (rows, LANES), 1) // HEAD_DIM
    return [jnp.where(lane == h, 1.0, 0.0).astype(BF16) for h in range(GROUP)]


def spread(x, masks, order=(0, 1, 2, 3)):
    return jnp.concatenate([x * masks[h] for h in order], axis=0)


def turn(p):
    both = jnp.concatenate([p[:, :LANES], p[:, LANES:]], axis=0).T
    return jnp.concatenate([both[:SLOT], both[SLOT:]], axis=1)


TURNED = (0, 2, 1, 3)


def gelu_pair(h):
    h = h.astype(BF16)
    z = jnp.abs(h) * jnp.asarray(ERFC_P * math.sqrt(0.5), BF16) + jnp.asarray(1.0, BF16)
    t = pl.reciprocal(z, approx=True)
    bell = jnp.exp2(h * h * jnp.asarray(-0.5 * math.log2(math.e), BF16))
    poly = jnp.full_like(t, 0.5 * ERFC[-1])
    for c in ERFC[-2::-1]:
        poly = poly * t + jnp.asarray(0.5 * c, BF16)
    tail = (poly * t) * bell
    cdf = jnp.where(h < 0, tail, 1 - tail)
    return h * cdf, cdf + (h * jnp.asarray(1.0 / math.sqrt(2.0 * math.pi), BF16)) * bell


def build_windows(z_ref, local_ref, row_ref):
    count, local_len, _ = local_ref.shape
    for w in range(count):
        z_ref[w * PITCH : w * PITCH + local_len] = local_ref[w].astype(F32)
        z_ref[w * PITCH + local_len : w * PITCH + local_len + 1] = row_ref[w : w + 1].astype(F32)


def split_windows(z, local_ref, row_ref):
    count, local_len, _ = local_ref.shape
    for w in range(count):
        local_ref[w] = z[w * PITCH : w * PITCH + local_len].astype(local_ref.dtype)
        row_ref[w : w + 1] = z[w * PITCH + local_len : w * PITCH + local_len + 1].astype(row_ref.dtype)


def pack_weights_kernel(
    wqkv_ref, wproj_ref, gains_ref, biases_ref, up_ref, down_ref, att_ref, mlp_ref, small_s
):
    row = 0
    small_s[...] = jnp.zeros_like(small_s)
    count, lanes = gains_ref.shape
    small_s[:count, :lanes] = gains_ref[...].astype(F32)
    small_s[count : count + biases_ref.shape[0], :lanes] = biases_ref[...].astype(F32)
    for ref in (wqkv_ref, wproj_ref, None):
        if ref is None:
            att_ref[row : row + lanes] = small_s[...].T[:lanes].astype(BF16)
            row += lanes
            continue
        for c in range(0, ref.shape[1], LANES):
            att_ref[row : row + ref.shape[0]] = ref[:, c : c + LANES]
            row += ref.shape[0]
    row = 0
    cols = down_ref.shape[1]
    for c in range(0, up_ref.shape[1], cols):
        mlp_ref[row : row + up_ref.shape[0]] = up_ref[:, c : c + cols]
        row += up_ref.shape[0]
    mlp_ref[row:] = down_ref[...]


def block_places(place_ref, stacks, codes):
    order, far_peers = codes
    per = len(stacks) // far_peers
    for i, stack in enumerate(stacks):
        deep = stack.shape[0]
        for k in range(deep):
            yield stack, k, place_ref[0] ^ (i // per), place_ref[1] ^ order[i % per * deep + k]


def assemble_attention(place_ref, stacks, codes, wqkv_ref, wproj_ref, norms_ref, small_s):
    peers, far_peers = len(codes[0]), codes[1]
    rows = wproj_ref.shape[0] // peers
    parts = [wqkv_ref.shape[1] // far_peers // LANES, wproj_ref.shape[1] // far_peers // LANES]
    for stack, k, d, f in block_places(place_ref, stacks, codes):
        here = pl.ds(pl.multiple_of(f * rows, rows), rows)
        row = 0
        for count, ref in zip(parts, (wqkv_ref, wproj_ref)):
            for j in range(count):
                to = pl.multiple_of((d * count + j) * LANES, LANES)
                ref[here, pl.ds(to, LANES)] = stack[k, row : row + rows]
                row += rows
        small_s[here] = stack[k, row : row + rows].astype(F32)
    norms_ref[...] = small_s[...].T[: norms_ref.shape[0]]


def pair_offsets(place_ref, peers, span):
    linear = place_ref[0] * peers + place_ref[1]
    for d in range(1, span + 1):
        low = lax.rem(linear, 2 * d) < d
        yield jnp.where(low, d, -d)
        yield jnp.where(low, -d, d)


def region_forward_kernel(place_ref, kid_ref, qid_ref, *refs, near, stacks, codes):
    x_refs, refs = refs[:near], refs[near:]
    if stacks:
        stack_refs, refs = refs[:stacks], refs[stacks:]
        mid_ref, hat_ref, qkv_ref, p_ref, o_ref, wqkv_ref, wproj_ref, norms_ref, small_s, x_s = refs
        assemble_attention(place_ref, stack_refs, codes, wqkv_ref, wproj_ref, norms_ref, small_s)
        own = mid_ref.shape[0]
        span = near // 2
        x_s[span * own : (span + 1) * own] = x_refs[0][...].astype(F32)
        for ref, by in zip(x_refs[1:], pair_offsets(place_ref, len(codes[0]), span)):
            x_s[pl.ds(pl.multiple_of((span + by) * own, 8), own)] = ref[...].astype(F32)
        x = x_s[...]
    else:
        wqkv_ref, wproj_ref, norms_ref, mid_ref, hat_ref, qkv_ref, p_ref, o_ref = refs
        x = jnp.concatenate([r[...].astype(F32) for r in x_refs], axis=0)
    own, width = mid_ref.shape
    rows = x.shape[0]
    first = (rows - own) // 2
    hat, _ = normalise(x)
    u = (hat * norms_ref[0:1] + norms_ref[3:4]).astype(BF16)
    hat_ref[...] = hat.astype(BF16)
    qkv = dot_nn(u, wqkv_ref[...])
    q = (qkv[:, :width] + norms_ref[6:7]).astype(BF16)
    k = qkv[:, width : 2 * width].astype(BF16)
    v = (qkv[:, 2 * width :] + norms_ref[7:8]).astype(BF16)
    qkv_ref[:, :width] = q
    qkv_ref[:, width : 2 * width] = k
    qkv_ref[:, 2 * width :] = v
    masks = head_masks(SLOT)
    same = kid_ref[...] == qid_ref[...]
    lane = lax.broadcasted_iota(jnp.int32, (1, GROUP * SLOT), 1)
    asked = (lane % SLOT) < own
    out_masks = [m.astype(F32) for m in masks]
    for c in range(width // LANES):
        cols = slice(c * LANES, (c + 1) * LANES)
        qx = spread(q[first : first + SLOT, cols], masks)
        s = jnp.where(same, dot_nt(k[:, cols], qx), NEGATIVE)
        e = jnp.exp2((s - jnp.max(s, axis=0, keepdims=True)) * EXP_SCALE)
        total = jnp.sum(e, axis=0, keepdims=True)
        p = (e * jnp.where(asked, 1.0 / total, 0.0)).astype(BF16)
        p_ref[c] = p
        mixed = dot_tn(p, v[:, cols])
        o = sum(mixed[h * SLOT : (h + 1) * SLOT] * out_masks[h] for h in range(GROUP))
        o_ref[:, cols] = o[:own].astype(BF16)
    mid_ref[...] = x[first : first + own] + dot_nn(o_ref[...], wproj_ref[...]) + norms_ref[8:9]


def window_forward_kernel(
    local_ref,
    row_ref,
    wqkv_ref,
    wproj_ref,
    norms_ref,
    *refs,
):
    z1_ref, hat_ref, qkv_ref, p_ref, o_ref, tick_ref, z_s, qkv_s, o_s = refs[-9:]
    tick_ref[...] = jnp.zeros_like(tick_ref)
    rows, width = z_s.shape
    count, local_len, _ = local_ref.shape

    @pl.when(pl.program_id(0) == 0)
    def _():
        z_s[...] = jnp.zeros_like(z_s)
        qkv_s[rows:, :] = jnp.zeros((qkv_s.shape[0] - rows, qkv_s.shape[1]), F32)

    build_windows(z_s, local_ref, row_ref)
    hat, _ = normalise(z_s[...])
    u = (hat * norms_ref[1:2] + norms_ref[4:5]).astype(BF16)
    hat_ref[...] = hat.astype(BF16)
    qkv_s[:rows, :width] = dot_nn(u, wqkv_ref[:, :width]) + norms_ref[6:7]
    qkv_s[:rows, width : 2 * width] = dot_nn(u, wqkv_ref[:, width : 2 * width])
    qkv_s[:rows, 2 * width :] = dot_nn(u, wqkv_ref[:, 2 * width :]) + norms_ref[7:8]
    masks = head_masks(SLOT)
    is_key = lax.broadcasted_iota(jnp.int32, (SLOT, GROUP * SLOT), 0) <= local_len
    lane = lax.broadcasted_iota(jnp.int32, (1, GROUP * SLOT), 1)
    asked = (lane % SLOT) <= local_len

    def window(w):
        base = pl.multiple_of(w * PITCH, 8)
        spots = [c * LANES for c in range(width // LANES)]
        scores, values = [], []
        for at in spots:
            q = qkv_s[pl.ds(base, SLOT), at : at + LANES].astype(BF16)
            k = qkv_s[pl.ds(base, SLOT), width + at : width + at + LANES].astype(BF16)
            v = qkv_s[pl.ds(base, SLOT), 2 * width + at : 2 * width + at + LANES].astype(BF16)
            qkv_ref[w, :, at : at + LANES] = q
            qkv_ref[w, :, width + at : width + at + LANES] = k
            qkv_ref[w, :, 2 * width + at : 2 * width + at + LANES] = v
            scores.append(dot_nt(k, spread(q, masks)))
            values.append(v)
        probs = []
        for c, s in enumerate(scores):
            s = jnp.where(is_key, s, NEGATIVE)
            e = jnp.exp2((s - jnp.max(s, axis=0, keepdims=True)) * EXP_SCALE)
            total = jnp.sum(e, axis=0, keepdims=True)
            p = (e * jnp.where(asked, 1.0 / total, 0.0)).astype(BF16)
            p_ref[w, c] = p
            probs.append(turn(p))
        for at, p, v in zip(spots, probs, values):
            o = dot_nn(p, spread(v, masks, TURNED))
            o_s[pl.ds(base, PITCH), at : at + LANES] = o[:PITCH]

    def windows(i, carry):
        for j in range(4):
            window(4 * i + j)
        return carry

    lax.fori_loop(0, count // 4, windows, 0)
    o = o_s[...].astype(BF16)
    o_ref[...] = o
    z1_ref[...] = z_s[...] + dot_nn(o, wproj_ref[...]) + norms_ref[8:9]


def assemble_mlp(place_ref, block_refs, up_ref, down_ref):
    fsdp, tall, cols = block_refs[0].shape
    far = place_ref[0]
    up_rows = up_ref.shape[0] // fsdp
    down_rows = down_ref.shape[0] // fsdp
    parts = (tall - down_rows) // up_rows
    for f in range(fsdp):
        for d, blocks_ref in enumerate(block_refs):
            col = d ^ far
            for j in range(parts):
                at = pl.multiple_of((col * parts + j) * cols, LANES)
                up_ref[f * up_rows : (f + 1) * up_rows, pl.ds(at, cols)] = blocks_ref[
                    f, j * up_rows : (j + 1) * up_rows
                ]
            at = pl.multiple_of(col * cols, LANES)
            down_ref[f * down_rows : (f + 1) * down_rows, pl.ds(at, cols)] = blocks_ref[
                f, parts * up_rows :
            ]


def pack_mlp(place_ref, gup_s, gdown_s, outs):
    wide, deep = outs[0].shape[:2]
    fsdp = wide * deep
    far, me = place_ref[0], place_ref[1]
    width, hidden = gdown_s.shape
    up_rows, up_cols = width // fsdp, hidden // len(outs)
    down_rows, down_cols = width // len(outs), hidden // fsdp
    parts = up_cols // LANES
    for r, out in enumerate(outs):
        d = r ^ far
        for p in range(fsdp):
            i, k = p % wide, p // wide
            f = me ^ p
            here = pl.ds(pl.multiple_of(f * up_rows, 8), up_rows)
            for j in range(parts):
                at = pl.multiple_of((d * parts + j) * LANES, LANES)
                out[i, k, j * up_rows : (j + 1) * up_rows] = gup_s[here, pl.ds(at, LANES)].astype(
                    BF16
                )
            at = pl.multiple_of(d * down_rows, 8)
            cols = pl.ds(pl.multiple_of(f * down_cols, LANES), down_cols)
            out[i, k, parts * up_rows :] = gdown_s[pl.ds(at, down_rows), cols].astype(BF16)


def mlp_kernel(place_ref, z_ref, cot_ref, cot_row_ref, norms_ref, *refs, packed):
    if packed:
        block_refs, refs = refs[:packed], refs[packed:]
        out_ref, out_row_ref, dz_ref, dz_row_ref, e_ref, sums_ref = refs[:6]
        grad_refs, refs = refs[6 : 6 + packed], refs[6 + packed :]
        dz_s, gup_s, gdown_s, acc_s, h_s, dg_s, g_s, eh_s, up_ref, down_ref = refs
    else:
        up_ref, down_ref, out_ref, out_row_ref, dz_ref, dz_row_ref, e_ref, sums_ref = refs[:8]
        grad_refs, refs = refs[8:10], refs[10:]
        dz_s, gup_s, gdown_s, acc_s, h_s, dg_s, g_s, eh_s = refs
    rows, width = z_ref.shape
    hidden = up_ref.shape[1]
    step = pl.program_id(0)

    @pl.when(step == 0)
    def _():
        if packed:
            assemble_mlp(place_ref, block_refs, up_ref, down_ref)
        dz_s[...] = jnp.zeros_like(dz_s)
        gup_s[...] = jnp.zeros_like(gup_s)
        gdown_s[...] = jnp.zeros_like(gdown_s)
        sums_ref[...] = jnp.zeros_like(sums_ref)

    build_windows(dz_s, cot_ref, cot_row_ref)
    hat, inv_std = normalise(z_ref[...])
    u = (hat * norms_ref[2:3] + norms_ref[5:6]).astype(BF16)
    e2 = dz_s[...].astype(BF16)
    ones = jnp.ones((16, rows), BF16)
    ut = jnp.concatenate([u.T, ones], axis=0)
    et = e2.T
    chunks = hidden // width
    strip = 32
    half = width // 2

    def begin(c):
        def up(n):
            cols = slice(c * width + n, c * width + n + half)
            h_s[c % 2, :, n : n + half] = dot_nn(u, up_ref[:, cols])

        def down(n):
            cols = slice(c * width + n, c * width + n + half)
            dg_s[c % 2, :, n : n + half] = dot_nt(e2, down_ref[cols, :])

        return [partial(f, n) for n in (0, half) for f in (up, down)]

    def middle(c):
        def part(r):
            bias = norms_ref[9 + c : 10 + c]
            g, slope = gelu_pair(h_s[c % 2, r : r + strip] + bias)
            g_s[c % 2, r : r + strip] = g
            eh_s[c % 2, r : r + strip] = dg_s[c % 2, r : r + strip].astype(BF16) * slope

        return [partial(part, r) for r in range(0, rows, strip)]

    def finish(c):
        whole = slice(c * width, (c + 1) * width)

        def add(ref, i, n, x):
            if c == 0:
                ref[i, :, n : n + half] = x
            else:
                ref[i, :, n : n + half] += x

        def forward(n):
            add(acc_s, 0, n, dot_nn(g_s[c % 2], down_ref[whole, n : n + half]))

        def back(n):
            add(acc_s, 1, n, dot_nt(eh_s[c % 2], up_ref[n : n + half, whole]))

        def down(n):
            cols = slice(c * width + n, c * width + n + half)
            gdown_s[:, cols] += dot_nn(et, g_s[c % 2, :, n : n + half])

        def up(n):
            cols = slice(c * width + n, c * width + n + half)
            gup_s[:, cols] += dot_nn(ut, eh_s[c % 2, :, n : n + half])

        return [partial(f, n) for n in (0, half) for f in (forward, back, down, up)]

    for f in begin(0):
        f()
    for c in range(chunks):
        products = begin(c + 1) if c + 1 < chunks else []
        if c > 0:
            products = products + finish(c - 1)
        strips = middle(c)
        done = 0
        for i, f in enumerate(strips):
            f()
            upto = len(products) * (i + 1) // len(strips)
            for g in products[done:upto]:
                g()
            done = upto
    for f in finish(chunks - 1):
        f()
    z2 = z_ref[...] + acc_s[0] + norms_ref[13:14]
    split_windows(z2, out_ref, out_row_ref)
    du = acc_s[1]
    dz2 = dz_s[...]
    sums_ref[1:2, :width] += jnp.sum(e2.astype(F32), axis=0, keepdims=True)
    sums_ref[2:3, :width] += jnp.sum(du * hat, axis=0, keepdims=True)
    sums_ref[3:4, :width] += jnp.sum(du, axis=0, keepdims=True)
    dz1 = dz2 + norm_back(du, hat, inv_std, norms_ref[2:3])
    dz_ref[...] = dz1
    local_len = cot_ref.shape[1]
    for w in range(cot_ref.shape[0]):
        at = w * PITCH + local_len
        dz_row_ref[w : w + 1] = dz1[at : at + 1]
    e = dz1.astype(BF16)
    e_ref[...] = e
    sums_ref[4:5, :width] += jnp.sum(e.astype(F32), axis=0, keepdims=True)

    @pl.when(step == pl.num_programs(0) - 1)
    def _():
        sums_ref[0:1, :] = gup_s[width : width + 1, :]
        if packed:
            pack_mlp(place_ref, gup_s, gdown_s, grad_refs)
        else:
            grad_refs[0][...] = gup_s[:width].astype(BF16)
            grad_refs[1][...] = gdown_s[...].astype(BF16)


def window_backward_kernel(
    e_ref,
    qkv_ref,
    p_ref,
    hat_ref,
    o_ref,
    wproj_ref,
    *refs,
    local_len,
):
    mixed_ref, mixed_row_ref, sums_ref, gqkv_ref, gproj_ref, do_s, mixed_s = refs[-7:]
    rows, width = e_ref.shape
    count = qkv_ref.shape[0]

    @pl.when(pl.program_id(0) == 0)
    def _():
        do_s[rows:, :] = jnp.zeros((do_s.shape[0] - rows, width), F32)
        for ref in (sums_ref, gqkv_ref, gproj_ref):
            ref[...] = jnp.zeros_like(ref)

    do_s[:rows, :] = dot_nt(e_ref[...], wproj_ref[...])
    gproj_ref[...] += dot_tn(o_ref[...], e_ref[...])
    masks = head_masks(SLOT)

    spots = [c * LANES for c in range(width // LANES)]

    def window(w):
        base = pl.multiple_of(w * PITCH, 8)
        upstream, slopes = [], []
        for at in spots:
            do = spread(do_s[pl.ds(base, SLOT), at : at + LANES].astype(BF16), masks)
            v = qkv_ref[w, :, 2 * width + at : 2 * width + at + LANES]
            slopes.append(dot_nt(v, do))
            upstream.append(do)
        for c, at in enumerate(spots):
            dv = dot_nn(p_ref[w, c], upstream[c])
            mixed_s[pl.ds(base, PITCH), 2 * width + at : 2 * width + at + LANES] = dv[:PITCH]
        scores = []
        for c, dp in enumerate(slopes):
            p = p_ref[w, c].astype(F32)
            ds = p * (dp - jnp.sum(dp * p, axis=0, keepdims=True))
            scores.append(ds.astype(BF16))
        turned = [turn(ds) for ds in scores]
        for at, ds in zip(spots, scores):
            dk = dot_nn(ds, spread(qkv_ref[w, :, at : at + LANES], masks)) * FACTOR
            mixed_s[pl.ds(base, PITCH), width + at : width + at + LANES] = dk[:PITCH]
        for at, ds in zip(spots, turned):
            k = qkv_ref[w, :, width + at : width + at + LANES]
            dq = dot_nn(ds, spread(k, masks, TURNED)) * FACTOR
            mixed_s[pl.ds(base, PITCH), at : at + LANES] = dq[:PITCH]

    def windows(i, carry):
        for j in range(4):
            window(4 * i + j)
        return carry

    lax.fori_loop(0, count // 4, windows, 0)
    mixed = mixed_s[...].astype(BF16)
    mixed_ref[...] = mixed
    for w in range(count):
        at = w * PITCH + local_len
        mixed_row_ref[w : w + 1] = mixed_s[at : at + 1].astype(BF16)
    sums_ref[0:1, :] += jnp.sum(mixed.astype(F32), axis=0, keepdims=True)
    gqkv_ref[...] += dot_tn(hat_ref[...], mixed)


def local_back_kernel(local_ref, dz_ref, mixed_ref, wqkv_ref, norms_ref, *refs):
    out_ref, tick_ref, z_s = refs[-3:]
    tick_ref[...] = jnp.zeros_like(tick_ref)
    count, local_len, _ = local_ref.shape

    @pl.when(pl.program_id(0) == 0)
    def _():
        z_s[...] = jnp.zeros_like(z_s)

    for w in range(count):
        z_s[w * PITCH : w * PITCH + local_len] = local_ref[w].astype(F32)
    du = dot_nt(mixed_ref[...], wqkv_ref[...])
    hat, inv_std = normalise(z_s[...])
    dz0 = dz_ref[...] + norm_back(du, hat, inv_std, norms_ref[1:2])
    for w in range(count):
        out_ref[w] = dz0[w * PITCH : w * PITCH + local_len].astype(BF16)


def pack_attention(place_ref, gqkv_s, gproj_s, small_s, du_s, own, outs):
    wide, deep = outs[0].shape[:2]
    peers = wide * deep
    width = gproj_s.shape[0]
    rows = width // peers
    quads = width // LANES
    counts = [gqkv_s.shape[1] // len(outs) // LANES, gproj_s.shape[1] // len(outs) // LANES]
    far, me = place_ref[0], place_ref[1]
    linear = far * peers + me
    near = du_s.shape[0] // own
    for r, out in enumerate(outs):
        d = r ^ far
        for p in range(peers):
            j, i = p % wide, p // wide
            f = me ^ p
            here = pl.ds(pl.multiple_of(f * rows, 8), rows)
            row = 0
            for count, grad in zip(counts, (gqkv_s, gproj_s)):
                for c in range(count):
                    at = pl.ds(pl.multiple_of((d * count + c) * LANES, LANES), LANES)
                    out[j, i, row : row + rows] = grad[here, at].astype(BF16)
                    row += rows
            out[j, i, row : row + rows] = small_s[here].astype(BF16)
            row += rows
            away = d * peers + f - linear + near // 2
            inside = (away >= 0) & (away < near)
            at = pl.ds(pl.multiple_of(jnp.where(inside, away, 0) * own, 8), own)
            share = jnp.where(inside, 1.0, 0.0)
            for c in range(quads):
                term = du_s[at, c * LANES : (c + 1) * LANES] * share
                out[j, i, row : row + own] = term.astype(BF16)
                row += own


def region_tail_kernel(
    place_ref,
    mixed_row_ref,
    dz_row_ref,
    mid_ref,
    hat_ref,
    qkv_ref,
    p_ref,
    o_ref,
    wqkv_ref,
    wproj_ref,
    norms_ref,
    gqkv_in_ref,
    gproj_in_ref,
    att_sums_ref,
    mlp_sums_ref,
    tie_ref,
    dmid_ref,
    *refs,
    packed,
):
    outs, refs = (refs[:packed], refs[packed:]) if packed else (refs[:4], refs[4:])
    near_s, du_s, gqkv_s, gproj_s, lines_s, small_s = refs
    own, width = mid_ref.shape
    rows = qkv_ref.shape[0]
    first = (rows - own) // 2
    mine = slice(first, first + own)

    mid_hat, mid_std = normalise(mid_ref[...])
    row_du = dot_nt(mixed_row_ref[...], wqkv_ref[...])
    dmid = dz_row_ref[...] + norm_back(row_du, mid_hat, mid_std, norms_ref[1:2])
    dmid_ref[...] = dmid
    e = dmid.astype(BF16)
    do = dot_nt(e, wproj_ref[...])
    do = jnp.concatenate([do, jnp.zeros((SLOT - own, width), F32)], axis=0).astype(BF16)
    masks = head_masks(SLOT)
    out_masks = [m.astype(F32) for m in masks]
    dqs = []
    for c in range(width // LANES):
        at = c * LANES
        q = qkv_ref[first : first + SLOT, at : at + LANES]
        k = qkv_ref[:, width + at : width + at + LANES]
        v = qkv_ref[:, 2 * width + at : 2 * width + at + LANES]
        dox = spread(do[:, at : at + LANES], masks)
        p = p_ref[c]
        near_s[:, width + at : width + at + LANES] = dot_nn(p, dox).astype(BF16)
        dp = dot_nt(v, dox)
        pf = p.astype(F32)
        ds = (pf * (dp - jnp.sum(dp * pf, axis=0, keepdims=True))).astype(BF16)
        near_s[:, at : at + LANES] = (dot_nn(ds, spread(q, masks)) * FACTOR).astype(BF16)
        wide = dot_tn(ds, k)
        dq = sum(wide[h * SLOT : (h + 1) * SLOT] * out_masks[h] for h in range(GROUP))
        dqs.append((dq[:own] * FACTOR).astype(BF16))
    dq = jnp.concatenate(dqs, axis=1)
    near = near_s[...]

    du_s[...] = dot_nt(near, wqkv_ref[:, width:])
    du_s[mine] += dot_nt(dq, wqkv_ref[:, :width])

    win_sum = att_sums_ref[0:1]
    near_sum = jnp.concatenate(
        [
            jnp.sum(dq.astype(F32), axis=0, keepdims=True),
            jnp.sum(near.astype(F32), axis=0, keepdims=True),
        ],
        axis=1,
    )
    sums = jnp.concatenate([near_sum, win_sum, jnp.zeros((6, 3 * width), F32)], axis=0)
    high = sums.astype(BF16)
    rest = (sums - high.astype(F32)).astype(BF16)
    both = jnp.concatenate([high, rest], axis=0)
    shifts = dot_nt(both, wqkv_ref[...])
    shifts = shifts[:8] + shifts[8:]
    lines_s[...] = jnp.zeros_like(lines_s)
    lines_s[:16] = norms_ref[...]
    columns = lines_s[...].T
    gain_0, gain_1 = columns[:, 0:1], columns[:, 1:2]
    shift_0, shift_1 = columns[:, 3:4], columns[:, 4:5]
    dgain_0 = jnp.zeros((width, 1), F32)
    dgain_1 = jnp.zeros((width, 1), F32)
    for i in range(3):
        cols = slice(i * width, (i + 1) * width)
        if i == 0:
            region = dot_tn(hat_ref[mine, :], dq)
        else:
            region = dot_tn(hat_ref[...], near[:, (i - 1) * width : i * width])
        window = gqkv_in_ref[:, cols]
        weight = wqkv_ref[:, cols].astype(F32)
        dgain_0 += jnp.sum(weight * region, axis=1, keepdims=True)
        dgain_1 += jnp.sum(weight * window, axis=1, keepdims=True)
        gqkv_s[:, cols] = (
            region * gain_0
            + window * gain_1
            + shift_0 * near_sum[:, cols]
            + shift_1 * win_sum[:, cols]
        )
    gproj_s[...] = gproj_in_ref[...] + dot_tn(o_ref[...], e)
    total = near_sum + win_sum
    hidden = mlp_sums_ref.shape[1]
    lines = [
        None,
        None,
        mlp_sums_ref[2:3, :width],
        shifts[0:1],
        shifts[1:2],
        mlp_sums_ref[3:4, :width],
        total[:, :width],
        total[:, 2 * width :],
        jnp.sum(e.astype(F32), axis=0, keepdims=True) + mlp_sums_ref[4:5, :width],
    ]
    lines += [mlp_sums_ref[0:1, c * width : (c + 1) * width] for c in range(hidden // width)]
    lines += [mlp_sums_ref[1:2, :width]]
    lines_s[...] = jnp.zeros_like(lines_s)
    for i, line in enumerate(lines):
        if line is not None:
            lines_s[i : i + 1] = line
    small_s[...] = lines_s[...].T
    small_s[:, 0:1] = dgain_0
    small_s[:, 1:2] = dgain_1
    if packed:
        pack_attention(place_ref, gqkv_s, gproj_s, small_s, du_s, own, outs)
    else:
        outs[0][...] = gqkv_s[...].astype(BF16)
        outs[1][...] = gproj_s[...].astype(BF16)
        outs[2][...] = small_s[...]
        outs[3][...] = du_s[...].astype(BF16)


def finish_kernel(
    x_ref,
    dmid_ref,
    norms_ref,
    *refs,
    terms,
):
    mlp_refs, refs = refs[:terms], refs[terms:]
    term_refs, outs = refs[:terms], refs[terms + 1 : -1]
    out_ref, gqkv_ref, gproj_ref, gup_ref, gdown_ref, ggains_ref, gbiases_ref = outs
    small_s = refs[-1]
    own, width = x_ref.shape

    def total(row, count, parts=term_refs):
        here = slice(row, row + count)
        return sum([t[here].astype(F32) for t in parts[1:]], parts[0][here].astype(F32))

    rows = gqkv_ref.shape[0]
    row = 0
    for ref in (gqkv_ref, gproj_ref):
        for c in range(0, ref.shape[1], LANES):
            ref[:, c : c + LANES] = total(row, rows)
            row += rows
    small_s[:rows] = total(row, rows)
    small = small_s[...].T
    count = ggains_ref.shape[0]
    ggains_ref[...] = small[:count, :rows]
    gbiases_ref[...] = small[count : count + gbiases_ref.shape[0], :rows]
    row += rows
    du = jnp.concatenate([total(row + c * own, own) for c in range(width // LANES)], axis=1)
    hat, inv_std = normalise(x_ref[...].astype(F32))
    out_ref[...] = (dmid_ref[...] + norm_back(du, hat, inv_std, norms_ref[0:1])).astype(BF16)
    row = 0
    for c in range(0, gup_ref.shape[1], LANES):
        gup_ref[:, c : c + LANES] = total(row, rows, mlp_refs)
        row += rows
    gdown_ref[...] = total(row, gdown_ref.shape[1], mlp_refs).T


def region_end_kernel(x_ref, dmid_ref, norms_ref, *refs):
    near_refs, out_ref = refs[:-1], refs[-1]
    du = near_refs[0][...].astype(F32)
    for ref in near_refs[1:]:
        du = du + ref[...].astype(F32)
    hat, inv_std = normalise(x_ref[...].astype(F32))
    out_ref[...] = (dmid_ref[...] + norm_back(du, hat, inv_std, norms_ref[0:1])).astype(BF16)


def axis_rounds(size):
    rounds = []
    shift = 0
    while (1 << shift) < size:
        width = min(4, size >> shift)
        rounds.append((shift, width))
        shift += width.bit_length() - 1
    return rounds


def swap_by(x, axis, code):
    pairs = [(i, i ^ code) for i in range(lax.axis_size(axis))]
    return lax.ppermute(x, axis, pairs)


def gather_axis(x, axis, stacked=True):
    size = lax.axis_size(axis)
    rounds = axis_rounds(size)
    if not stacked and len(rounds) == 1:
        return [x] + [swap_by(x, axis, j) for j in range(1, size)], list(range(size))
    stack = x[None]
    codes = [0]
    for shift, width in reversed(rounds):
        parts = [stack] + [swap_by(stack, axis, j << shift) for j in range(1, width)]
        stack = jnp.concatenate(parts, axis=0)
        codes = [c ^ (j << shift) for j in range(width) for c in codes]
    return stack, codes


def in_order(stack, codes, axis):
    place = [0] * len(codes)
    for p, c in enumerate(codes):
        place[c] = p
    wanted = jnp.arange(len(codes), dtype=jnp.int32) ^ lax.axis_index(axis)
    return jnp.take(stack, jnp.asarray(place, dtype=jnp.int32)[wanted], axis=0)


def scatter_axis(blocks, axis):
    size = lax.axis_size(axis)
    me = lax.axis_index(axis)
    rest = blocks.shape[1:]
    for shift, width in axis_rounds(size):
        left = blocks.shape[0] // width
        cut = blocks.reshape((left, width) + rest)
        mine = (me >> shift) & (width - 1)
        total = lax.dynamic_index_in_dim(cut, mine, 1, keepdims=False).astype(jnp.float32)
        for j in range(1, width):
            out = lax.dynamic_index_in_dim(cut, mine ^ j, 1, keepdims=False)
            total = total + swap_by(out, axis, j << shift).astype(jnp.float32)
        blocks = total.astype(blocks.dtype)
    return blocks[0]


def join(blocks):
    dp, fsdp, rows, cols = blocks.shape
    return blocks.transpose(1, 2, 0, 3).reshape(fsdp * rows, dp * cols)


def cut(whole, dp, fsdp):
    rows, cols = whole.shape
    return whole.reshape(fsdp, rows // fsdp, dp, cols // dp).transpose(2, 0, 1, 3)


def scatter_all(blocks):
    return scatter_axis(scatter_axis(blocks, "dp"), "fsdp").astype(jnp.float32)


def shifted(x, by):
    axes = ("dp", "fsdp")
    peers = lax.axis_size(axes)
    pairs = [(i, i + by) for i in range(peers) if 0 <= i + by < peers]
    return lax.ppermute(x, axes, pairs)


def matched(x, by, second):
    axes = ("dp", "fsdp")
    peers = lax.axis_size(axes)
    pairs = []
    for i in range(peers):
        low = i % (2 * by) < by
        to = i + by if low != bool(second) else i - by
        if 0 <= to < peers:
            pairs.append((i, to))
    return lax.ppermute(x, axes, pairs)


def full(shape):
    return pl.BlockSpec(shape, lambda *_: (0,) * len(shape))


def once(shape):
    return pl.BlockSpec(shape, lambda *_: (0,) * len(shape), pipeline_mode=pl.Buffered(1))


def tiled(shape, begin=0):
    return pl.BlockSpec(shape, lambda i: (i + begin,) + (0,) * (len(shape) - 1))


def like(shape, dtype):
    return jax.ShapeDtypeStruct(shape, dtype)


def smem():
    return pl.BlockSpec(memory_space=pltpu.SMEM)


def vmem():
    return pl.BlockSpec(memory_space=pltpu.VMEM)


def gather_round(stack, axis, which):
    shift, width = axis_rounds(lax.axis_size(axis))[::-1][which]
    return [stack] + [swap_by(stack, axis, j << shift) for j in range(1, width)]


def gather_parts(block, axis):
    rounds = axis_rounds(lax.axis_size(axis))[::-1]
    parts = [block[None]]
    codes = [0]
    for which, (shift, width) in enumerate(rounds):
        parts = gather_round(jnp.concatenate(parts, axis=0), axis, which)
        codes = [c ^ (j << shift) for j in range(width) for c in codes]
    return parts, codes


def far_parts(parts):
    return parts + [
        swap_by(x, "dp", r) for r in range(1, lax.axis_size("dp")) for x in parts
    ]


def send_far(grads):
    return [swap_by(g, "dp", r) for r, g in enumerate(grads) if r > 0]


def send_round(terms, step):
    return [swap_by(x, "fsdp", j * step) for j, x in enumerate(terms) if j > 0]


def reduce_round(terms, got):
    total = terms[0].astype(F32)
    for x in got:
        total = total + x.astype(F32)
    return total.astype(BF16)


def takes(us):
    return pl.CostEstimate(flops=int(us * 1.1e9), bytes_accessed=int(us * 1e6), transcendentals=0)


def params():
    return pltpu.CompilerParams(vmem_limit_bytes=VMEM_BYTES)


def on_device(
    x_regional,
    x_local,
    w_qkv,
    w_proj,
    w_fc1,
    w_fc2,
    gains,
    biases,
    region_counts,
    cot_regional,
    cot_local,
):
    regions, local_len, width = x_local.shape
    group = 8
    steps = regions // group
    rows = group * PITCH
    all_rows = regions * PITCH
    quads = width // LANES
    span = (regions + MAX_REGIONS - 2) // regions
    all_regions = regions * lax.axis_size(("dp", "fsdp"))
    linear = lax.axis_index(("dp", "fsdp"))
    first_row = linear * regions
    dp, fsdp = lax.axis_size("dp"), lax.axis_size("fsdp")
    qkv_cols, proj_cols = w_qkv.shape[1], w_proj.shape[1]
    in_blocks = qkv_cols % LANES == 0 and proj_cols % LANES == 0 and w_fc2.shape[0] == LANES
    small_rows = gains.shape[0] + biases.shape[0]

    mlp_cols = w_fc2.shape[1]
    if in_blocks:
        att_rows = (qkv_cols + proj_cols + LANES) // LANES * w_qkv.shape[0]
        mlp_rows = w_fc1.shape[0] * w_fc1.shape[1] // mlp_cols + w_fc2.shape[0]
        att_block, mlp_block = pl.pallas_call(
            pack_weights_kernel,
            out_shape=(like((att_rows, LANES), BF16), like((mlp_rows, mlp_cols), BF16)),
            scratch_shapes=[pltpu.VMEM((LANES, LANES), F32)],
            compiler_params=params(),
            cost_estimate=takes(2),
            name="pack_weights",
        )(w_qkv, w_proj, gains, biases, w_fc1, w_fc2)
    else:
        small = jnp.concatenate([gains, biases], axis=0).T
        small = jnp.pad(small, ((0, 0), (0, LANES - small_rows)))
        att_block = jnp.concatenate([w_qkv, w_proj, small], axis=1)
        up_parts = [w_fc1[:, i : i + mlp_cols] for i in range(0, w_fc1.shape[1], mlp_cols)]
        mlp_block = jnp.concatenate(up_parts + [w_fc2], axis=0)
    hidden = w_fc1.shape[1] * dp

    place = jnp.stack([lax.axis_index("dp"), lax.axis_index("fsdp")]).astype(jnp.int32)
    near_rows = (2 * span + 1) * regions
    wide = axis_rounds(fsdp)[0][1]
    if in_blocks:
        att_parts, order = gather_parts(att_block, "fsdp")
        codes = (order, dp)
        near = [matched(x_regional, d, s) for d in range(1, span + 1) for s in range(2)]
        (*att_parts, x_own), near = lax.optimization_barrier(((*att_parts, x_regional), near))
        near = [x_own] + near
        att_stacks = far_parts(att_parts)
        mlp_half = lax.all_gather(mlp_block, "fsdp", axis=0, tiled=False)
    else:
        att_stack, order = gather_axis(att_block, "fsdp")
        codes = (order, dp)
        att_stacks, far_codes = gather_axis(att_stack, "dp")
        mlp_stack, _ = gather_axis(mlp_block, "fsdp")
        mlp_stack = in_order(mlp_stack, order, "fsdp")
        mlp_stack, _ = gather_axis(mlp_stack, "dp")
        mlp_stack = in_order(mlp_stack, far_codes, "dp")

    image_ends = jnp.minimum(jnp.cumsum(region_counts), all_regions)
    key_rows = first_row - span * regions + jnp.arange(near_rows, dtype=jnp.int32)
    key_image = jnp.sum((image_ends[None, :] <= key_rows[:, None]).astype(jnp.int32), axis=1)
    inside = (key_rows >= 0) & (key_rows < all_regions)
    key_image = jnp.where(inside, key_image, -1)
    query_image = jnp.pad(
        key_image[span * regions : (span + 1) * regions],
        (0, SLOT - regions),
        constant_values=-2,
    )
    query_image = jnp.tile(query_image, GROUP)[None]

    region_outs = (
        like((regions, width), F32),
        like((near_rows, width), BF16),
        like((near_rows, 3 * width), BF16),
        like((quads, near_rows, GROUP * SLOT), BF16),
        like((regions, width), BF16),
    )
    if in_blocks:
        whole = (
            like((width, 3 * width), BF16),
            like((width, width), BF16),
            like((16, width), F32),
        )
        region_mid, region_hat, region_qkv, region_p, region_o, qkv_full, proj_full, norms = (
            pl.pallas_call(
                partial(
                    region_forward_kernel, near=len(near), stacks=len(att_stacks), codes=codes
                ),
                in_specs=[smem()] + [vmem()] * (2 + len(near) + len(att_stacks)),
                out_shape=region_outs + whole,
                scratch_shapes=[
                    pltpu.VMEM((width, LANES), F32),
                    pltpu.VMEM((near_rows, width), F32),
                ],
                compiler_params=params(),
                cost_estimate=takes(6),
                name="region_forward",
            )(place, key_image[:, None], query_image, *near, *att_stacks)
        )
    else:
        near = [
            x_regional if offset == 0 else shifted(x_regional, -offset)
            for offset in range(-span, span + 1)
        ]
        blocks = in_order(jnp.stack([in_order(s, order, "fsdp") for s in att_stacks]), far_codes, "dp")
        qkv_full = join(blocks[..., :qkv_cols])
        proj_full = join(blocks[..., qkv_cols : qkv_cols + proj_cols])
        small = blocks[0, :, :, qkv_cols + proj_cols :].reshape(width, LANES)
        norms = small.astype(F32).T[:16]
        region_mid, region_hat, region_qkv, region_p, region_o = pl.pallas_call(
            partial(region_forward_kernel, near=len(near), stacks=0, codes=codes),
            in_specs=[smem()] + [vmem()] * (5 + len(near)),
            out_shape=region_outs,
            compiler_params=params(),
            cost_estimate=takes(6),
            name="region_forward",
        )(place, key_image[:, None], query_image, *near, qkv_full, proj_full, norms)

    first_half = steps // 2
    forward_outs = (
        like((all_rows, width), F32),
        like((all_rows, width), BF16),
        like((regions, SLOT, 3 * width), BF16),
        like((regions, quads, SLOT, GROUP * SLOT), BF16),
        like((all_rows, width), BF16),
        like((8, LANES), F32),
    )

    def window_forward(begin, count, held, ties):
        operands = (x_local, region_mid, qkv_full, proj_full, norms)
        return pl.pallas_call(
            window_forward_kernel,
            grid=(count,),
            in_specs=[
                tiled((group, local_len, width), begin),
                tiled((group, width), begin),
                full(qkv_full.shape),
                full(proj_full.shape),
                full(norms.shape),
            ]
            + [pl.BlockSpec(memory_space=pl.ANY)] * (len(held) + len(ties)),
            out_specs=[
                tiled((rows, width), begin),
                tiled((rows, width), begin),
                tiled((group, SLOT, 3 * width), begin),
                tiled((group, quads, SLOT, GROUP * SLOT), begin),
                tiled((rows, width), begin),
                full((8, LANES)),
            ],
            out_shape=forward_outs,
            scratch_shapes=[
                pltpu.VMEM((rows, width), F32),
                pltpu.VMEM((rows + 8, 3 * width), F32),
                pltpu.VMEM((rows, width), F32),
            ],
            input_output_aliases={len(operands) + i: i for i in range(len(held))},
            compiler_params=params(),
            cost_estimate=takes(6 * count),
            name="window_forward",
        )(*operands, *held, *ties)

    *held, tick = window_forward(0, first_half, (), ())
    if in_blocks:
        mlp_half, tick = lax.optimization_barrier((mlp_half, tick))
        mlp_stacks = far_parts([mlp_half])
    z1, win_hat, win_qkv, win_p, win_o, _ = window_forward(
        first_half, steps - first_half, held, (tick,)
    )

    mlp_group = group
    mlp_steps = regions // mlp_group
    mlp_rows_in = mlp_group * PITCH
    mlp_outs = [
        like(x_local.shape, BF16),
        like(x_regional.shape, BF16),
        like((all_rows, width), F32),
        like(x_regional.shape, F32),
        like((all_rows, width), BF16),
        like((8, hidden), F32),
    ]
    mlp_specs = [
        tiled((mlp_group, local_len, width)),
        tiled((mlp_group, width)),
        tiled((mlp_rows_in, width)),
        tiled((mlp_group, width)),
        tiled((mlp_rows_in, width)),
        full((8, hidden)),
    ]
    mlp_scratch = [
        pltpu.VMEM((mlp_rows_in, width), F32),
        pltpu.VMEM((width + 16, hidden), F32),
        pltpu.VMEM((width, hidden), F32),
        pltpu.VMEM((2, mlp_rows_in, width), F32),
        pltpu.VMEM((2, mlp_rows_in, width), F32),
        pltpu.VMEM((2, mlp_rows_in, width), F32),
        pltpu.VMEM((2, mlp_rows_in, width), BF16),
        pltpu.VMEM((2, mlp_rows_in, width), BF16),
    ]
    if in_blocks:
        weights = tuple(mlp_stacks)
        tall = mlp_block.shape[0] * mlp_cols // LANES
        grad_shapes = [(wide, fsdp // wide, tall, LANES)] * dp
        mlp_scratch += [pltpu.VMEM((width, hidden), BF16), pltpu.VMEM((hidden, width), BF16)]
    else:
        blocks = mlp_stack.transpose(1, 0, 2, 3)
        up_full = blocks[:, :, : mlp_block.shape[0] - w_fc2.shape[0]]
        up_full = up_full.reshape(fsdp, dp, -1, w_fc1.shape[0], mlp_cols)
        up_full = up_full.transpose(0, 3, 1, 2, 4).reshape(width, hidden)
        down_full = blocks[:, :, mlp_block.shape[0] - w_fc2.shape[0] :]
        down_full = down_full.transpose(0, 2, 1, 3).reshape(hidden, width)
        weights = (up_full, down_full)
        grad_shapes = [(width, hidden)] * 2
    out_local, out_regional, dz1, dz_row, win_e, mlp_sums, *mlp_grads = pl.pallas_call(
        partial(mlp_kernel, packed=dp if in_blocks else 0),
        grid=(mlp_steps,),
        in_specs=[
            smem(),
            tiled((mlp_rows_in, width)),
            tiled((mlp_group, local_len, width)),
            tiled((mlp_group, width)),
            full(norms.shape),
        ]
        + [once(w.shape) for w in weights],
        out_specs=mlp_specs + [once(g) for g in grad_shapes],
        out_shape=mlp_outs + [like(g, BF16) for g in grad_shapes],
        scratch_shapes=mlp_scratch,
        compiler_params=params(),
        cost_estimate=takes(50),
        name="mlp",
    )(place, z1, cot_local, cot_regional, norms, *weights)

    ties, tail_tie = (), norms
    if in_blocks:
        far = send_far(mlp_grads)
        mlp_terms = [
            sum([g[j].astype(F32) for g in far], mlp_grads[0][j].astype(F32)).astype(BF16)
            for j in range(wide)
        ]
        mlp_got = send_round(mlp_terms, 1)
        ties = tuple(mlp_terms)

    win_mixed, mixed_row, att_sums, grad_qkv, grad_proj = pl.pallas_call(
        partial(window_backward_kernel, local_len=local_len),
        grid=(steps,),
        in_specs=[
            tiled((rows, width)),
            tiled((group, SLOT, 3 * width)),
            tiled((group, quads, SLOT, GROUP * SLOT)),
            tiled((rows, width)),
            tiled((rows, width)),
            full(proj_full.shape),
        ]
        + [pl.BlockSpec(memory_space=pl.ANY)] * len(ties),
        out_specs=[
            tiled((rows, 3 * width)),
            tiled((group, 3 * width)),
            full((8, 3 * width)),
            full((width, 3 * width)),
            full((width, width)),
        ],
        out_shape=(
            like((all_rows, 3 * width), BF16),
            like((regions, 3 * width), BF16),
            like((8, 3 * width), F32),
            like((width, 3 * width), F32),
            like((width, width), F32),
        ),
        scratch_shapes=[
            pltpu.VMEM((rows + 8, width), F32),
            pltpu.VMEM((rows, 3 * width), F32),
        ],
        compiler_params=params(),
        cost_estimate=takes(35),
        name="window_backward",
    )(win_e, win_qkv, win_p, win_hat, win_o, proj_full, *ties)
    if in_blocks:
        (*mlp_got, mixed_row) = lax.optimization_barrier((*mlp_got, mixed_row))
        tail_tie = reduce_round(mlp_terms, mlp_got)
        mlp_terms = [tail_tie[j] for j in range(fsdp // wide)]
        mlp_terms = mlp_terms[:1] + send_round(mlp_terms, wide)

    if in_blocks:
        tall = att_rows + regions * quads
        grad_shapes = [like((wide, fsdp // wide, tall, LANES), BF16)] * dp
    else:
        grad_shapes = [
            like((width, 3 * width), BF16),
            like((width, width), BF16),
            like((width, LANES), F32),
            like((near_rows, width), BF16),
        ]
    operands = (
        mixed_row,
        dz_row,
        region_mid,
        region_hat,
        region_qkv,
        region_p,
        region_o,
        qkv_full,
        proj_full,
        norms,
        grad_qkv,
        grad_proj,
        att_sums,
        mlp_sums,
        tail_tie,
    )
    dmid, *att_grads = pl.pallas_call(
        partial(region_tail_kernel, packed=dp if in_blocks else 0),
        in_specs=[smem()]
        + [vmem()] * (len(operands) - 1)
        + [pl.BlockSpec(memory_space=pl.ANY)],
        out_shape=[like((regions, width), F32)] + grad_shapes,
        scratch_shapes=[
            pltpu.VMEM((near_rows, 2 * width), BF16),
            pltpu.VMEM((near_rows, width), F32),
            pltpu.VMEM((width, 3 * width), F32),
            pltpu.VMEM((width, width), F32),
            pltpu.VMEM((LANES, width), F32),
            pltpu.VMEM((width, LANES), F32),
        ],
        compiler_params=params(),
        cost_estimate=takes(10),
        name="region_tail",
    )(place, *operands)

    def local_back(begin, count, ties, held):
        return pl.pallas_call(
            local_back_kernel,
            grid=(count,),
            in_specs=[
                tiled((group, local_len, width), begin),
                tiled((rows, width), begin),
                tiled((rows, 3 * width), begin),
                full(qkv_full.shape),
                full(norms.shape),
            ]
            + [pl.BlockSpec(memory_space=pl.ANY)] * (len(ties) + len(held)),
            out_specs=[tiled((group, local_len, width), begin), full((8, LANES))],
            out_shape=(like(x_local.shape, BF16), like((8, LANES), F32)),
            scratch_shapes=[pltpu.VMEM((rows, width), F32)],
            input_output_aliases={5: 0} if held else {},
            compiler_params=params(),
            cost_estimate=takes(3 * count),
            name="local_back",
        )(x_local, dz1, win_mixed, qkv_full, norms, *held, *ties)

    cuts = [steps * i // 3 for i in range(4)]

    def local_part(i, ties, held):
        return local_back(cuts[i], cuts[i + 1] - cuts[i], ties, held)

    if in_blocks:
        far = send_far(att_grads)
        grad_local, tick = local_part(0, (att_grads[0],), ())
        (*far, tick) = lax.optimization_barrier((*far, tick))
        terms = [
            sum([g[j].astype(F32) for g in far], att_grads[0][j].astype(F32)).astype(BF16)
            for j in range(wide)
        ]
        got = send_round(terms, 1)
        grad_local, tick = local_part(1, (tick, terms[0]), (grad_local,))
        grad_local, tick = local_part(2, (), (grad_local,))
        (*got, tick) = lax.optimization_barrier((*got, tick))
        terms = reduce_round(terms, got)
        terms = [terms[j] for j in range(fsdp // wide)]
        terms = terms[:1] + send_round(terms, wide)
        operands = (x_regional, dmid, norms, *mlp_terms, *terms, tick)
        out_specs = (
            like(x_regional.shape, BF16),
            like(w_qkv.shape, F32),
            like(w_proj.shape, F32),
            like(w_fc1.shape, F32),
            like(w_fc2.shape, F32),
            like(gains.shape, F32),
            like(biases.shape, F32),
        )
        grad_regional, grad_qkv, grad_proj, grad_up, grad_down, grad_gains, grad_biases = (
            pl.pallas_call(
                partial(finish_kernel, terms=len(terms)),
                in_specs=[vmem()] * (len(operands) - 1) + [pl.BlockSpec(memory_space=pl.ANY)],
                out_shape=out_specs,
                scratch_shapes=[pltpu.VMEM((LANES, LANES), F32)],
                compiler_params=params(),
                cost_estimate=takes(2),
                name="finish",
            )(*operands)
        )
    else:
        up_rows = w_fc1.shape[0]
        up_blocks = cut(mlp_grads[0], dp, fsdp).reshape(dp, fsdp, up_rows, -1, mlp_cols)
        up_blocks = up_blocks.transpose(0, 1, 3, 2, 4).reshape(dp, fsdp, -1, mlp_cols)
        down_blocks = cut(mlp_grads[1].T, dp, fsdp)
        mlp_sum = scatter_all(jnp.concatenate([up_blocks, down_blocks], axis=2))
        grad_up = mlp_sum[: up_blocks.shape[2]].reshape(-1, up_rows, mlp_cols)
        grad_up = grad_up.transpose(1, 0, 2).reshape(w_fc1.shape)
        grad_down = mlp_sum[up_blocks.shape[2] :]
        grad_qkv, grad_proj, small, du_near = att_grads
        small = small.astype(BF16).reshape(1, fsdp, -1, LANES)
        small = jnp.broadcast_to(small, (dp,) + small.shape[1:])
        blocks = [cut(grad_qkv, dp, fsdp), cut(grad_proj, dp, fsdp), small]
        att = scatter_all(jnp.concatenate(blocks, axis=3))
        grad_qkv = att[:, :qkv_cols]
        grad_proj = att[:, qkv_cols : qkv_cols + proj_cols]
        small = att[:, qkv_cols + proj_cols :].T[:small_rows]
        grad_gains, grad_biases = small[: gains.shape[0]], small[gains.shape[0] :]
        held = ()
        for i in range(3):
            grad_local, tick = local_part(i, (), held)
            held = (grad_local,)
        returned = []
        for offset in range(-span, span + 1):
            part = du_near[(offset + span) * regions : (offset + span + 1) * regions]
            returned.append(part if offset == 0 else shifted(part, offset))
        grad_regional = pl.pallas_call(
            region_end_kernel,
            out_shape=like(x_regional.shape, BF16),
            compiler_params=params(),
            name="region_end",
        )(x_regional, dmid, norms, *returned)
    return (
        out_regional,
        out_local,
        grad_regional,
        grad_local,
        grad_qkv,
        grad_proj,
        grad_up,
        grad_down,
        grad_gains,
        grad_biases,
    )


def solution(mesh):
    in_specs = (
        P(("dp", "fsdp"), None),
        P(("dp", "fsdp"), None, None),
        P("fsdp", "dp"),
        P("fsdp", "dp"),
        P("fsdp", "dp"),
        P("fsdp", "dp"),
        P(None, "fsdp"),
        P(None, "fsdp"),
        P(),
        P(("dp", "fsdp"), None),
        P(("dp", "fsdp"), None, None),
    )
    out_specs = (
        P(("dp", "fsdp"), None),
        P(("dp", "fsdp"), None, None),
        P(("dp", "fsdp"), None),
        P(("dp", "fsdp"), None, None),
        P("fsdp", "dp"),
        P("fsdp", "dp"),
        P("fsdp", "dp"),
        P("fsdp", "dp"),
        P(None, "fsdp"),
        P(None, "fsdp"),
    )
    return jax.shard_map(
        on_device, mesh=mesh, in_specs=in_specs, out_specs=out_specs, check_vma=False
    )
```

```python
import math
from functools import partial

import jax
import jax.numpy as jnp
from jax import lax
from jax.experimental import pallas as pl
from jax.experimental.pallas import tpu as pltpu
from jax.sharding import PartitionSpec as P

HEAD_DIM = 32
MAX_REGIONS = 144
EPSILON = 1e-05
NEGATIVE = -1e30
PITCH = 56
SLOT = 64
LANES = 128
GROUP = LANES // HEAD_DIM
EXP_SCALE = HEAD_DIM ** (-0.5) * math.log2(math.e)
FACTOR = HEAD_DIM ** (-0.5)
VMEM_BYTES = 60 * 1024 * 1024

ERFC_P = 0.42
ERFC = (
    0.23681994,
    0.23965002,
    0.19433459,
    0.27000812,
    -0.13287422,
    0.44318139,
    -0.32169076,
    0.07057076,
)

BF16 = jnp.bfloat16
F32 = jnp.float32


def dot_nn(a, b):
    return lax.dot_general(a, b, (((1,), (0,)), ((), ())), preferred_element_type=F32)


def dot_nt(a, b):
    return lax.dot_general(a, b, (((1,), (1,)), ((), ())), preferred_element_type=F32)


def dot_tn(a, b):
    return lax.dot_general(a, b, (((0,), (0,)), ((), ())), preferred_element_type=F32)


def normalise(x):
    centred = x - jnp.mean(x, axis=-1, keepdims=True)
    inv_std = lax.rsqrt(jnp.mean(centred * centred, axis=-1, keepdims=True) + EPSILON)
    return centred * inv_std, inv_std


def norm_back(dy, hat, inv_std, gain):
    scaled = dy * gain
    mean_s = jnp.mean(scaled, axis=-1, keepdims=True)
    mean_h = jnp.mean(scaled * hat, axis=-1, keepdims=True)
    return inv_std * (scaled - mean_s - hat * mean_h)


def head_masks(rows):
    lane = lax.broadcasted_iota(jnp.int32, (rows, LANES), 1) // HEAD_DIM
    return [jnp.where(lane == h, 1.0, 0.0).astype(BF16) for h in range(GROUP)]


def spread(x, masks, order=(0, 1, 2, 3)):
    return jnp.concatenate([x * masks[h] for h in order], axis=0)


def turn(p):
    both = jnp.concatenate([p[:, :LANES], p[:, LANES:]], axis=0).T
    return jnp.concatenate([both[:SLOT], both[SLOT:]], axis=1)


TURNED = (0, 2, 1, 3)


def gelu_pair(h):
    z = jnp.abs(h) * jnp.asarray(ERFC_P * math.sqrt(0.5), BF16) + jnp.asarray(1.0, BF16)
    t = pl.reciprocal(z, approx=True)
    bell = jnp.exp2(h * h * jnp.asarray(-0.5 * math.log2(math.e), BF16))
    poly = jnp.full_like(t, 0.5 * ERFC[-1])
    for c in ERFC[-2::-1]:
        poly = poly * t + jnp.asarray(0.5 * c, BF16)
    tail = (poly * t) * bell
    cdf = jnp.where(h < 0, tail, 1 - tail)
    return h * cdf, cdf + (h * jnp.asarray(1.0 / math.sqrt(2.0 * math.pi), BF16)) * bell


def build_windows(z_ref, local_ref, row_ref):
    count, local_len, _ = local_ref.shape
    for w in range(count):
        z_ref[w * PITCH : w * PITCH + local_len] = local_ref[w].astype(F32)
        z_ref[w * PITCH + local_len : w * PITCH + local_len + 1] = row_ref[w : w + 1].astype(F32)


def split_windows(z, local_ref, row_ref):
    count, local_len, _ = local_ref.shape
    for w in range(count):
        local_ref[w] = z[w * PITCH : w * PITCH + local_len].astype(local_ref.dtype)
        row_ref[w : w + 1] = z[w * PITCH + local_len : w * PITCH + local_len + 1].astype(row_ref.dtype)


def pack_weights_kernel(
    wqkv_ref, wproj_ref, gains_ref, biases_ref, up_ref, down_ref, att_ref, mlp_ref, small_s
):
    row = 0
    small_s[...] = jnp.zeros_like(small_s)
    count, lanes = gains_ref.shape
    small_s[:count, :lanes] = gains_ref[...].astype(F32)
    small_s[count : count + biases_ref.shape[0], :lanes] = biases_ref[...].astype(F32)
    for ref in (wqkv_ref, wproj_ref, None):
        if ref is None:
            att_ref[row : row + lanes] = small_s[...].T[:lanes].astype(BF16)
            row += lanes
            continue
        for c in range(0, ref.shape[1], LANES):
            att_ref[row : row + ref.shape[0]] = ref[:, c : c + LANES]
            row += ref.shape[0]
    row = 0
    cols = down_ref.shape[1]
    for c in range(0, up_ref.shape[1], cols):
        mlp_ref[row : row + up_ref.shape[0]] = up_ref[:, c : c + cols]
        row += up_ref.shape[0]
    mlp_ref[row:] = down_ref[...]


def block_places(place_ref, stacks, codes):
    order, far_peers = codes
    per = len(stacks) // far_peers
    for i, stack in enumerate(stacks):
        deep = stack.shape[0]
        for k in range(deep):
            yield stack, k, place_ref[0] ^ (i // per), place_ref[1] ^ order[i % per * deep + k]


def assemble_attention(place_ref, stacks, codes, wqkv_ref, wproj_ref, norms_ref, small_s):
    peers, far_peers = len(codes[0]), codes[1]
    rows = wproj_ref.shape[0] // peers
    parts = [wqkv_ref.shape[1] // far_peers // LANES, wproj_ref.shape[1] // far_peers // LANES]
    for stack, k, d, f in block_places(place_ref, stacks, codes):
        here = pl.ds(pl.multiple_of(f * rows, rows), rows)
        row = 0
        for count, ref in zip(parts, (wqkv_ref, wproj_ref)):
            for j in range(count):
                to = pl.multiple_of((d * count + j) * LANES, LANES)
                ref[here, pl.ds(to, LANES)] = stack[k, row : row + rows]
                row += rows
        small_s[here] = stack[k, row : row + rows].astype(F32)
    norms_ref[...] = small_s[...].T[: norms_ref.shape[0]]


def pair_offsets(place_ref, peers, span):
    linear = place_ref[0] * peers + place_ref[1]
    for d in range(1, span + 1):
        low = lax.rem(linear, 2 * d) < d
        yield jnp.where(low, d, -d)
        yield jnp.where(low, -d, d)


def region_forward_kernel(place_ref, kid_ref, qid_ref, *refs, near, stacks, codes):
    x_refs, refs = refs[:near], refs[near:]
    if stacks:
        stack_refs, refs = refs[:stacks], refs[stacks + 1 :]
        mid_ref, hat_ref, qkv_ref, p_ref, o_ref, wqkv_ref, wproj_ref, norms_ref, small_s, x_s = refs
        assemble_attention(place_ref, stack_refs, codes, wqkv_ref, wproj_ref, norms_ref, small_s)
        own = mid_ref.shape[0]
        span = near // 2
        x_s[span * own : (span + 1) * own] = x_refs[0][...].astype(F32)
        for ref, by in zip(x_refs[1:], pair_offsets(place_ref, len(codes[0]), span)):
            x_s[pl.ds(pl.multiple_of((span + by) * own, 8), own)] = ref[...].astype(F32)
        x = x_s[...]
    else:
        wqkv_ref, wproj_ref, norms_ref, mid_ref, hat_ref, qkv_ref, p_ref, o_ref = refs
        x = jnp.concatenate([r[...].astype(F32) for r in x_refs], axis=0)
    own, width = mid_ref.shape
    rows = x.shape[0]
    first = (rows - own) // 2
    hat, _ = normalise(x)
    u = (hat * norms_ref[0:1] + norms_ref[3:4]).astype(BF16)
    hat_ref[...] = hat.astype(BF16)
    qkv = dot_nn(u, wqkv_ref[...])
    q = (qkv[:, :width] + norms_ref[6:7]).astype(BF16)
    k = qkv[:, width : 2 * width].astype(BF16)
    v = (qkv[:, 2 * width :] + norms_ref[7:8]).astype(BF16)
    qkv_ref[:, :width] = q
    qkv_ref[:, width : 2 * width] = k
    qkv_ref[:, 2 * width :] = v
    masks = head_masks(SLOT)
    same = kid_ref[...] == qid_ref[...]
    lane = lax.broadcasted_iota(jnp.int32, (1, GROUP * SLOT), 1)
    asked = (lane % SLOT) < own
    out_masks = [m.astype(F32) for m in masks]
    for c in range(width // LANES):
        cols = slice(c * LANES, (c + 1) * LANES)
        qx = spread(q[first : first + SLOT, cols], masks)
        s = jnp.where(same, dot_nt(k[:, cols], qx), NEGATIVE)
        e = jnp.exp2((s - jnp.max(s, axis=0, keepdims=True)) * EXP_SCALE)
        total = jnp.sum(e, axis=0, keepdims=True)
        p = (e * jnp.where(asked, 1.0 / total, 0.0)).astype(BF16)
        p_ref[c] = p
        mixed = dot_tn(p, v[:, cols])
        o = sum(mixed[h * SLOT : (h + 1) * SLOT] * out_masks[h] for h in range(GROUP))
        o_ref[:, cols] = o[:own].astype(BF16)
    mid_ref[...] = x[first : first + own] + dot_nn(o_ref[...], wproj_ref[...]) + norms_ref[8:9]


def window_forward_kernel(
    local_ref,
    row_ref,
    wqkv_ref,
    wproj_ref,
    norms_ref,
    *refs,
):
    z1_ref, hat_ref, qkv_ref, p_ref, o_ref, tick_ref, z_s, qkv_s, o_s = refs[-9:]
    tick_ref[...] = jnp.zeros_like(tick_ref)
    rows, width = z_s.shape
    count, local_len, _ = local_ref.shape

    @pl.when(pl.program_id(0) == 0)
    def _():
        z_s[...] = jnp.zeros_like(z_s)
        qkv_s[rows:, :] = jnp.zeros((qkv_s.shape[0] - rows, qkv_s.shape[1]), F32)

    build_windows(z_s, local_ref, row_ref)
    hat, _ = normalise(z_s[...])
    u = (hat * norms_ref[1:2] + norms_ref[4:5]).astype(BF16)
    hat_ref[...] = hat.astype(BF16)
    qkv_s[:rows, :width] = dot_nn(u, wqkv_ref[:, :width]) + norms_ref[6:7]
    qkv_s[:rows, width : 2 * width] = dot_nn(u, wqkv_ref[:, width : 2 * width])
    qkv_s[:rows, 2 * width :] = dot_nn(u, wqkv_ref[:, 2 * width :]) + norms_ref[7:8]
    masks = head_masks(SLOT)
    is_key = lax.broadcasted_iota(jnp.int32, (SLOT, GROUP * SLOT), 0) <= local_len
    lane = lax.broadcasted_iota(jnp.int32, (1, GROUP * SLOT), 1)
    asked = (lane % SLOT) <= local_len

    def window(w):
        base = pl.multiple_of(w * PITCH, 8)
        spots = [c * LANES for c in range(width // LANES)]
        scores, values = [], []
        for at in spots:
            q = qkv_s[pl.ds(base, SLOT), at : at + LANES].astype(BF16)
            k = qkv_s[pl.ds(base, SLOT), width + at : width + at + LANES].astype(BF16)
            v = qkv_s[pl.ds(base, SLOT), 2 * width + at : 2 * width + at + LANES].astype(BF16)
            qkv_ref[w, :, at : at + LANES] = q
            qkv_ref[w, :, width + at : width + at + LANES] = k
            qkv_ref[w, :, 2 * width + at : 2 * width + at + LANES] = v
            scores.append(dot_nt(k, spread(q, masks)))
            values.append(v)
        probs = []
        for c, s in enumerate(scores):
            s = jnp.where(is_key, s, NEGATIVE)
            e = jnp.exp2((s - jnp.max(s, axis=0, keepdims=True)) * EXP_SCALE)
            total = jnp.sum(e, axis=0, keepdims=True)
            p = (e * jnp.where(asked, 1.0 / total, 0.0)).astype(BF16)
            p_ref[w, c] = p
            probs.append(turn(p))
        for at, p, v in zip(spots, probs, values):
            o = dot_nn(p, spread(v, masks, TURNED))
            o_s[pl.ds(base, PITCH), at : at + LANES] = o[:PITCH]

    def windows(i, carry):
        for j in range(8):
            window(8 * i + j)
        return carry

    lax.fori_loop(0, count // 8, windows, 0)
    o = o_s[...].astype(BF16)
    o_ref[...] = o
    z1_ref[...] = z_s[...] + dot_nn(o, wproj_ref[...]) + norms_ref[8:9]


def assemble_mlp(place_ref, block_refs, up_ref, down_ref):
    fsdp, tall, cols = block_refs[0].shape
    far = place_ref[0]
    up_rows = up_ref.shape[0] // fsdp
    down_rows = down_ref.shape[0] // fsdp
    parts = (tall - down_rows) // up_rows
    for f in range(fsdp):
        for d, blocks_ref in enumerate(block_refs):
            col = d ^ far
            for j in range(parts):
                at = pl.multiple_of((col * parts + j) * cols, LANES)
                up_ref[f * up_rows : (f + 1) * up_rows, pl.ds(at, cols)] = blocks_ref[
                    f, j * up_rows : (j + 1) * up_rows
                ]
            at = pl.multiple_of(col * cols, LANES)
            down_ref[f * down_rows : (f + 1) * down_rows, pl.ds(at, cols)] = blocks_ref[
                f, parts * up_rows :
            ]


def pack_mlp(place_ref, gup_s, gdown_s, outs):
    wide, deep = outs[0].shape[:2]
    fsdp = wide * deep
    far, me = place_ref[0], place_ref[1]
    width, hidden = gdown_s.shape
    up_rows, up_cols = width // fsdp, hidden // len(outs)
    down_rows, down_cols = width // len(outs), hidden // fsdp
    parts = up_cols // LANES
    for r, out in enumerate(outs):
        d = r ^ far
        for p in range(fsdp):
            i, k = p % wide, p // wide
            f = me ^ p
            here = pl.ds(pl.multiple_of(f * up_rows, 8), up_rows)
            for j in range(parts):
                at = pl.multiple_of((d * parts + j) * LANES, LANES)
                out[i, k, j * up_rows : (j + 1) * up_rows] = gup_s[here, pl.ds(at, LANES)].astype(
                    BF16
                )
            at = pl.multiple_of(d * down_rows, 8)
            cols = pl.ds(pl.multiple_of(f * down_cols, LANES), down_cols)
            out[i, k, parts * up_rows :] = gdown_s[pl.ds(at, down_rows), cols].astype(BF16)


def mlp_kernel(place_ref, z_ref, cot_ref, cot_row_ref, norms_ref, *refs, packed):
    if packed:
        block_refs, refs = refs[:packed], refs[packed:]
        out_ref, out_row_ref, dz_ref, dz_row_ref, e_ref, sums_ref = refs[:6]
        grad_refs, refs = refs[6 : 6 + packed], refs[6 + packed :]
        dz_s, gup_s, gdown_s, acc_s, h_s, dg_s, g_s, eh_s, up_ref, down_ref = refs
    else:
        up_ref, down_ref, out_ref, out_row_ref, dz_ref, dz_row_ref, e_ref, sums_ref = refs[:8]
        grad_refs, refs = refs[8:10], refs[10:]
        dz_s, gup_s, gdown_s, acc_s, h_s, dg_s, g_s, eh_s = refs
    rows, width = z_ref.shape
    hidden = up_ref.shape[1]
    step = pl.program_id(0)

    @pl.when(step == 0)
    def _():
        if packed:
            assemble_mlp(place_ref, block_refs, up_ref, down_ref)
        dz_s[...] = jnp.zeros_like(dz_s)
        gup_s[...] = jnp.zeros_like(gup_s)
        gdown_s[...] = jnp.zeros_like(gdown_s)
        sums_ref[...] = jnp.zeros_like(sums_ref)

    build_windows(dz_s, cot_ref, cot_row_ref)
    hat, inv_std = normalise(z_ref[...])
    u = (hat * norms_ref[2:3] + norms_ref[5:6]).astype(BF16)
    e2 = dz_s[...].astype(BF16)
    ones = jnp.ones((16, rows), BF16)
    ut = jnp.concatenate([u.T, ones], axis=0)
    et = e2.T
    chunks = hidden // width
    strip = 32
    half = width // 2

    def begin(c):
        def up(n):
            cols = slice(c * width + n, c * width + n + half)
            line, at = 9 + (c * width + n) // width, n
            h = dot_nn(u, up_ref[:, cols]) + norms_ref[line : line + 1, at : at + half]
            h_s[c % 2, :, n : n + half] = h.astype(BF16)

        def down(n):
            cols = slice(c * width + n, c * width + n + half)
            dg_s[c % 2, :, n : n + half] = dot_nt(e2, down_ref[cols, :]).astype(BF16)

        return [partial(f, n) for n in (0, half) for f in (up, down)]

    def middle(c):
        def part(r):
            g, slope = gelu_pair(h_s[c % 2, r : r + strip])
            g_s[c % 2, r : r + strip] = g
            eh_s[c % 2, r : r + strip] = dg_s[c % 2, r : r + strip] * slope

        return [partial(part, r) for r in range(0, rows, strip)]

    def finish(c):
        whole = slice(c * width, (c + 1) * width)

        def add(ref, i, n, x):
            if c == 0:
                ref[i, :, n : n + half] = x
            else:
                ref[i, :, n : n + half] += x

        def forward(n):
            add(acc_s, 0, n, dot_nn(g_s[c % 2], down_ref[whole, n : n + half]))

        def back(n):
            add(acc_s, 1, n, dot_nt(eh_s[c % 2], up_ref[n : n + half, whole]))

        def down(n):
            cols = slice(c * width + n, c * width + n + half)
            gdown_s[:, cols] += dot_nn(et, g_s[c % 2, :, n : n + half])

        def up(n):
            cols = slice(c * width + n, c * width + n + half)
            gup_s[:, cols] += dot_nn(ut, eh_s[c % 2, :, n : n + half])

        return [partial(f, n) for n in (0, half) for f in (forward, back, down, up)]

    for f in begin(0):
        f()
    for c in range(chunks):
        products = begin(c + 1) if c + 1 < chunks else []
        if c > 0:
            products = products + finish(c - 1)
        strips = middle(c)
        done = 0
        for i, f in enumerate(strips):
            f()
            upto = len(products) * (i + 1) // len(strips)
            for g in products[done:upto]:
                g()
            done = upto
    for f in finish(chunks - 1):
        f()
    z2 = z_ref[...] + acc_s[0] + norms_ref[13:14]
    split_windows(z2, out_ref, out_row_ref)
    du = acc_s[1]
    dz2 = dz_s[...]
    sums_ref[1:2, :width] += jnp.sum(e2.astype(F32), axis=0, keepdims=True)
    sums_ref[2:3, :width] += jnp.sum(du * hat, axis=0, keepdims=True)
    sums_ref[3:4, :width] += jnp.sum(du, axis=0, keepdims=True)
    dz1 = dz2 + norm_back(du, hat, inv_std, norms_ref[2:3])
    dz_ref[...] = dz1
    local_len = cot_ref.shape[1]
    for w in range(cot_ref.shape[0]):
        at = w * PITCH + local_len
        dz_row_ref[w : w + 1] = dz1[at : at + 1]
    e = dz1.astype(BF16)
    e_ref[...] = e
    sums_ref[4:5, :width] += jnp.sum(e.astype(F32), axis=0, keepdims=True)

    @pl.when(step == pl.num_programs(0) - 1)
    def _():
        sums_ref[0:1, :] = gup_s[width : width + 1, :]
        if packed:
            pack_mlp(place_ref, gup_s, gdown_s, grad_refs)
        else:
            grad_refs[0][...] = gup_s[:width].astype(BF16)
            grad_refs[1][...] = gdown_s[...].astype(BF16)


def projection_back_kernel(e_ref, o_ref, wproj_ref, do_ref, gproj_ref):
    @pl.when(pl.program_id(0) == 0)
    def _():
        gproj_ref[...] = jnp.zeros_like(gproj_ref)

    do_ref[...] = dot_nt(e_ref[...], wproj_ref[...])
    gproj_ref[...] += dot_tn(o_ref[...], e_ref[...])


def window_backward_kernel(do_ref, qkv_ref, p_ref, hat_ref, *refs, local_len):
    mixed_ref, mixed_row_ref, sums_ref, gqkv_ref, do_s, mixed_s = refs[-6:]
    rows, width = do_ref.shape
    count = qkv_ref.shape[0]

    @pl.when(pl.program_id(0) == 0)
    def _():
        do_s[rows:, :] = jnp.zeros((do_s.shape[0] - rows, width), F32)
        for ref in (sums_ref, gqkv_ref):
            ref[...] = jnp.zeros_like(ref)

    do_s[:rows, :] = do_ref[...]
    masks = head_masks(SLOT)

    spots = [c * LANES for c in range(width // LANES)]

    def window(w):
        base = pl.multiple_of(w * PITCH, 8)
        upstream, slopes = [], []
        for at in spots:
            do = spread(do_s[pl.ds(base, SLOT), at : at + LANES].astype(BF16), masks)
            v = qkv_ref[w, :, 2 * width + at : 2 * width + at + LANES]
            slopes.append(dot_nt(v, do))
            upstream.append(do)
        for c, at in enumerate(spots):
            dv = dot_nn(p_ref[w, c], upstream[c])
            mixed_s[pl.ds(base, PITCH), 2 * width + at : 2 * width + at + LANES] = dv[:PITCH]
        scores = []
        for c, dp in enumerate(slopes):
            p = p_ref[w, c].astype(F32)
            ds = p * (dp - jnp.sum(dp * p, axis=0, keepdims=True))
            scores.append(ds.astype(BF16))
        turned = [turn(ds) for ds in scores]
        for at, ds in zip(spots, scores):
            dk = dot_nn(ds, spread(qkv_ref[w, :, at : at + LANES], masks)) * FACTOR
            mixed_s[pl.ds(base, PITCH), width + at : width + at + LANES] = dk[:PITCH]
        for at, ds in zip(spots, turned):
            k = qkv_ref[w, :, width + at : width + at + LANES]
            dq = dot_nn(ds, spread(k, masks, TURNED)) * FACTOR
            mixed_s[pl.ds(base, PITCH), at : at + LANES] = dq[:PITCH]

    def windows(i, carry):
        for j in range(8):
            window(8 * i + j)
        return carry

    lax.fori_loop(0, count // 8, windows, 0)
    mixed = mixed_s[...].astype(BF16)
    mixed_ref[...] = mixed
    for w in range(count):
        at = w * PITCH + local_len
        mixed_row_ref[w : w + 1] = mixed_s[at : at + 1].astype(BF16)
    sums_ref[0:1, :] += jnp.sum(mixed.astype(F32), axis=0, keepdims=True)
    gqkv_ref[...] += dot_tn(hat_ref[...], mixed)


def local_back_kernel(local_ref, dz_ref, mixed_ref, wqkv_ref, norms_ref, *refs):
    out_ref, tick_ref, z_s = refs[-3:]
    tick_ref[...] = jnp.zeros_like(tick_ref)
    count, local_len, _ = local_ref.shape

    @pl.when(pl.program_id(0) == 0)
    def _():
        z_s[...] = jnp.zeros_like(z_s)

    for w in range(count):
        z_s[w * PITCH : w * PITCH + local_len] = local_ref[w].astype(F32)
    du = dot_nt(mixed_ref[...], wqkv_ref[...])
    hat, inv_std = normalise(z_s[...])
    dz0 = dz_ref[...] + norm_back(du, hat, inv_std, norms_ref[1:2])
    for w in range(count):
        out_ref[w] = dz0[w * PITCH : w * PITCH + local_len].astype(BF16)


def pack_attention(place_ref, gqkv_s, gproj_s, small_s, du_s, own, outs):
    wide, deep = outs[0].shape[:2]
    peers = wide * deep
    width = gproj_s.shape[0]
    rows = width // peers
    quads = width // LANES
    counts = [gqkv_s.shape[1] // len(outs) // LANES, gproj_s.shape[1] // len(outs) // LANES]
    far, me = place_ref[0], place_ref[1]
    linear = far * peers + me
    near = du_s.shape[0] // own
    for r, out in enumerate(outs):
        d = r ^ far
        for p in range(peers):
            j, i = p % wide, p // wide
            f = me ^ p
            here = pl.ds(pl.multiple_of(f * rows, 8), rows)
            row = 0
            for count, grad in zip(counts, (gqkv_s, gproj_s)):
                for c in range(count):
                    at = pl.ds(pl.multiple_of((d * count + c) * LANES, LANES), LANES)
                    out[j, i, row : row + rows] = grad[here, at].astype(BF16)
                    row += rows
            out[j, i, row : row + rows] = small_s[here].astype(BF16)
            row += rows
            away = d * peers + f - linear + near // 2
            inside = (away >= 0) & (away < near)
            at = pl.ds(pl.multiple_of(jnp.where(inside, away, 0) * own, 8), own)
            share = jnp.where(inside, 1.0, 0.0)
            for c in range(quads):
                term = du_s[at, c * LANES : (c + 1) * LANES] * share
                out[j, i, row : row + own] = term.astype(BF16)
                row += own


def region_tail_kernel(
    place_ref,
    mixed_row_ref,
    dz_row_ref,
    mid_ref,
    hat_ref,
    qkv_ref,
    p_ref,
    o_ref,
    wqkv_ref,
    wproj_ref,
    norms_ref,
    gqkv_in_ref,
    gproj_in_ref,
    att_sums_ref,
    mlp_sums_ref,
    tie_ref,
    dmid_ref,
    *refs,
    packed,
):
    outs, refs = (refs[:packed], refs[packed:]) if packed else (refs[:4], refs[4:])
    near_s, du_s, gqkv_s, gproj_s, lines_s, small_s = refs
    own, width = mid_ref.shape
    rows = qkv_ref.shape[0]
    first = (rows - own) // 2
    mine = slice(first, first + own)

    mid_hat, mid_std = normalise(mid_ref[...])
    row_du = dot_nt(mixed_row_ref[...], wqkv_ref[...])
    dmid = dz_row_ref[...] + norm_back(row_du, mid_hat, mid_std, norms_ref[1:2])
    dmid_ref[...] = dmid
    e = dmid.astype(BF16)
    do = dot_nt(e, wproj_ref[...])
    do = jnp.concatenate([do, jnp.zeros((SLOT - own, width), F32)], axis=0).astype(BF16)
    masks = head_masks(SLOT)
    out_masks = [m.astype(F32) for m in masks]
    dqs = []
    for c in range(width // LANES):
        at = c * LANES
        q = qkv_ref[first : first + SLOT, at : at + LANES]
        k = qkv_ref[:, width + at : width + at + LANES]
        v = qkv_ref[:, 2 * width + at : 2 * width + at + LANES]
        dox = spread(do[:, at : at + LANES], masks)
        p = p_ref[c]
        near_s[:, width + at : width + at + LANES] = dot_nn(p, dox).astype(BF16)
        dp = dot_nt(v, dox)
        pf = p.astype(F32)
        ds = (pf * (dp - jnp.sum(dp * pf, axis=0, keepdims=True))).astype(BF16)
        near_s[:, at : at + LANES] = (dot_nn(ds, spread(q, masks)) * FACTOR).astype(BF16)
        wide = dot_tn(ds, k)
        dq = sum(wide[h * SLOT : (h + 1) * SLOT] * out_masks[h] for h in range(GROUP))
        dqs.append((dq[:own] * FACTOR).astype(BF16))
    dq = jnp.concatenate(dqs, axis=1)
    near = near_s[...]

    du_s[...] = dot_nt(near, wqkv_ref[:, width:])
    du_s[mine] += dot_nt(dq, wqkv_ref[:, :width])

    win_sum = att_sums_ref[0:1]
    near_sum = jnp.concatenate(
        [
            jnp.sum(dq.astype(F32), axis=0, keepdims=True),
            jnp.sum(near.astype(F32), axis=0, keepdims=True),
        ],
        axis=1,
    )
    sums = jnp.concatenate([near_sum, win_sum, jnp.zeros((6, 3 * width), F32)], axis=0)
    high = sums.astype(BF16)
    rest = (sums - high.astype(F32)).astype(BF16)
    both = jnp.concatenate([high, rest], axis=0)
    shifts = dot_nt(both, wqkv_ref[...])
    shifts = shifts[:8] + shifts[8:]
    lines_s[...] = jnp.zeros_like(lines_s)
    lines_s[:16] = norms_ref[...]
    columns = lines_s[...].T
    gain_0, gain_1 = columns[:, 0:1], columns[:, 1:2]
    shift_0, shift_1 = columns[:, 3:4], columns[:, 4:5]
    dgain_0 = jnp.zeros((width, 1), F32)
    dgain_1 = jnp.zeros((width, 1), F32)
    for i in range(3):
        cols = slice(i * width, (i + 1) * width)
        if i == 0:
            region = dot_tn(hat_ref[mine, :], dq)
        else:
            region = dot_tn(hat_ref[...], near[:, (i - 1) * width : i * width])
        window = gqkv_in_ref[:, cols]
        weight = wqkv_ref[:, cols].astype(F32)
        dgain_0 += jnp.sum(weight * region, axis=1, keepdims=True)
        dgain_1 += jnp.sum(weight * window, axis=1, keepdims=True)
        gqkv_s[:, cols] = (
            region * gain_0
            + window * gain_1
            + shift_0 * near_sum[:, cols]
            + shift_1 * win_sum[:, cols]
        )
    gproj_s[...] = gproj_in_ref[...] + dot_tn(o_ref[...], e)
    total = near_sum + win_sum
    hidden = mlp_sums_ref.shape[1]
    lines = [
        None,
        None,
        mlp_sums_ref[2:3, :width],
        shifts[0:1],
        shifts[1:2],
        mlp_sums_ref[3:4, :width],
        total[:, :width],
        total[:, 2 * width :],
        jnp.sum(e.astype(F32), axis=0, keepdims=True) + mlp_sums_ref[4:5, :width],
    ]
    lines += [mlp_sums_ref[0:1, c * width : (c + 1) * width] for c in range(hidden // width)]
    lines += [mlp_sums_ref[1:2, :width]]
    lines_s[...] = jnp.zeros_like(lines_s)
    for i, line in enumerate(lines):
        if line is not None:
            lines_s[i : i + 1] = line
    small_s[...] = lines_s[...].T
    small_s[:, 0:1] = dgain_0
    small_s[:, 1:2] = dgain_1
    if packed:
        pack_attention(place_ref, gqkv_s, gproj_s, small_s, du_s, own, outs)
    else:
        outs[0][...] = gqkv_s[...].astype(BF16)
        outs[1][...] = gproj_s[...].astype(BF16)
        outs[2][...] = small_s[...]
        outs[3][...] = du_s[...].astype(BF16)


def finish_kernel(
    x_ref,
    dmid_ref,
    norms_ref,
    *refs,
    terms,
):
    mlp_refs, refs = refs[:terms], refs[terms:]
    term_refs, outs = refs[:terms], refs[terms + 1 : -1]
    out_ref, gqkv_ref, gproj_ref, gup_ref, gdown_ref, ggains_ref, gbiases_ref = outs
    small_s = refs[-1]
    own, width = x_ref.shape

    def total(row, count, parts=term_refs):
        here = slice(row, row + count)
        return sum([t[here].astype(F32) for t in parts[1:]], parts[0][here].astype(F32))

    rows = gqkv_ref.shape[0]
    row = 0
    for ref in (gqkv_ref, gproj_ref):
        for c in range(0, ref.shape[1], LANES):
            ref[:, c : c + LANES] = total(row, rows)
            row += rows
    small_s[:rows] = total(row, rows)
    small = small_s[...].T
    count = ggains_ref.shape[0]
    ggains_ref[...] = small[:count, :rows]
    gbiases_ref[...] = small[count : count + gbiases_ref.shape[0], :rows]
    row += rows
    du = jnp.concatenate([total(row + c * own, own) for c in range(width // LANES)], axis=1)
    hat, inv_std = normalise(x_ref[...].astype(F32))
    out_ref[...] = (dmid_ref[...] + norm_back(du, hat, inv_std, norms_ref[0:1])).astype(BF16)
    row = 0
    for c in range(0, gup_ref.shape[1], LANES):
        gup_ref[:, c : c + LANES] = total(row, rows, mlp_refs)
        row += rows
    gdown_ref[...] = total(row, gdown_ref.shape[1], mlp_refs).T


def region_end_kernel(x_ref, dmid_ref, norms_ref, *refs):
    near_refs, out_ref = refs[:-1], refs[-1]
    du = near_refs[0][...].astype(F32)
    for ref in near_refs[1:]:
        du = du + ref[...].astype(F32)
    hat, inv_std = normalise(x_ref[...].astype(F32))
    out_ref[...] = (dmid_ref[...] + norm_back(du, hat, inv_std, norms_ref[0:1])).astype(BF16)


def axis_rounds(size):
    rounds = []
    shift = 0
    while (1 << shift) < size:
        width = min(4, size >> shift)
        rounds.append((shift, width))
        shift += width.bit_length() - 1
    return rounds


def swap_by(x, axis, code):
    pairs = [(i, i ^ code) for i in range(lax.axis_size(axis))]
    return lax.ppermute(x, axis, pairs)


def gather_axis(x, axis, stacked=True):
    size = lax.axis_size(axis)
    rounds = axis_rounds(size)
    if not stacked and len(rounds) == 1:
        return [x] + [swap_by(x, axis, j) for j in range(1, size)], list(range(size))
    stack = x[None]
    codes = [0]
    for shift, width in reversed(rounds):
        parts = [stack] + [swap_by(stack, axis, j << shift) for j in range(1, width)]
        stack = jnp.concatenate(parts, axis=0)
        codes = [c ^ (j << shift) for j in range(width) for c in codes]
    return stack, codes


def in_order(stack, codes, axis):
    place = [0] * len(codes)
    for p, c in enumerate(codes):
        place[c] = p
    wanted = jnp.arange(len(codes), dtype=jnp.int32) ^ lax.axis_index(axis)
    return jnp.take(stack, jnp.asarray(place, dtype=jnp.int32)[wanted], axis=0)


def scatter_axis(blocks, axis):
    size = lax.axis_size(axis)
    me = lax.axis_index(axis)
    rest = blocks.shape[1:]
    for shift, width in axis_rounds(size):
        left = blocks.shape[0] // width
        cut = blocks.reshape((left, width) + rest)
        mine = (me >> shift) & (width - 1)
        total = lax.dynamic_index_in_dim(cut, mine, 1, keepdims=False).astype(jnp.float32)
        for j in range(1, width):
            out = lax.dynamic_index_in_dim(cut, mine ^ j, 1, keepdims=False)
            total = total + swap_by(out, axis, j << shift).astype(jnp.float32)
        blocks = total.astype(blocks.dtype)
    return blocks[0]


def join(blocks):
    dp, fsdp, rows, cols = blocks.shape
    return blocks.transpose(1, 2, 0, 3).reshape(fsdp * rows, dp * cols)


def cut(whole, dp, fsdp):
    rows, cols = whole.shape
    return whole.reshape(fsdp, rows // fsdp, dp, cols // dp).transpose(2, 0, 1, 3)


def scatter_all(blocks):
    return scatter_axis(scatter_axis(blocks, "dp"), "fsdp").astype(jnp.float32)


def shifted(x, by):
    axes = ("dp", "fsdp")
    peers = lax.axis_size(axes)
    pairs = [(i, i + by) for i in range(peers) if 0 <= i + by < peers]
    return lax.ppermute(x, axes, pairs)


def matched(x, by, second):
    axes = ("dp", "fsdp")
    peers = lax.axis_size(axes)
    pairs = []
    for i in range(peers):
        low = i % (2 * by) < by
        to = i + by if low != bool(second) else i - by
        if 0 <= to < peers:
            pairs.append((i, to))
    return lax.ppermute(x, axes, pairs)


def full(shape):
    return pl.BlockSpec(shape, lambda *_: (0,) * len(shape))


def once(shape):
    return pl.BlockSpec(shape, lambda *_: (0,) * len(shape), pipeline_mode=pl.Buffered(1))


def tiled(shape, begin=0):
    return pl.BlockSpec(shape, lambda i: (i + begin,) + (0,) * (len(shape) - 1))


def like(shape, dtype):
    return jax.ShapeDtypeStruct(shape, dtype)


def smem():
    return pl.BlockSpec(memory_space=pltpu.SMEM)


def vmem():
    return pl.BlockSpec(memory_space=pltpu.VMEM)


def gather_round(stack, axis, which):
    shift, width = axis_rounds(lax.axis_size(axis))[::-1][which]
    return [stack] + [swap_by(stack, axis, j << shift) for j in range(1, width)]


def gather_parts(block, axis):
    rounds = axis_rounds(lax.axis_size(axis))[::-1]
    parts = [block[None]]
    codes = [0]
    for which, (shift, width) in enumerate(rounds):
        parts = gather_round(jnp.concatenate(parts, axis=0), axis, which)
        codes = [c ^ (j << shift) for j in range(width) for c in codes]
    return parts, codes


def far_parts(parts):
    return parts + [
        swap_by(x, "dp", r) for r in range(1, lax.axis_size("dp")) for x in parts
    ]


def send_far(grads):
    return [swap_by(g, "dp", r) for r, g in enumerate(grads) if r > 0]


def send_round(terms, step):
    return [swap_by(x, "fsdp", j * step) for j, x in enumerate(terms) if j > 0]


def reduce_round(terms, got):
    total = terms[0].astype(F32)
    for x in got:
        total = total + x.astype(F32)
    return total.astype(BF16)


def takes(us):
    return pl.CostEstimate(flops=int(us * 1.1e9), bytes_accessed=int(us * 1e6), transcendentals=0)


def params():
    return pltpu.CompilerParams(vmem_limit_bytes=VMEM_BYTES)


def on_device(
    x_regional,
    x_local,
    w_qkv,
    w_proj,
    w_fc1,
    w_fc2,
    gains,
    biases,
    region_counts,
    cot_regional,
    cot_local,
):
    regions, local_len, width = x_local.shape
    group = 8
    steps = regions // group
    rows = group * PITCH
    all_rows = regions * PITCH
    quads = width // LANES
    span = (regions + MAX_REGIONS - 2) // regions
    all_regions = regions * lax.axis_size(("dp", "fsdp"))
    linear = lax.axis_index(("dp", "fsdp"))
    first_row = linear * regions
    dp, fsdp = lax.axis_size("dp"), lax.axis_size("fsdp")
    qkv_cols, proj_cols = w_qkv.shape[1], w_proj.shape[1]
    in_blocks = qkv_cols % LANES == 0 and proj_cols % LANES == 0 and w_fc2.shape[0] == LANES
    small_rows = gains.shape[0] + biases.shape[0]

    mlp_cols = w_fc2.shape[1]
    if in_blocks:
        att_rows = (qkv_cols + proj_cols + LANES) // LANES * w_qkv.shape[0]
        mlp_rows = w_fc1.shape[0] * w_fc1.shape[1] // mlp_cols + w_fc2.shape[0]
        att_block, mlp_block = pl.pallas_call(
            pack_weights_kernel,
            out_shape=(like((att_rows, LANES), BF16), like((mlp_rows, mlp_cols), BF16)),
            scratch_shapes=[pltpu.VMEM((LANES, LANES), F32)],
            compiler_params=params(),
            cost_estimate=takes(2),
            name="pack_weights",
        )(w_qkv, w_proj, gains, biases, w_fc1, w_fc2)
    else:
        small = jnp.concatenate([gains, biases], axis=0).T
        small = jnp.pad(small, ((0, 0), (0, LANES - small_rows)))
        att_block = jnp.concatenate([w_qkv, w_proj, small], axis=1)
        up_parts = [w_fc1[:, i : i + mlp_cols] for i in range(0, w_fc1.shape[1], mlp_cols)]
        mlp_block = jnp.concatenate(up_parts + [w_fc2], axis=0)
    hidden = w_fc1.shape[1] * dp

    place = jnp.stack([lax.axis_index("dp"), lax.axis_index("fsdp")]).astype(jnp.int32)
    near_rows = (2 * span + 1) * regions
    wide = axis_rounds(fsdp)[0][1]
    if in_blocks:
        att_parts, order = gather_parts(att_block, "fsdp")
        codes = (order, dp)
        near = [matched(x_regional, d, s) for d in range(1, span + 1) for s in range(2)]
        (*att_parts, x_own), near = lax.optimization_barrier(((*att_parts, x_regional), near))
        near = [x_own] + near
        att_stacks = far_parts(att_parts)
        mlp_half = lax.all_gather(mlp_block, "fsdp", axis=0, tiled=False)
    else:
        att_stack, order = gather_axis(att_block, "fsdp")
        codes = (order, dp)
        att_stacks, far_codes = gather_axis(att_stack, "dp")
        mlp_stack, _ = gather_axis(mlp_block, "fsdp")
        mlp_stack = in_order(mlp_stack, order, "fsdp")
        mlp_stack, _ = gather_axis(mlp_stack, "dp")
        mlp_stack = in_order(mlp_stack, far_codes, "dp")

    image_ends = jnp.minimum(jnp.cumsum(region_counts), all_regions)
    key_rows = first_row - span * regions + jnp.arange(near_rows, dtype=jnp.int32)
    key_image = jnp.sum((image_ends[None, :] <= key_rows[:, None]).astype(jnp.int32), axis=1)
    inside = (key_rows >= 0) & (key_rows < all_regions)
    key_image = jnp.where(inside, key_image, -1)
    query_image = jnp.pad(
        key_image[span * regions : (span + 1) * regions],
        (0, SLOT - regions),
        constant_values=-2,
    )
    query_image = jnp.tile(query_image, GROUP)[None]

    region_outs = (
        like((regions, width), F32),
        like((near_rows, width), BF16),
        like((near_rows, 3 * width), BF16),
        like((quads, near_rows, GROUP * SLOT), BF16),
        like((regions, width), BF16),
    )
    if in_blocks:
        whole = (
            like((width, 3 * width), BF16),
            like((width, width), BF16),
            like((16, width), F32),
        )
        region_mid, region_hat, region_qkv, region_p, region_o, qkv_full, proj_full, norms = (
            pl.pallas_call(
                partial(
                    region_forward_kernel, near=len(near), stacks=len(att_stacks), codes=codes
                ),
                in_specs=[smem()]
                + [vmem()] * (2 + len(near) + len(att_stacks))
                + [pl.BlockSpec(memory_space=pl.ANY)],
                out_shape=region_outs + whole,
                scratch_shapes=[
                    pltpu.VMEM((width, LANES), F32),
                    pltpu.VMEM((near_rows, width), F32),
                ],
                compiler_params=params(),
                cost_estimate=takes(6),
                name="region_forward",
            )(place, key_image[:, None], query_image, *near, *att_stacks, cot_local)
        )
    else:
        near = [
            x_regional if offset == 0 else shifted(x_regional, -offset)
            for offset in range(-span, span + 1)
        ]
        blocks = in_order(jnp.stack([in_order(s, order, "fsdp") for s in att_stacks]), far_codes, "dp")
        qkv_full = join(blocks[..., :qkv_cols])
        proj_full = join(blocks[..., qkv_cols : qkv_cols + proj_cols])
        small = blocks[0, :, :, qkv_cols + proj_cols :].reshape(width, LANES)
        norms = small.astype(F32).T[:16]
        region_mid, region_hat, region_qkv, region_p, region_o = pl.pallas_call(
            partial(region_forward_kernel, near=len(near), stacks=0, codes=codes),
            in_specs=[smem()] + [vmem()] * (5 + len(near)),
            out_shape=region_outs,
            compiler_params=params(),
            cost_estimate=takes(6),
            name="region_forward",
        )(place, key_image[:, None], query_image, *near, qkv_full, proj_full, norms)

    first_half = steps // 2
    forward_outs = (
        like((all_rows, width), F32),
        like((all_rows, width), BF16),
        like((regions, SLOT, 3 * width), BF16),
        like((regions, quads, SLOT, GROUP * SLOT), BF16),
        like((all_rows, width), BF16),
        like((8, LANES), F32),
    )

    def window_forward(begin, count, held, ties):
        operands = (x_local, region_mid, qkv_full, proj_full, norms)
        return pl.pallas_call(
            window_forward_kernel,
            grid=(count,),
            in_specs=[
                tiled((group, local_len, width), begin),
                tiled((group, width), begin),
                full(qkv_full.shape),
                full(proj_full.shape),
                full(norms.shape),
            ]
            + [pl.BlockSpec(memory_space=pl.ANY)] * (len(held) + len(ties)),
            out_specs=[
                tiled((rows, width), begin),
                tiled((rows, width), begin),
                tiled((group, SLOT, 3 * width), begin),
                tiled((group, quads, SLOT, GROUP * SLOT), begin),
                tiled((rows, width), begin),
                full((8, LANES)),
            ],
            out_shape=forward_outs,
            scratch_shapes=[
                pltpu.VMEM((rows, width), F32),
                pltpu.VMEM((rows + 8, 3 * width), F32),
                pltpu.VMEM((rows, width), F32),
            ],
            input_output_aliases={len(operands) + i: i for i in range(len(held))},
            compiler_params=params(),
            cost_estimate=takes(6 * count),
            name="window_forward",
        )(*operands, *held, *ties)

    *held, tick = window_forward(0, first_half, (), ())
    if in_blocks:
        mlp_half, tick = lax.optimization_barrier((mlp_half, tick))
        mlp_stacks = far_parts([mlp_half])
    z1, win_hat, win_qkv, win_p, win_o, _ = window_forward(
        first_half, steps - first_half, held, (tick,)
    )

    mlp_group = group
    mlp_steps = regions // mlp_group
    mlp_rows_in = mlp_group * PITCH
    mlp_outs = [
        like(x_local.shape, BF16),
        like(x_regional.shape, BF16),
        like((all_rows, width), F32),
        like(x_regional.shape, F32),
        like((all_rows, width), BF16),
        like((8, hidden), F32),
    ]
    mlp_specs = [
        tiled((mlp_group, local_len, width)),
        tiled((mlp_group, width)),
        tiled((mlp_rows_in, width)),
        tiled((mlp_group, width)),
        tiled((mlp_rows_in, width)),
        full((8, hidden)),
    ]
    mlp_scratch = [
        pltpu.VMEM((mlp_rows_in, width), F32),
        pltpu.VMEM((width + 16, hidden), F32),
        pltpu.VMEM((width, hidden), F32),
        pltpu.VMEM((2, mlp_rows_in, width), F32),
        pltpu.VMEM((2, mlp_rows_in, width), BF16),
        pltpu.VMEM((2, mlp_rows_in, width), BF16),
        pltpu.VMEM((2, mlp_rows_in, width), BF16),
        pltpu.VMEM((2, mlp_rows_in, width), BF16),
    ]
    if in_blocks:
        weights = tuple(mlp_stacks)
        tall = mlp_block.shape[0] * mlp_cols // LANES
        grad_shapes = [(wide, fsdp // wide, tall, LANES)] * dp
        mlp_scratch += [pltpu.VMEM((width, hidden), BF16), pltpu.VMEM((hidden, width), BF16)]
    else:
        blocks = mlp_stack.transpose(1, 0, 2, 3)
        up_full = blocks[:, :, : mlp_block.shape[0] - w_fc2.shape[0]]
        up_full = up_full.reshape(fsdp, dp, -1, w_fc1.shape[0], mlp_cols)
        up_full = up_full.transpose(0, 3, 1, 2, 4).reshape(width, hidden)
        down_full = blocks[:, :, mlp_block.shape[0] - w_fc2.shape[0] :]
        down_full = down_full.transpose(0, 2, 1, 3).reshape(hidden, width)
        weights = (up_full, down_full)
        grad_shapes = [(width, hidden)] * 2
    out_local, out_regional, dz1, dz_row, win_e, mlp_sums, *mlp_grads = pl.pallas_call(
        partial(mlp_kernel, packed=dp if in_blocks else 0),
        grid=(mlp_steps,),
        in_specs=[
            smem(),
            tiled((mlp_rows_in, width)),
            tiled((mlp_group, local_len, width)),
            tiled((mlp_group, width)),
            full(norms.shape),
        ]
        + [once(w.shape) for w in weights],
        out_specs=mlp_specs + [once(g) for g in grad_shapes],
        out_shape=mlp_outs + [like(g, BF16) for g in grad_shapes],
        scratch_shapes=mlp_scratch,
        compiler_params=params(),
        cost_estimate=takes(50),
        name="mlp",
    )(place, z1, cot_local, cot_regional, norms, *weights)

    win_do, grad_proj = pl.pallas_call(
        projection_back_kernel,
        grid=(steps,),
        in_specs=[tiled((rows, width)), tiled((rows, width)), full(proj_full.shape)],
        out_specs=[tiled((rows, width)), full((width, width))],
        out_shape=(like((all_rows, width), F32), like((width, width), F32)),
        compiler_params=params(),
        cost_estimate=takes(6),
        name="projection_back",
    )(win_e, win_o, proj_full)
    ties, tail_tie = (), norms
    if in_blocks:
        far = send_far(mlp_grads)
        (*far, grad_proj) = lax.optimization_barrier((*far, grad_proj))
        mlp_terms = [
            sum([g[j].astype(F32) for g in far], mlp_grads[0][j].astype(F32)).astype(BF16)
            for j in range(wide)
        ]
        mlp_got = send_round(mlp_terms, 1)
        ties = tuple(mlp_terms)

    win_mixed, mixed_row, att_sums, grad_qkv = pl.pallas_call(
        partial(window_backward_kernel, local_len=local_len),
        grid=(steps,),
        in_specs=[
            tiled((rows, width)),
            tiled((group, SLOT, 3 * width)),
            tiled((group, quads, SLOT, GROUP * SLOT)),
            tiled((rows, width)),
        ]
        + [pl.BlockSpec(memory_space=pl.ANY)] * len(ties),
        out_specs=[
            tiled((rows, 3 * width)),
            tiled((group, 3 * width)),
            full((8, 3 * width)),
            full((width, 3 * width)),
        ],
        out_shape=(
            like((all_rows, 3 * width), BF16),
            like((regions, 3 * width), BF16),
            like((8, 3 * width), F32),
            like((width, 3 * width), F32),
        ),
        scratch_shapes=[
            pltpu.VMEM((rows + 8, width), F32),
            pltpu.VMEM((rows, 3 * width), F32),
        ],
        compiler_params=params(),
        cost_estimate=takes(35),
        name="window_backward",
    )(win_do, win_qkv, win_p, win_hat, *ties)
    if in_blocks:
        (*mlp_got, mixed_row) = lax.optimization_barrier((*mlp_got, mixed_row))
        tail_tie = reduce_round(mlp_terms, mlp_got)
        mlp_terms = [tail_tie[j] for j in range(fsdp // wide)]
        mlp_terms = mlp_terms[:1] + send_round(mlp_terms, wide)

    if in_blocks:
        tall = att_rows + regions * quads
        grad_shapes = [like((wide, fsdp // wide, tall, LANES), BF16)] * dp
    else:
        grad_shapes = [
            like((width, 3 * width), BF16),
            like((width, width), BF16),
            like((width, LANES), F32),
            like((near_rows, width), BF16),
        ]
    operands = (
        mixed_row,
        dz_row,
        region_mid,
        region_hat,
        region_qkv,
        region_p,
        region_o,
        qkv_full,
        proj_full,
        norms,
        grad_qkv,
        grad_proj,
        att_sums,
        mlp_sums,
        tail_tie,
    )
    dmid, *att_grads = pl.pallas_call(
        partial(region_tail_kernel, packed=dp if in_blocks else 0),
        in_specs=[smem()]
        + [vmem()] * (len(operands) - 1)
        + [pl.BlockSpec(memory_space=pl.ANY)],
        out_shape=[like((regions, width), F32)] + grad_shapes,
        scratch_shapes=[
            pltpu.VMEM((near_rows, 2 * width), BF16),
            pltpu.VMEM((near_rows, width), F32),
            pltpu.VMEM((width, 3 * width), F32),
            pltpu.VMEM((width, width), F32),
            pltpu.VMEM((LANES, width), F32),
            pltpu.VMEM((width, LANES), F32),
        ],
        compiler_params=params(),
        cost_estimate=takes(10),
        name="region_tail",
    )(place, *operands)

    def local_back(begin, count, ties, held):
        return pl.pallas_call(
            local_back_kernel,
            grid=(count,),
            in_specs=[
                tiled((group, local_len, width), begin),
                tiled((rows, width), begin),
                tiled((rows, 3 * width), begin),
                full(qkv_full.shape),
                full(norms.shape),
            ]
            + [pl.BlockSpec(memory_space=pl.ANY)] * (len(ties) + len(held)),
            out_specs=[tiled((group, local_len, width), begin), full((8, LANES))],
            out_shape=(like(x_local.shape, BF16), like((8, LANES), F32)),
            scratch_shapes=[pltpu.VMEM((rows, width), F32)],
            input_output_aliases={5: 0} if held else {},
            compiler_params=params(),
            cost_estimate=takes(3 * count),
            name="local_back",
        )(x_local, dz1, win_mixed, qkv_full, norms, *held, *ties)

    cuts = [steps * i // 3 for i in range(4)]

    def local_part(i, ties, held):
        return local_back(cuts[i], cuts[i + 1] - cuts[i], ties, held)

    if in_blocks:
        far = send_far(att_grads)
        grad_local, tick = local_part(0, (att_grads[0],), ())
        (*far, tick) = lax.optimization_barrier((*far, tick))
        terms = [
            sum([g[j].astype(F32) for g in far], att_grads[0][j].astype(F32)).astype(BF16)
            for j in range(wide)
        ]
        got = send_round(terms, 1)
        grad_local, tick = local_part(1, (tick, terms[0]), (grad_local,))
        grad_local, tick = local_part(2, (), (grad_local,))
        (*got, tick) = lax.optimization_barrier((*got, tick))
        terms = reduce_round(terms, got)
        terms = [terms[j] for j in range(fsdp // wide)]
        terms = terms[:1] + send_round(terms, wide)
        operands = (x_regional, dmid, norms, *mlp_terms, *terms, tick)
        out_specs = (
            like(x_regional.shape, BF16),
            like(w_qkv.shape, F32),
            like(w_proj.shape, F32),
            like(w_fc1.shape, F32),
            like(w_fc2.shape, F32),
            like(gains.shape, F32),
            like(biases.shape, F32),
        )
        grad_regional, grad_qkv, grad_proj, grad_up, grad_down, grad_gains, grad_biases = (
            pl.pallas_call(
                partial(finish_kernel, terms=len(terms)),
                in_specs=[vmem()] * (len(operands) - 1) + [pl.BlockSpec(memory_space=pl.ANY)],
                out_shape=out_specs,
                scratch_shapes=[pltpu.VMEM((LANES, LANES), F32)],
                compiler_params=params(),
                cost_estimate=takes(2),
                name="finish",
            )(*operands)
        )
    else:
        up_rows = w_fc1.shape[0]
        up_blocks = cut(mlp_grads[0], dp, fsdp).reshape(dp, fsdp, up_rows, -1, mlp_cols)
        up_blocks = up_blocks.transpose(0, 1, 3, 2, 4).reshape(dp, fsdp, -1, mlp_cols)
        down_blocks = cut(mlp_grads[1].T, dp, fsdp)
        mlp_sum = scatter_all(jnp.concatenate([up_blocks, down_blocks], axis=2))
        grad_up = mlp_sum[: up_blocks.shape[2]].reshape(-1, up_rows, mlp_cols)
        grad_up = grad_up.transpose(1, 0, 2).reshape(w_fc1.shape)
        grad_down = mlp_sum[up_blocks.shape[2] :]
        grad_qkv, grad_proj, small, du_near = att_grads
        small = small.astype(BF16).reshape(1, fsdp, -1, LANES)
        small = jnp.broadcast_to(small, (dp,) + small.shape[1:])
        blocks = [cut(grad_qkv, dp, fsdp), cut(grad_proj, dp, fsdp), small]
        att = scatter_all(jnp.concatenate(blocks, axis=3))
        grad_qkv = att[:, :qkv_cols]
        grad_proj = att[:, qkv_cols : qkv_cols + proj_cols]
        small = att[:, qkv_cols + proj_cols :].T[:small_rows]
        grad_gains, grad_biases = small[: gains.shape[0]], small[gains.shape[0] :]
        held = ()
        for i in range(3):
            grad_local, tick = local_part(i, (), held)
            held = (grad_local,)
        returned = []
        for offset in range(-span, span + 1):
            part = du_near[(offset + span) * regions : (offset + span + 1) * regions]
            returned.append(part if offset == 0 else shifted(part, offset))
        grad_regional = pl.pallas_call(
            region_end_kernel,
            out_shape=like(x_regional.shape, BF16),
            compiler_params=params(),
            name="region_end",
        )(x_regional, dmid, norms, *returned)
    return (
        out_regional,
        out_local,
        grad_regional,
        grad_local,
        grad_qkv,
        grad_proj,
        grad_up,
        grad_down,
        grad_gains,
        grad_biases,
    )


def solution(mesh):
    in_specs = (
        P(("dp", "fsdp"), None),
        P(("dp", "fsdp"), None, None),
        P("fsdp", "dp"),
        P("fsdp", "dp"),
        P("fsdp", "dp"),
        P("fsdp", "dp"),
        P(None, "fsdp"),
        P(None, "fsdp"),
        P(),
        P(("dp", "fsdp"), None),
        P(("dp", "fsdp"), None, None),
    )
    out_specs = (
        P(("dp", "fsdp"), None),
        P(("dp", "fsdp"), None, None),
        P(("dp", "fsdp"), None),
        P(("dp", "fsdp"), None, None),
        P("fsdp", "dp"),
        P("fsdp", "dp"),
        P("fsdp", "dp"),
        P("fsdp", "dp"),
        P(None, "fsdp"),
        P(None, "fsdp"),
    )
    return jax.shard_map(
        on_device, mesh=mesh, in_specs=in_specs, out_specs=out_specs, check_vma=False
    )
```
